512 devices in a mesh: group: 16 (over y, core), dev: 32 (over z, x).
Axes of the slice: x: 4, y: 8, z: 8, core: 2. Of those that a mesh axis runs over, the one named last changes fastest.
Arguments:
- direction: float32 [524288], P(('group', 'dev')), may hold values from -6 to 6
- krylov: float32 [8, 524288], P(None, ('group', 'dev')), may hold values from -0.0078125 to 0.0078125
- bases: bfloat16 [2048, 32, 256], P(('group', 'dev')), may hold values from -0.375 to 0.375
- near_tiles: bfloat16 [6144, 256, 256], P(('group', 'dev')), may hold values from -0.15625 to 0.15625
- near_pairs: int32 [6144, 2], P(('group', 'dev')), may hold values from 0 to 127
- near_mask: int32 [6144], P(('group', 'dev')), may hold values 0 or 1
- far_blocks: bfloat16 [32768, 1024], P(('group', 'dev')), may hold values from -0.1875 to 0.1875
- far_pairs: int32 [32768, 2], P(('group', 'dev')), may hold values from 0 to 2047, as said below
- far_mask: int32 [32768], P(('group', 'dev')), may hold values 0 or 1
Outputs:
- next_vector: float32 [524288], P(('group', 'dev'))
- projections: float32 [8], replicated
The draws below stay inside these ranges and needn't reach their ends.
Inputs may be any that keep to these rules, and one draw needn't show every extreme that they name: `far_pairs`: the first cluster of far slot s lies in the group of the device that owns the slot; the second lies in that group or in one of the two groups next to it along the group axis, counted cyclically.
All inputs are finite; a program needn't handle non-finite values. No bound on the sum of `near_mask` or of `far_mask` on one device may be relied on, other than what follows from the above.
Results may differ from the reference program's by a relative error of at most 0.0047.
Values may be sent and summed in bfloat16 or wider, within the bound.
No kernel may reach another device: no remote copies, remote signals or barrier semaphores. Data moves between devices by JAX's collectives and lax.ppermute only.
A program may use at most 64 MiB of HBM per device.

```python
import jax
import jax.numpy as jnp
from jax import lax

LEAF = 256
RANK = 32
KRYLOV = 8
NEAR_SLOTS = 12
FAR_SLOTS = 64
GROUP_LEAVES = 128
CLUSTERS = 2048
PANELS = 524288
N_GROUP = 16
N_DEV = 32
DEVICES = 512


def draw_far_pairs(key, part):
    key = jax.random.fold_in(key, 7)
    first_key, pick_key, second_key = jax.random.split(key, 3)
    rows = DEVICES * FAR_SLOTS
    owner_group = jnp.arange(rows, dtype=jnp.int32) // (FAR_SLOTS * N_DEV)
    first = owner_group * GROUP_LEAVES + jax.random.randint(first_key, (rows,), 0, GROUP_LEAVES, dtype=jnp.int32)
    picked = jax.random.randint(pick_key, (rows,), 0, 10, dtype=jnp.int32)
    offset = jnp.where(picked == 0, -1, jnp.where(picked == 1, 1, 0)).astype(jnp.int32)
    other_group = (owner_group + offset + N_GROUP) % N_GROUP
    second = other_group * GROUP_LEAVES + jax.random.randint(second_key, (rows,), 0, GROUP_LEAVES, dtype=jnp.int32)
    return jnp.stack([first, second], axis=1).astype(jnp.int32)


def plant(array, own_key, low, top_value):
    longest = array.shape.index(max(array.shape))
    spots = []
    for shift in (0, 1):
        where = [jax.random.randint(jax.random.fold_in(own_key, axis), (), 0, length) for axis, length in enumerate(array.shape)]
        where[longest] = (where[longest] + shift) % array.shape[longest]
        spots.append(tuple(where))
    return array.at[spots[0]].set(low).at[spots[1]].set(top_value)


def shard_levels(rng, extent, shards, smallest, high):
    level = 1.0
    for dim, shards_of in shards:
        draws = jax.random.uniform(jax.random.fold_in(jax.random.fold_in(rng, 6), dim), (shards_of,), jnp.float32, smallest / len(shards), high / len(shards))
        level = level * jnp.repeat(jnp.exp(draws), extent[dim] // shards_of).reshape((-1,) + (1,) * (len(extent) - 1 - dim))
    return level


def normal_values(own_key, dims, width, bound, cuts=(), kind=jnp.bfloat16):
    result = width * jax.random.normal(own_key, dims, jnp.float32)
    if cuts:
        result = result * shard_levels(own_key, dims, cuts, -0.22, 0.18)
    return jnp.clip(result, -bound, bound).astype(kind)


def setup_inputs(seed: int = 0) -> dict:
    seeds = jax.random.split(jax.random.key(seed), 10)
    return {
        "direction": normal_values(seeds[0], (PANELS,), 1.0, 6.0, ((0, 512),), jnp.float32),
        "krylov": normal_values(seeds[1], (KRYLOV, PANELS), PANELS ** -0.5, 0.0078125, ((1, 512),), jnp.float32),
        "bases": normal_values(seeds[2], (CLUSTERS, RANK, LEAF), LEAF ** -0.5, 0.375, ((0, 512),)),
        "near_tiles": normal_values(seeds[3], (DEVICES * NEAR_SLOTS, LEAF, LEAF), (6 * LEAF) ** -0.5, 0.15625, ((0, 512),)),
        "near_pairs": plant(jax.random.randint(seeds[4], (DEVICES * NEAR_SLOTS, 2), 0, GROUP_LEAVES), jax.random.fold_in(seeds[4], 1), 0, GROUP_LEAVES - 1).astype(jnp.int32),
        "near_mask": plant((jax.random.randint(seeds[5], (DEVICES * NEAR_SLOTS,), 0, 4) < 3).astype(jnp.int32), jax.random.fold_in(seeds[5], 1), 0, 1),
        "far_blocks": normal_values(seeds[6], (DEVICES * FAR_SLOTS, RANK * RANK), (32 * RANK) ** -0.5, 0.1875, ((0, 512),)),
        "far_pairs": draw_far_pairs(jax.random.fold_in(seeds[9], 71), 0),
        "far_mask": plant((jax.random.randint(seeds[8], (DEVICES * FAR_SLOTS,), 0, 4) < 3).astype(jnp.int32), jax.random.fold_in(seeds[8], 1), 0, 1),
    }


def near_group(packed):
    tiles, pairs, alive, panels_bf = packed
    left_ids = pairs[:, 0]
    right_ids = pairs[:, 1]
    tiles_f = tiles.astype(jnp.float32)
    forward = jnp.einsum('spq,sq->sp', tiles_f, panels_bf[right_ids].astype(jnp.float32))
    backward = jnp.einsum('spq,sp->sq', tiles_f, panels_bf[left_ids].astype(jnp.float32))
    live_slots = alive.astype(jnp.float32)
    forward = forward * live_slots[:, None]
    backward = backward * (live_slots * (left_ids != right_ids).astype(jnp.float32))[:, None]
    summed = jnp.zeros((GROUP_LEAVES, LEAF), jnp.float32)
    return summed.at[left_ids].add(forward).at[right_ids].add(backward)

def reference(direction, krylov, bases, near_tiles, near_pairs, near_mask, far_blocks, far_pairs, far_mask):
    panels_bf = direction.astype(jnp.bfloat16).reshape(CLUSTERS, LEAF)
    near_part = lax.map(near_group, (near_tiles.reshape(N_GROUP, N_DEV * NEAR_SLOTS, LEAF, LEAF), near_pairs.reshape(N_GROUP, N_DEV * NEAR_SLOTS, 2), near_mask.reshape(N_GROUP, N_DEV * NEAR_SLOTS), panels_bf.reshape(N_GROUP, GROUP_LEAVES, LEAF))).reshape(PANELS)
    bases_f = bases.astype(jnp.float32)
    coeffs = jnp.einsum('crp,cp->cr', bases_f, panels_bf.astype(jnp.float32)).astype(jnp.bfloat16)
    blocks = far_blocks.astype(jnp.float32).reshape(-1, RANK, RANK)
    left_ids = far_pairs[:, 0]
    right_ids = far_pairs[:, 1]
    forward = jnp.einsum('srq,sq->sr', blocks, coeffs[right_ids].astype(jnp.float32))
    backward = jnp.einsum('srq,sr->sq', blocks, coeffs[left_ids].astype(jnp.float32))
    live_slots = far_mask.astype(jnp.float32)
    forward = forward * live_slots[:, None]
    backward = backward * (live_slots * (left_ids != right_ids).astype(jnp.float32))[:, None]
    far_coef = jnp.zeros((CLUSTERS, RANK), jnp.float32).at[left_ids].add(forward).at[right_ids].add(backward)
    far_coef = far_coef.astype(jnp.bfloat16)
    far_part = jnp.einsum('crp,cr->cp', bases_f, far_coef.astype(jnp.float32)).reshape(PANELS)
    product = near_part + far_part
    projections = jnp.dot(krylov, product, precision=lax.Precision.HIGHEST)
    remainder = product - jnp.dot(projections, krylov, precision=lax.Precision.HIGHEST)
    root_mean = jnp.sqrt(jnp.mean(remainder * remainder))
    return (remainder / root_mean, projections)
```

```python
import jax
import jax.numpy as jnp
from jax import lax
from jax.experimental import pallas as pl
from jax.experimental.pallas import tpu as pltpu
from jax.sharding import PartitionSpec as P

F32 = jnp.float32
BF16 = jnp.bfloat16
NX, NZ, NY = 4, 8, 8
VMEM = pl.BlockSpec(memory_space=pltpu.VMEM)
HBM = pl.BlockSpec(memory_space=pltpu.HBM)
SMEM = pl.BlockSpec(memory_space=pltpu.SMEM)


def call(body, outs, specs, scratch=()):
    kernel = pl.pallas_call(
        body,
        out_shape=outs,
        in_specs=specs,
        out_specs=jax.tree.map(lambda _: VMEM, outs),
        scratch_shapes=list(scratch),
        compiler_params=pltpu.CompilerParams(vmem_limit_bytes=24 * 1024 * 1024),
    )

    def run(*args):
        return kernel(
            *(
                pltpu.with_memory_space_constraint(arg, pltpu.HBM) if spec is HBM else arg
                for arg, spec in zip(args, specs, strict=True)
            )
        )

    return run


def iota(shape, dim):
    return lax.broadcasted_iota(jnp.int32, shape, dim)


def mm(a, b):
    return lax.dot_general(a, b, (((1,), (0,)), ((), ())), preferred_element_type=F32)


def mm_t(a, b):
    return lax.dot_general(a, b, (((1,), (1,)), ((), ())), preferred_element_type=F32)


def mm_exact(a, b, dims):
    return lax.dot_general(
        a, b, (dims, ((), ())), precision=lax.Precision.HIGHEST, preferred_element_type=F32
    )


def halves(value):
    high = value.astype(BF16)
    return high, (value - high.astype(F32)).astype(BF16)


def one_hot(mask):
    return mask.astype(F32).astype(BF16)


def columns(rows):
    width = rows.shape[1]
    same = one_hot(iota((width, width), 0) == iota((width, width), 1))
    return mm_t(same, rows.astype(F32).astype(BF16)).astype(jnp.int32)


def to_all(value, axis):
    return lax.all_to_all(value, axis, split_axis=0, concat_axis=0, tiled=True)


def group_shift(value, step):
    return lax.ppermute(value, "group", [(g, (g + step) % (2 * NY)) for g in range(2 * NY)])


def pack_body(direction_hbm, bases_hbm, out_ref, own_ref, direction_ref, bases_ref, sems):
    copies = [
        pltpu.make_async_copy(direction_hbm, direction_ref, sems.at[0]),
        pltpu.make_async_copy(bases_hbm, bases_ref, sems.at[1]),
    ]
    for copy in copies:
        copy.start()
    for copy in copies:
        copy.wait()
    xb = direction_ref[...].astype(BF16)
    rank_rows = bases_ref[...]
    low = mm_t(xb, rank_rows[:, :128])
    high = mm_t(xb, rank_rows[:, 128:])
    row = iota((8, 128), 0)
    twice = (iota((8, 128), 1) >> 5) * 2
    kept = jnp.where(row == twice, low, 0.0) + jnp.where(row == twice + 1, high, 0.0)
    coeffs = jnp.sum(kept, axis=0, keepdims=True)
    own_ref[...] = coeffs.astype(BF16)
    out_ref[...] = jnp.concatenate([xb, jnp.where(row == 0, coeffs, 0.0).astype(BF16)], axis=0)


def copies_body(packed_ref, before_ref, after_ref, out_ref):
    row = iota((16, 128), 0)
    packed = packed_ref[...].astype(F32)
    packed = jnp.where(row == 9, before_ref[...].astype(F32), packed)
    packed = jnp.where(row == 10, after_ref[...].astype(F32), packed).astype(BF16)
    for d in range(out_ref.shape[0]):
        out_ref[d] = packed


def prep_body(blocks_hbm, pairs_hbm, mask_hbm, near_pairs_hbm, near_mask_hbm, krylov_hbm,
              out_ref, near_ref, gram_ref, pairs_ref, mask_ref, krylov_ref, sems):
    slots = blocks_hbm.shape[0]
    ends = (
        (blocks_hbm, out_ref.at[0:slots]),
        (pairs_hbm, pairs_ref),
        (mask_hbm, mask_ref),
        (near_pairs_hbm, near_ref.at[0:2]),
        (near_mask_hbm, near_ref.at[2:3]),
        (krylov_hbm, krylov_ref),
    )
    copies = [pltpu.make_async_copy(*end, sems.at[k]) for k, end in enumerate(ends)]
    for copy in copies:
        copy.start()
    for copy in copies:
        copy.wait()
    i_row, j_row = pairs_ref[0:1, :], pairs_ref[1:2, :]
    row = iota((16, slots), 0)
    digits = jnp.zeros((16, slots), jnp.int32)
    for k, value in enumerate((i_row >> 7, i_row & 127, j_row >> 7, j_row & 127, mask_ref[...])):
        digits = jnp.where(row == k, value, digits)
    out_ref[slots : slots + 16, :] = jnp.zeros((16, out_ref.shape[1]), BF16)
    out_ref[slots : slots + 16, 0:slots] = digits.astype(F32).astype(BF16)
    rows = krylov_ref[...]
    gram = mm_exact(rows, rows, ((1,), (1,)))
    lane, row = iota((8, 128), 1) - 8, iota((8, 128), 0)
    inside = (lane >= 0) & (lane < 64)
    wide = mm_exact(gram, jnp.where(inside & ((lane & 7) == row), 1.0, 0.0), ((1,), (0,)))
    gram_ref[...] = jnp.sum(
        jnp.where(inside & ((lane >> 3) == row), wide, 0.0), axis=0, keepdims=True
    )


def near_field(gathered, tiles, pairs):
    slots = len(tiles)
    i_row, j_row, mask = pairs[0:1, :], pairs[1:2, :], pairs[2:3, :]
    cols = columns(pairs)
    lanes = iota((slots, gathered.shape[0]), 1)

    def gather(c):
        row = (c >> 2) * 16 + (c & 3) * 2
        first = mm(one_hot(lanes == row), gathered)
        second = mm(one_hot(lanes == row + 1), gathered)
        return jnp.concatenate([first, second], axis=1).astype(BF16)

    right = gather(cols[:, 1:2])
    left = gather(cols[:, 0:1])
    slot = iota((slots, 256), 0)
    forward = jnp.zeros((slots, 256), F32)
    backward = jnp.zeros((slots, 256), F32)
    for s in range(slots):
        tile = tiles[s]()
        forward = jnp.where(slot == s, mm_t(right, tile), forward)
        backward = jnp.where(slot == s, mm(left, tile), backward)
    rows = iota((256, slots), 0)
    i_target = jnp.where(mask == 1, i_row * 2, -8)
    j_target = jnp.where((mask == 1) & (i_row != j_row), j_row * 2, -8)
    total = jnp.zeros((256, 128), F32)
    for target, value in ((i_target, forward), (j_target, backward)):
        for half in range(2):
            pick = one_hot(rows == target + half)
            for part in halves(value[:, half * 128 : half * 128 + 128]):
                total = total + mm(pick, part)
    return total


def far_field(gathered, bundles, group):
    slots = bundles[0].shape[0] - 16
    digits = [bundle[slots : slots + 16, 0:slots] for bundle in bundles]
    rows = [d.astype(F32).astype(jnp.int32) for d in digits]
    cols = jnp.concatenate([columns(r) for r in rows], axis=0)
    blocks = jnp.concatenate([bundle[0:slots, :] for bundle in bundles], axis=0).astype(F32)
    total_slots = blocks.shape[0]
    i_group, i_low, j_group, j_low, live = (cols[:, k : k + 1] for k in range(5))

    def gather(c_group, c_low):
        step = (c_group - group) & (2 * NY - 1)
        which = jnp.where(step == 0, 0, jnp.where(step == 1, 2, 1))
        place = (c_low >> 2) * 16 + 8 + which
        n = c_low.shape[0]
        taken = mm(one_hot(iota((n, gathered.shape[0]), 1) == place), gathered)
        return jnp.where((iota((n, 128), 1) >> 5) == (c_low & 3), taken, 0.0).astype(BF16)

    right = gather(j_group[0:slots], j_low[0:slots])
    left = gather(i_group, i_low)
    rank = iota((128, 1024), 0) & 31
    column = iota((128, 1024), 1)
    by_column = one_hot(rank == (column & 31))
    by_row = one_hot(rank == (column >> 5))
    forward = jnp.zeros((slots, 128), F32)
    for part in halves(blocks[0:slots] * mm(right, by_column)):
        forward = forward + mm_t(part, by_row)
    backward = jnp.zeros((total_slots, 128), F32)
    for part in halves(blocks * mm(left, by_row)):
        backward = backward + mm_t(part, by_column)
    lane_block = iota((total_slots, 128), 1) >> 5
    forward = jnp.where(
        (live[0:slots] == 1) & (lane_block[0:slots] == (i_low[0:slots] & 3)), forward, 0.0
    )
    different = (i_group != j_group) | (i_low != j_low)
    mine = (live == 1) & (j_group == group) & different
    backward = jnp.where(mine & (lane_block == (j_low & 3)), backward, 0.0)
    owner = iota((NZ * NX, slots), 0)
    total = jnp.zeros((NZ * NX, 128), F32)
    pick = one_hot(owner == (rows[0][1:2, :] >> 2))
    for part in halves(forward):
        total = total + mm(pick, part)
    for k in range(len(bundles)):
        pick = one_hot(owner == (rows[k][3:4, :] >> 2))
        for part in halves(backward[k * slots : k * slots + slots]):
            total = total + mm(pick, part)
    return total


def main_body(place_ref, near_ref, own_ref, before_ref, after_ref, gathered_ref,
              tiles_hbm, out_ref, tiles_ref, sems):
    slots = tiles_ref.shape[0]
    copies = [
        pltpu.make_async_copy(tiles_hbm.at[s], tiles_ref.at[s], sems.at[s]) for s in range(slots)
    ]
    for copy in copies:
        copy.start()
    gathered = gathered_ref[...]
    bundles = [ref[...] for ref in (own_ref, before_ref, after_ref)]
    far = far_field(gathered, bundles, place_ref[0])
    for d in range(NZ * NX):
        out_ref[d, :, 1024:1152] = far[d : d + 1, :]

    def tile(s):
        def load():
            copies[s].wait()
            return tiles_ref[s]
        return load

    near = near_field(gathered, [tile(s) for s in range(slots)], near_ref[...])
    for d in range(NZ * NX):
        for r in range(8):
            out_ref[d, :, r * 128 : r * 128 + 128] = near[d * 8 + r : d * 8 + r + 1, :]


def product_body(pieces_ref, bases_ref, krylov_ref, gram_ref, product_ref, copies_ref):
    total = jnp.sum(pieces_ref[...], axis=0)
    near = jnp.concatenate([total[:, r * 128 : r * 128 + 128] for r in range(8)], axis=0)
    coef = total[:, 1024:1152].astype(BF16).astype(F32)
    row, lane = iota((8, 128), 0), iota((8, 128), 1)
    spread = jnp.where((lane >> 5) == (row >> 1), coef, 0.0).astype(BF16)
    low = mm(spread, bases_ref[:, :128])
    high = mm(spread, bases_ref[:, 128:])
    product = near + jnp.where((row & 1) == 0, low, high)
    product_ref[...] = product
    acc = jnp.zeros((8, 128), F32)
    for r in range(8):
        acc = acc + krylov_ref[:, r * 128 : r * 128 + 128] * product[r : r + 1, :]
    proj = jnp.sum(acc, axis=1, keepdims=True)
    square = jnp.sum(product * product, axis=1, keepdims=True)
    values = jnp.where(lane == row, proj, 0.0) + jnp.where(lane == 72, square, 0.0)
    payload = jnp.sum(values, axis=0, keepdims=True) + gram_ref[...]
    for d in range(copies_ref.shape[0]):
        copies_ref[d] = payload


def last_body(count, pieces_ref, product_ref, krylov_ref, next_ref, proj_ref):
    total = jnp.sum(pieces_ref[...], axis=0)
    row, lane = iota((8, 128), 0), iota((8, 128), 1)
    proj = jnp.sum(jnp.where(lane == row, total, 0.0), axis=1, keepdims=True)
    inside = (lane >= 8) & (lane < 72)
    first = jnp.sum(jnp.where(inside & (((lane - 8) >> 3) == row), proj, 0.0), axis=0, keepdims=True)
    second = jnp.sum(jnp.where(inside & ((lane & 7) == row), proj, 0.0), axis=0, keepdims=True)
    lane = iota((1, 128), 1)
    terms = total * jnp.where(lane < 8, -2.0 * total, first * second)
    terms = jnp.where(lane == 72, total, jnp.where(lane < 72, terms, 0.0))
    length_sq = jnp.sum(terms, axis=1, keepdims=True)
    scale = 1.0 / jnp.sqrt(jnp.maximum(length_sq, 0.0) / count)
    for r in range(8):
        taken = jnp.sum(proj * krylov_ref[:, r * 128 : r * 128 + 128], axis=0, keepdims=True)
        next_ref[r : r + 1, :] = (product_ref[r : r + 1, :] - taken) * scale
    proj_ref[...] = total[:, 0:8]


def local(
    direction, krylov, bases, near_tiles, near_pairs, near_mask, far_blocks, far_pairs, far_mask
):
    panels = direction.shape[0]
    devs, groups = NZ * NX, 2 * NY
    rank_rows = bases.reshape(-1, bases.shape[2])
    place = lax.axis_index("group").astype(jnp.int32)[None]
    sds = jax.ShapeDtypeStruct
    slots, far_slots = near_tiles.shape[0], far_blocks.shape[0]

    packed, own = call(
        pack_body,
        [sds((16, 128), BF16), sds((1, 128), BF16)],
        [HBM, HBM],
        [pltpu.VMEM((8, 128), F32), pltpu.VMEM(rank_rows.shape, BF16), pltpu.SemaphoreType.DMA((2,))],
    )(direction.reshape(8, 128), rank_rows)
    copies = call(copies_body, sds((devs, 16, 128), BF16), [VMEM] * 3)(
        packed, group_shift(own, 1), group_shift(own, -1)
    )
    gathered = to_all(copies, "dev")
    bundle, near_rows, gram = call(
        prep_body,
        [
            sds((far_slots + 16, far_blocks.shape[1]), BF16),
            sds((3, slots), jnp.int32),
            sds((1, 128), F32),
        ],
        [HBM] * 6,
        [
            pltpu.VMEM((2, far_slots), jnp.int32),
            pltpu.VMEM((1, far_slots), jnp.int32),
            pltpu.VMEM(krylov.shape, F32),
            pltpu.SemaphoreType.DMA((6,)),
        ],
    )(far_blocks, far_pairs.T, far_mask[None], near_pairs.T, near_mask[None], krylov)
    before, after = group_shift(bundle, 1), group_shift(bundle, -1)

    parts = call(
        main_body,
        sds((devs, 1, 1152), F32),
        [SMEM] + [VMEM] * 5 + [HBM],
        [pltpu.VMEM(near_tiles.shape, BF16), pltpu.SemaphoreType.DMA((slots,))],
    )(
        place, near_rows, bundle, before, after,
        gathered.reshape(-1, 128), near_tiles,
    )
    product, copies = call(
        product_body, [sds((8, 128), F32), sds((groups * devs, 1, 128), F32)], [VMEM] * 4
    )(to_all(parts, "dev"), rank_rows, krylov, gram)
    count = float(panels * devs * groups)

    def finish(*refs):
        last_body(count, *refs)

    next_vector, projections = call(finish, [sds((8, 128), F32), sds((1, 8), F32)], [VMEM] * 3)(
        to_all(copies, ("group", "dev")), product, krylov
    )
    return (next_vector.reshape(-1), projections.reshape(-1))


def solution(mesh):
    in_specs = (
        P(("group", "dev")),
        P(None, ("group", "dev")),
        P(("group", "dev"), None, None),
        P(("group", "dev"), None, None),
        P(("group", "dev"), None),
        P(("group", "dev")),
        P(("group", "dev"), None),
        P(("group", "dev"), None),
        P(("group", "dev")),
    )
    out_specs = (P(("group", "dev")), P())
    return jax.shard_map(local, mesh=mesh, in_specs=in_specs, out_specs=out_specs, check_vma=False)
```

```python
import jax
import jax.numpy as jnp
from jax import lax
from jax.experimental import pallas as pl
from jax.experimental.pallas import tpu as pltpu
from jax.sharding import PartitionSpec as P

F32 = jnp.float32
BF16 = jnp.bfloat16
I32 = jnp.int32
NX, NZ, NY = 4, 8, 8
DEVS, GROUPS = NZ * NX, 2 * NY
VMEM = pl.BlockSpec(memory_space=pltpu.VMEM)
HBM = pl.BlockSpec(memory_space=pltpu.HBM)
SMEM = pl.BlockSpec(memory_space=pltpu.SMEM)
sds = jax.ShapeDtypeStruct


def call(body, outs, specs, scratch=()):
    kernel = pl.pallas_call(
        body,
        out_shape=outs,
        in_specs=specs,
        out_specs=jax.tree.map(lambda _: VMEM, outs),
        scratch_shapes=list(scratch),
        compiler_params=pltpu.CompilerParams(vmem_limit_bytes=24 * 1024 * 1024),
    )

    def run(*args):
        return kernel(
            *(
                pltpu.with_memory_space_constraint(arg, pltpu.HBM) if spec is HBM else arg
                for arg, spec in zip(args, specs, strict=True)
            )
        )

    return run


def iota(shape, dim):
    return lax.broadcasted_iota(I32, shape, dim)


def mm(a, b):
    return lax.dot_general(a, b, (((1,), (0,)), ((), ())), preferred_element_type=F32)


def mm_t(a, b):
    return lax.dot_general(a, b, (((1,), (1,)), ((), ())), preferred_element_type=F32)


def mm_exact(a, b, dims):
    return lax.dot_general(
        a, b, (dims, ((), ())), precision=lax.Precision.HIGHEST, preferred_element_type=F32
    )


def halves(value):
    high = value.astype(BF16)
    return high, (value - high.astype(F32)).astype(BF16)


def one_hot(mask):
    return mask.astype(F32).astype(BF16)


def small(rows):
    return rows.astype(F32).astype(BF16)


def columns(rows):
    width = rows.shape[1]
    same = one_hot(iota((width, width), 0) == iota((width, width), 1))
    return mm_t(same, small(rows)).astype(I32)


def to_all(value, axis):
    return lax.all_to_all(value, axis, split_axis=0, concat_axis=0, tiled=True)


def group_shift(value, step):
    return lax.ppermute(value, "group", [(g, (g + step) % GROUPS) for g in range(GROUPS)])


def started(ends, sems):
    copies = [pltpu.make_async_copy(*end, sems.at[k]) for k, end in enumerate(ends)]
    for copy in copies:
        copy.start()
    return copies


def pack_body(direction_hbm, bases_hbm, out_ref, direction_ref, bases_ref, sems):
    for copy in started(((direction_hbm, direction_ref), (bases_hbm, bases_ref)), sems):
        copy.wait()
    xb = direction_ref[...].astype(BF16)
    rank_rows = bases_ref[...]
    low = mm_t(xb, rank_rows[:, :128])
    high = mm_t(xb, rank_rows[:, 128:])
    row = iota((8, 128), 0)
    twice = (iota((8, 128), 1) >> 5) * 2
    kept = jnp.where(row == twice, low, 0.0) + jnp.where(row == twice + 1, high, 0.0)
    coeffs = jnp.sum(kept, axis=0, keepdims=True)
    packed = jnp.concatenate([xb, jnp.where(row == 0, coeffs, 0.0).astype(BF16)], axis=0)
    for d in range(DEVS):
        out_ref[d] = packed


def prep_body(tiles_hbm, blocks_hbm, pairs_hbm, mask_hbm, near_pairs_hbm, near_mask_hbm, krylov_hbm,
              out_ref, tiles_ref, gather_ref, scatter_ref, gram_ref,
              pairs_ref, mask_ref, near_pairs_ref, near_mask_ref, krylov_ref, sems, tile_sem):
    fetched = pltpu.make_async_copy(tiles_hbm, tiles_ref, tile_sem)
    slots = blocks_hbm.shape[0]
    ends = (
        (blocks_hbm, out_ref.at[0:slots]),
        (pairs_hbm, pairs_ref),
        (mask_hbm, mask_ref),
        (near_pairs_hbm, near_pairs_ref),
        (near_mask_hbm, near_mask_ref),
        (krylov_hbm, krylov_ref),
    )
    copies = started(ends, sems)
    fetched.start()
    for copy in copies:
        copy.wait()
    i_row, j_row = pairs_ref[0:1, :], pairs_ref[1:2, :]
    row = iota((16, slots), 0)
    digits = jnp.zeros((16, slots), I32)
    for k, value in enumerate((i_row >> 7, i_row & 127, j_row >> 7, j_row & 127, mask_ref[...])):
        digits = jnp.where(row == k, value, digits)
    out_ref[slots : slots + 16, :] = jnp.zeros((16, out_ref.shape[1]), BF16)
    out_ref[slots : slots + 16, 0:slots] = small(digits)
    near = near_pairs_ref[...]
    live = near_mask_ref[...]
    near_slots = near.shape[1]
    row = iota((8, near_slots), 0)
    info = jnp.where(row == 0, near[0:1, :], jnp.where(row == 1, near[1:2, :], live))
    m = iota((64, near_slots), 0)
    pick = one_hot((m & 15) == iota((64, near_slots), 1))
    info_cols = mm_t(pick, small(info)).astype(I32)
    i_col, j_col = info_cols[:, 0:1], info_cols[:, 1:2]
    m = iota((64, 1), 0) >> 4
    c = jnp.where(m < 2, j_col, i_col)
    place = (c >> 2) * 16 + (c & 3) * 2 + (m & 1)
    gather_ref[...] = one_hot(iota((64, DEVS * 16), 1) == place)
    lane = iota((near_slots, 128), 1)
    pick = one_hot((lane & 15) == iota((near_slots, 128), 0))
    info_lanes = mm(small(info), pick).astype(I32)
    i_lane, j_lane, live_lane = (info_lanes[k : k + 1, :] for k in range(3))
    kind = (iota((1, 128), 1) >> 4) & 3
    used = (live_lane == 1) & ((kind < 2) | (i_lane != j_lane))
    target = jnp.where(kind < 2, i_lane, j_lane) * 2 + (kind & 1)
    target = jnp.where(used, target, -1)
    scatter_ref[...] = one_hot(iota((DEVS * 8, 128), 0) == target)
    rows = krylov_ref[...]
    gram = mm_exact(rows, rows, ((1,), (1,)))
    lane, row = iota((8, 128), 1) - 8, iota((8, 128), 0)
    inside = (lane >= 0) & (lane < 64)
    wide = mm_exact(gram, jnp.where(inside & ((lane & 7) == row), 1.0, 0.0), ((1,), (0,)))
    gram_ref[...] = jnp.sum(
        jnp.where(inside & ((lane >> 3) == row), wide, 0.0), axis=0, keepdims=True
    )
    fetched.wait()


def coeffs_body(gathered_ref, out_ref):
    rows = iota((DEVS, DEVS * 16), 0) * 16 + 8
    pick = one_hot(iota((DEVS, DEVS * 16), 1) == rows)
    out_ref[...] = mm(pick, gathered_ref[...]).astype(BF16)


def near_body(gathered_ref, gather_ref, scatter_ref, tiles_ref, out_ref):
    taken = mm(gather_ref[...], gathered_ref[...])
    right = jnp.concatenate([taken[0:16], taken[16:32]], axis=1).astype(BF16)
    left = jnp.concatenate([taken[32:48], taken[48:64]], axis=1).astype(BF16)
    slot = iota((16, 256), 0)
    forward = jnp.zeros((16, 256), F32)
    backward = jnp.zeros((16, 256), F32)
    for s in range(tiles_ref.shape[0]):
        tile = tiles_ref[s]
        forward = jnp.where(slot == s, mm_t(right, tile), forward)
        backward = jnp.where(slot == s, mm(left, tile), backward)
    values = jnp.concatenate(
        [forward[:, :128], forward[:, 128:], backward[:, :128], backward[:, 128:]], axis=0
    )
    out_ref[...] = mm(scatter_ref[...], jnp.concatenate(halves(values), axis=0))


def far_body(place_ref, near_ref, own_ref, before_ref, after_ref, own_coef_ref, before_coef_ref,
             after_coef_ref, out_ref):
    group = place_ref[0]
    bundles = (own_ref, before_ref, after_ref)
    slots = own_ref.shape[0] - 16
    total_slots = 3 * slots
    rows = [b[slots : slots + 16, 0:slots].astype(F32).astype(I32) for b in bundles]
    cols = jnp.concatenate([columns(r) for r in rows], axis=0)
    i_group, i_low, j_group, j_low, live = (cols[:, k : k + 1] for k in range(5))
    coeffs = jnp.concatenate([own_coef_ref[...], before_coef_ref[...], after_coef_ref[...]], axis=0)

    def gather(c_group, c_low):
        step = (c_group - group) & (GROUPS - 1)
        which = jnp.where(step == 0, 0, jnp.where(step == 1, 2, 1))
        n = c_low.shape[0]
        taken = mm(one_hot(iota((n, 3 * DEVS), 1) == which * DEVS + (c_low >> 2)), coeffs)
        return jnp.where((iota((n, 128), 1) >> 5) == (c_low & 3), taken, 0.0).astype(BF16)

    right = gather(j_group[0:slots], j_low[0:slots])
    left = gather(i_group, i_low)
    sub, lane = iota((128, 128), 0), iota((128, 128), 1)
    tiled = mm(right, one_hot((sub & 31) == (lane & 31)))
    forward = jnp.zeros((slots, 128), F32)
    backward = jnp.zeros((total_slots, 128), F32)
    for k in range(8):
        parts = [b[0:slots, k * 128 : k * 128 + 128] for b in bundles]
        part = jnp.concatenate(parts, axis=0).astype(F32)
        backward = backward + part * mm(left, one_hot((sub & 31) == 4 * k + (lane >> 5)))
        give = one_hot((lane & 31) == 4 * k + (sub >> 5))
        for piece in halves(part[0:slots] * tiled):
            forward = forward + mm(piece, give)
    backward = backward + pltpu.roll(backward, 64, 1)
    backward = backward + pltpu.roll(backward, 32, 1)
    lane_block = iota((total_slots, 128), 1) >> 5
    forward = jnp.where(
        (live[0:slots] == 1) & (lane_block[0:slots] == (i_low[0:slots] & 3)), forward, 0.0
    )
    different = (i_group != j_group) | (i_low != j_low)
    mine = (live == 1) & (j_group == group) & different
    backward = jnp.where(mine & (lane_block == (j_low & 3)), backward, 0.0)
    owner = iota((DEVS, slots), 0)
    total = jnp.zeros((DEVS, 128), F32)
    pick = one_hot(owner == (rows[0][1:2, :] >> 2))
    for part in halves(forward):
        total = total + mm(pick, part)
    for k in range(3):
        pick = one_hot(owner == (rows[k][3:4, :] >> 2))
        for part in halves(backward[k * slots : k * slots + slots]):
            total = total + mm(pick, part)
    row = iota((8, 128), 0)
    for d in range(DEVS):
        near = near_ref[d * 8 : d * 8 + 8, :]
        near_high = near.astype(BF16).astype(F32)
        far = total[d : d + 1, :]
        far_high = far.astype(BF16).astype(F32)
        tail = jnp.where(row == 0, far_high, jnp.where(row == 1, far - far_high, 0.0))
        out_ref[d] = jnp.concatenate([near_high, near - near_high, tail], axis=0).astype(BF16)


def product_body(pieces_ref, bases_ref, krylov_ref, gram_ref, product_ref, copies_ref):
    total = jnp.sum(pieces_ref[...].astype(F32), axis=0)
    near = total[0:8, :] + total[8:16, :]
    coef = (total[16:17, :] + total[17:18, :]).astype(BF16).astype(F32)
    row, lane = iota((8, 128), 0), iota((8, 128), 1)
    spread = jnp.where((lane >> 5) == (row >> 1), coef, 0.0).astype(BF16)
    low = mm(spread, bases_ref[:, :128])
    high = mm(spread, bases_ref[:, 128:])
    product = near + jnp.where((row & 1) == 0, low, high)
    product_ref[...] = product
    acc = jnp.zeros((8, 128), F32)
    for r in range(8):
        acc = acc + krylov_ref[:, r * 128 : r * 128 + 128] * product[r : r + 1, :]
    proj = jnp.sum(acc, axis=1, keepdims=True)
    square = jnp.sum(product * product, axis=1, keepdims=True)
    values = jnp.where(lane == row, proj, 0.0) + jnp.where(lane == 72, square, 0.0)
    payload = jnp.sum(values, axis=0, keepdims=True) + gram_ref[...]
    for d in range(copies_ref.shape[0]):
        copies_ref[d] = payload


def spread_body(pieces_ref, out_ref):
    total = jnp.sum(pieces_ref[...], axis=0)
    for d in range(out_ref.shape[0]):
        out_ref[d] = total


def last_body(count, pieces_ref, product_ref, krylov_ref, next_ref, proj_ref):
    total = jnp.sum(pieces_ref[...], axis=0)
    row, lane = iota((8, 128), 0), iota((8, 128), 1)
    proj = jnp.sum(jnp.where(lane == row, total, 0.0), axis=1, keepdims=True)
    inside = (lane >= 8) & (lane < 72)
    first = jnp.sum(jnp.where(inside & (((lane - 8) >> 3) == row), proj, 0.0), axis=0, keepdims=True)
    second = jnp.sum(jnp.where(inside & ((lane & 7) == row), proj, 0.0), axis=0, keepdims=True)
    lane = iota((1, 128), 1)
    terms = total * jnp.where(lane < 8, -2.0 * total, first * second)
    terms = jnp.where(lane == 72, total, jnp.where(lane < 72, terms, 0.0))
    length_sq = jnp.sum(terms, axis=1, keepdims=True)
    scale = 1.0 / jnp.sqrt(jnp.maximum(length_sq, 0.0) / count)
    for r in range(8):
        taken = jnp.sum(proj * krylov_ref[:, r * 128 : r * 128 + 128], axis=0, keepdims=True)
        next_ref[r : r + 1, :] = (product_ref[r : r + 1, :] - taken) * scale
    proj_ref[...] = total[:, 0:8]


def local(
    direction, krylov, bases, near_tiles, near_pairs, near_mask, far_blocks, far_pairs, far_mask
):
    panels = direction.shape[0]
    rank_rows = bases.reshape(-1, bases.shape[2])
    place = lax.axis_index("group").astype(I32)[None]
    slots, far_slots = near_tiles.shape[0], far_blocks.shape[0]

    copies = call(
        pack_body,
        sds((DEVS, 16, 128), BF16),
        [HBM, HBM],
        [pltpu.VMEM((8, 128), F32), pltpu.VMEM(rank_rows.shape, BF16), pltpu.SemaphoreType.DMA((2,))],
    )(direction.reshape(8, 128), rank_rows)
    gathered = to_all(copies, "dev").reshape(-1, 128)
    bundle, tiles, gather, scatter, gram = call(
        prep_body,
        [
            sds((far_slots + 16, far_blocks.shape[1]), BF16),
            pltpu.VMEM(near_tiles.shape, BF16),
            sds((64, DEVS * 16), BF16),
            sds((DEVS * 8, 128), BF16),
            sds((1, 128), F32),
        ],
        [HBM] * 7,
        [
            pltpu.VMEM((2, far_slots), I32),
            pltpu.VMEM((1, far_slots), I32),
            pltpu.VMEM((2, slots), I32),
            pltpu.VMEM((1, slots), I32),
            pltpu.VMEM(krylov.shape, F32),
            pltpu.SemaphoreType.DMA((6,)),
            pltpu.SemaphoreType.DMA,
        ],
    )(near_tiles, far_blocks, far_pairs.T, far_mask[None], near_pairs.T, near_mask[None], krylov)
    before, after = group_shift(bundle, 1), group_shift(bundle, -1)

    coeffs = call(coeffs_body, sds((DEVS, 128), BF16), [VMEM])(gathered)
    coeffs_before, coeffs_after = group_shift(coeffs, 1), group_shift(coeffs, -1)
    near = call(near_body, sds((DEVS * 8, 128), F32), [VMEM] * 4)(gathered, gather, scatter, tiles)
    parts = call(far_body, sds((DEVS, 24, 128), BF16), [SMEM] + [VMEM] * 7)(
        place, near, bundle, before, after, coeffs, coeffs_before, coeffs_after
    )
    product, copies = call(
        product_body, [sds((8, 128), F32), sds((GROUPS, 1, 128), F32)], [VMEM] * 4
    )(to_all(parts, "dev"), rank_rows, krylov, gram)
    copies = call(spread_body, sds((DEVS, 1, 128), F32), [VMEM])(to_all(copies, "group"))
    pieces = to_all(copies, "dev")
    count = float(panels * DEVS * GROUPS)

    def finish(*refs):
        last_body(count, *refs)

    next_vector, projections = call(finish, [sds((8, 128), F32), sds((1, 8), F32)], [VMEM] * 3)(
        pieces, product, krylov
    )
    return (next_vector.reshape(-1), projections.reshape(-1))


def solution(mesh):
    in_specs = (
        P(("group", "dev")),
        P(None, ("group", "dev")),
        P(("group", "dev"), None, None),
        P(("group", "dev"), None, None),
        P(("group", "dev"), None),
        P(("group", "dev")),
        P(("group", "dev"), None),
        P(("group", "dev"), None),
        P(("group", "dev")),
    )
    out_specs = (P(("group", "dev")), P())
    return jax.shard_map(local, mesh=mesh, in_specs=in_specs, out_specs=out_specs, check_vma=False)
```

```python
import jax
import jax.numpy as jnp
from jax import lax
from jax.experimental import pallas as pl
from jax.experimental.pallas import tpu as pltpu
from jax.sharding import PartitionSpec as P

F32 = jnp.float32
BF16 = jnp.bfloat16
I32 = jnp.int32
NX, NZ, NY = 4, 8, 8
DEVS, GROUPS = NZ * NX, 2 * NY
VMEM = pl.BlockSpec(memory_space=pltpu.VMEM)
HBM = pl.BlockSpec(memory_space=pltpu.HBM)
SMEM = pl.BlockSpec(memory_space=pltpu.SMEM)
sds = jax.ShapeDtypeStruct


def call(body, outs, specs, scratch=()):
    kernel = pl.pallas_call(
        body,
        out_shape=outs,
        in_specs=specs,
        out_specs=jax.tree.map(lambda _: VMEM, outs),
        scratch_shapes=list(scratch),
        compiler_params=pltpu.CompilerParams(vmem_limit_bytes=24 * 1024 * 1024),
    )

    def run(*args):
        return kernel(
            *(
                pltpu.with_memory_space_constraint(arg, pltpu.HBM) if spec is HBM else arg
                for arg, spec in zip(args, specs, strict=True)
            )
        )

    return run


def iota(shape, dim):
    return lax.broadcasted_iota(I32, shape, dim)


def mm(a, b):
    return lax.dot_general(a, b, (((1,), (0,)), ((), ())), preferred_element_type=F32)


def mm_t(a, b):
    return lax.dot_general(a, b, (((1,), (1,)), ((), ())), preferred_element_type=F32)


def mm_exact(a, b, dims):
    return lax.dot_general(
        a, b, (dims, ((), ())), precision=lax.Precision.HIGHEST, preferred_element_type=F32
    )


def halves(value):
    high = value.astype(BF16)
    return high, (value - high.astype(F32)).astype(BF16)


def one_hot(mask):
    return mask.astype(F32).astype(BF16)


def small(rows):
    return rows.astype(F32).astype(BF16)


def columns(rows):
    width = rows.shape[1]
    same = one_hot(iota((width, width), 0) == iota((width, width), 1))
    return mm_t(same, small(rows)).astype(I32)


def to_all(value, axis, index_groups=None):
    return lax.all_to_all(
        value, axis, split_axis=0, concat_axis=0, tiled=True, axis_index_groups=index_groups
    )


def group_shift(value, step):
    return lax.ppermute(value, "group", [(g, (g + step) % GROUPS) for g in range(GROUPS)])


def started(ends, sems):
    copies = [pltpu.make_async_copy(*end, sems.at[k]) for k, end in enumerate(ends)]
    for copy in copies:
        copy.start()
    return copies


def pack_body(direction_hbm, bases_hbm, out_ref, direction_ref, bases_ref, sems):
    for copy in started(((direction_hbm, direction_ref), (bases_hbm, bases_ref)), sems):
        copy.wait()
    xb = direction_ref[...].astype(BF16)
    rank_rows = bases_ref[...]
    low = mm_t(xb, rank_rows[:, :128])
    high = mm_t(xb, rank_rows[:, 128:])
    row = iota((8, 128), 0)
    twice = (iota((8, 128), 1) >> 5) * 2
    kept = jnp.where(row == twice, low, 0.0) + jnp.where(row == twice + 1, high, 0.0)
    coeffs = jnp.sum(kept, axis=0, keepdims=True)
    packed = jnp.concatenate([xb, jnp.where(row == 0, coeffs, 0.0).astype(BF16)], axis=0)
    for d in range(DEVS):
        out_ref[d] = packed


def prep_body(tiles_hbm, blocks_hbm, pairs_hbm, mask_hbm, near_pairs_hbm, near_mask_hbm, krylov_hbm,
              out_ref, tiles_ref, gather_ref, scatter_ref, take_ref, give_ref, gram_ref,
              pairs_ref, mask_ref, near_pairs_ref, near_mask_ref, krylov_ref, sems, tile_sem):
    fetched = pltpu.make_async_copy(tiles_hbm, tiles_ref, tile_sem)
    slots = blocks_hbm.shape[0]
    ends = (
        (blocks_hbm, out_ref.at[0:slots]),
        (pairs_hbm, pairs_ref),
        (mask_hbm, mask_ref),
        (near_pairs_hbm, near_pairs_ref),
        (near_mask_hbm, near_mask_ref),
        (krylov_hbm, krylov_ref),
    )
    copies = started(ends, sems)
    fetched.start()
    for copy in copies:
        copy.wait()
    i_row, j_row = pairs_ref[0:1, :], pairs_ref[1:2, :]
    row = iota((16, slots), 0)
    digits = jnp.zeros((16, slots), I32)
    for k, value in enumerate((i_row >> 7, i_row & 127, j_row >> 7, j_row & 127, mask_ref[...])):
        digits = jnp.where(row == k, value, digits)
    out_ref[slots : slots + 16, :] = jnp.zeros((16, out_ref.shape[1]), BF16)
    out_ref[slots : slots + 16, 0:slots] = small(digits)
    near = near_pairs_ref[...]
    live = near_mask_ref[...]
    near_slots = near.shape[1]
    row = iota((8, near_slots), 0)
    info = jnp.where(row == 0, near[0:1, :], jnp.where(row == 1, near[1:2, :], live))
    m = iota((64, near_slots), 0)
    pick = one_hot((m & 15) == iota((64, near_slots), 1))
    info_cols = mm_t(pick, small(info)).astype(I32)
    i_col, j_col = info_cols[:, 0:1], info_cols[:, 1:2]
    m = iota((64, 1), 0) >> 4
    c = jnp.where(m < 2, j_col, i_col)
    place = (c >> 2) * 16 + (c & 3) * 2 + (m & 1)
    gather_ref[...] = one_hot(iota((64, DEVS * 16), 1) == place)
    lane = iota((near_slots, 128), 1)
    pick = one_hot((lane & 15) == iota((near_slots, 128), 0))
    info_lanes = mm(small(info), pick).astype(I32)
    i_lane, j_lane, live_lane = (info_lanes[k : k + 1, :] for k in range(3))
    kind = (iota((1, 128), 1) >> 4) & 3
    used = (live_lane == 1) & ((kind < 2) | (i_lane != j_lane))
    target = jnp.where(kind < 2, i_lane, j_lane) * 2 + (kind & 1)
    target = jnp.where(used, target, -1)
    scatter_ref[...] = one_hot(iota((DEVS * 8, 128), 0) == target)
    take_ref[...] = one_hot((iota((128, 1024), 0) & 31) == (iota((128, 1024), 1) >> 5))
    give_ref[...] = one_hot((iota((1024, 128), 0) >> 5) == (iota((1024, 128), 1) & 31))
    rows = krylov_ref[...]
    gram = mm_exact(rows, rows, ((1,), (1,)))
    lane, row = iota((8, 128), 1) - 8, iota((8, 128), 0)
    inside = (lane >= 0) & (lane < 64)
    wide = mm_exact(gram, jnp.where(inside & ((lane & 7) == row), 1.0, 0.0), ((1,), (0,)))
    gram_ref[...] = jnp.sum(
        jnp.where(inside & ((lane >> 3) == row), wide, 0.0), axis=0, keepdims=True
    )
    fetched.wait()


def coeffs_body(gathered_ref, out_ref):
    rows = iota((DEVS, DEVS * 16), 0) * 16 + 8
    pick = one_hot(iota((DEVS, DEVS * 16), 1) == rows)
    out_ref[...] = mm(pick, gathered_ref[...]).astype(BF16)


def near_body(gathered_ref, gather_ref, scatter_ref, tiles_ref, out_ref):
    taken = mm(gather_ref[...], gathered_ref[...])
    right = jnp.concatenate([taken[0:16], taken[16:32]], axis=1).astype(BF16)
    left = jnp.concatenate([taken[32:48], taken[48:64]], axis=1).astype(BF16)
    slot = iota((16, 256), 0)
    forward = jnp.zeros((16, 256), F32)
    backward = jnp.zeros((16, 256), F32)
    for s in range(tiles_ref.shape[0]):
        tile = tiles_ref[s]
        forward = jnp.where(slot == s, mm_t(right, tile), forward)
        backward = jnp.where(slot == s, mm(left, tile), backward)
    values = jnp.concatenate(
        [forward[:, :128], forward[:, 128:], backward[:, :128], backward[:, 128:]], axis=0
    )
    out_ref[...] = mm(scatter_ref[...], jnp.concatenate(halves(values), axis=0))


def slot_info(bundle_ref):
    slots = bundle_ref.shape[0] - 16
    rows = bundle_ref[slots : slots + 16, 0:slots].astype(F32).astype(I32)
    return rows, columns(rows)


def picked(index, low, coeffs):
    n = index.shape[0]
    taken = mm(one_hot(iota((n, coeffs.shape[0]), 1) == index), coeffs)
    return jnp.where((iota((n, 128), 1) >> 5) == (low & 3), taken, 0.0).astype(BF16)


def block_columns(bundle_ref, k):
    return bundle_ref[0 : bundle_ref.shape[0] - 16, k * 128 : k * 128 + 128].astype(F32)


def forward_sums(bundle_ref, right, give_ref):
    sub, lane = iota((128, 128), 0), iota((128, 128), 1)
    tiled = mm(right, one_hot((sub & 31) == (lane & 31)))
    total = jnp.zeros(tiled.shape, F32)
    for k in range(8):
        for piece in halves(block_columns(bundle_ref, k) * tiled):
            total = total + mm(piece, give_ref[k * 128 : k * 128 + 128, :])
    return total


def backward_sums(bundle_refs, left, take_ref):
    total = jnp.zeros(left.shape, F32)
    for k in range(8):
        blocks = jnp.concatenate([block_columns(ref, k) for ref in bundle_refs], axis=0)
        total = total + blocks * mm(left, take_ref[:, k * 128 : k * 128 + 128])
    total = total + pltpu.roll(total, 64, 1)
    return total + pltpu.roll(total, 32, 1)


def in_lanes(value, keep, low):
    lane_block = iota(value.shape, 1) >> 5
    return jnp.where(keep & (lane_block == (low & 3)), value, 0.0)


def owners_sum(low_row, value):
    pick = one_hot(iota((DEVS, low_row.shape[1]), 0) == (low_row >> 2))
    high, low = halves(value)
    return mm(pick, high) + mm(pick, low)


def far_own_body(place_ref, bundle_ref, coef_ref, take_ref, give_ref, out_ref):
    group = place_ref[0]
    coeffs = coef_ref[...]
    rows, cols = slot_info(bundle_ref)
    i_low, j_group, j_low, live = (cols[:, k : k + 1] for k in (1, 2, 3, 4))
    here = j_group == group
    right = picked(jnp.where(here, j_low >> 2, -1), j_low, coeffs)
    left = picked(i_low >> 2, i_low, coeffs)
    forward = in_lanes(forward_sums(bundle_ref, right, give_ref), live == 1, i_low)
    backward = in_lanes(
        backward_sums((bundle_ref,), left, take_ref),
        (live == 1) & here & (i_low != j_low),
        j_low,
    )
    out_ref[...] = owners_sum(rows[1:2, :], forward) + owners_sum(rows[3:4, :], backward)


def far_body(place_ref, near_ref, far_ref, own_ref, before_ref, after_ref, before_coef_ref,
             after_coef_ref, take_ref, give_ref, out_ref):
    group = place_ref[0]
    both = jnp.concatenate([before_coef_ref[...], after_coef_ref[...]], axis=0)
    rows, cols = slot_info(own_ref)
    i_low, j_group, j_low, live = (cols[:, k : k + 1] for k in (1, 2, 3, 4))
    step = (j_group - group) & (GROUPS - 1)
    index = jnp.where(step == 0, -1, jnp.where(step == 1, DEVS, 0) + (j_low >> 2))
    right = picked(index, j_low, both)
    forward = in_lanes(forward_sums(own_ref, right, give_ref), live == 1, i_low)
    total = far_ref[...] + owners_sum(rows[1:2, :], forward)
    infos = [slot_info(ref) for ref in (before_ref, after_ref)]
    cols = jnp.concatenate([cols for _, cols in infos], axis=0)
    i_low, j_group, j_low, live = (cols[:, k : k + 1] for k in (1, 2, 3, 4))
    slots = rows.shape[1]
    side = jnp.where(iota((2 * slots, 1), 0) < slots, 0, DEVS)
    left = picked(side + (i_low >> 2), i_low, both)
    backward = in_lanes(
        backward_sums((before_ref, after_ref), left, take_ref),
        (live == 1) & (j_group == group),
        j_low,
    )
    for k in range(2):
        total = total + owners_sum(infos[k][0][3:4, :], backward[k * slots : k * slots + slots])
    row = iota((8, 128), 0)
    for d in range(DEVS):
        near = near_ref[d * 8 : d * 8 + 8, :]
        near_high = near.astype(BF16).astype(F32)
        far = total[d : d + 1, :]
        far_high = far.astype(BF16).astype(F32)
        tail = jnp.where(row == 0, far_high, jnp.where(row == 1, far - far_high, 0.0))
        out_ref[d] = jnp.concatenate([near_high, near - near_high, tail], axis=0).astype(BF16)


def product_body(pieces_ref, bases_ref, krylov_ref, gram_ref, product_ref, copies_ref):
    total = jnp.sum(pieces_ref[...].astype(F32), axis=0)
    near = total[0:8, :] + total[8:16, :]
    coef = (total[16:17, :] + total[17:18, :]).astype(BF16).astype(F32)
    row, lane = iota((8, 128), 0), iota((8, 128), 1)
    spread = jnp.where((lane >> 5) == (row >> 1), coef, 0.0).astype(BF16)
    low = mm(spread, bases_ref[:, :128])
    high = mm(spread, bases_ref[:, 128:])
    product = near + jnp.where((row & 1) == 0, low, high)
    product_ref[...] = product
    acc = jnp.zeros((8, 128), F32)
    for r in range(8):
        acc = acc + krylov_ref[:, r * 128 : r * 128 + 128] * product[r : r + 1, :]
    proj = jnp.sum(acc, axis=1, keepdims=True)
    square = jnp.sum(product * product, axis=1, keepdims=True)
    values = jnp.where(lane == row, proj, 0.0) + jnp.where(lane == 72, square, 0.0)
    payload = jnp.sum(values, axis=0, keepdims=True) + gram_ref[...]
    for d in range(copies_ref.shape[0]):
        copies_ref[d] = payload


def spread_body(pieces_ref, out_ref):
    total = jnp.sum(pieces_ref[...], axis=0)
    for d in range(out_ref.shape[0]):
        out_ref[d] = total


def last_body(count, pieces_ref, product_ref, krylov_ref, next_ref, proj_ref):
    total = jnp.sum(pieces_ref[...], axis=0)
    row, lane = iota((8, 128), 0), iota((8, 128), 1)
    proj = jnp.sum(jnp.where(lane == row, total, 0.0), axis=1, keepdims=True)
    inside = (lane >= 8) & (lane < 72)
    first = jnp.sum(jnp.where(inside & (((lane - 8) >> 3) == row), proj, 0.0), axis=0, keepdims=True)
    second = jnp.sum(jnp.where(inside & ((lane & 7) == row), proj, 0.0), axis=0, keepdims=True)
    lane = iota((1, 128), 1)
    terms = total * jnp.where(lane < 8, -2.0 * total, first * second)
    terms = jnp.where(lane == 72, total, jnp.where(lane < 72, terms, 0.0))
    length_sq = jnp.sum(terms, axis=1, keepdims=True)
    scale = 1.0 / jnp.sqrt(jnp.maximum(length_sq, 0.0) / count)
    for r in range(8):
        taken = jnp.sum(proj * krylov_ref[:, r * 128 : r * 128 + 128], axis=0, keepdims=True)
        next_ref[r : r + 1, :] = (product_ref[r : r + 1, :] - taken) * scale
    proj_ref[...] = total[:, 0:8]


def all_reduce_sets():
    def number(y, core, z, x_high, x_low):
        return (y * 2 + core) * DEVS + z * NX + x_high * 2 + x_low

    ys, zs, bits = range(NY), range(NZ), range(2)
    first = [[number(y, c, z, h, l) for y in ys for h in bits] for c in bits for z in zs for l in bits]
    second = [[number(y, c, z, h, l) for c in bits for z in zs for l in bits] for y in ys for h in bits]
    return first, second


def local(
    direction, krylov, bases, near_tiles, near_pairs, near_mask, far_blocks, far_pairs, far_mask
):
    panels = direction.shape[0]
    rank_rows = bases.reshape(-1, bases.shape[2])
    place = lax.axis_index("group").astype(I32)[None]
    slots, far_slots = near_tiles.shape[0], far_blocks.shape[0]

    copies = call(
        pack_body,
        sds((DEVS, 16, 128), BF16),
        [HBM, HBM],
        [pltpu.VMEM((8, 128), F32), pltpu.VMEM(rank_rows.shape, BF16), pltpu.SemaphoreType.DMA((2,))],
    )(direction.reshape(8, 128), rank_rows)
    gathered = to_all(copies, "dev").reshape(-1, 128)
    bundle, tiles, gather, scatter, take, give, gram = call(
        prep_body,
        [
            sds((far_slots + 16, far_blocks.shape[1]), BF16),
            pltpu.VMEM(near_tiles.shape, BF16),
            sds((64, DEVS * 16), BF16),
            sds((DEVS * 8, 128), BF16),
            pltpu.VMEM((128, 1024), BF16),
            pltpu.VMEM((1024, 128), BF16),
            sds((1, 128), F32),
        ],
        [HBM] * 7,
        [
            pltpu.VMEM((2, far_slots), I32),
            pltpu.VMEM((1, far_slots), I32),
            pltpu.VMEM((2, slots), I32),
            pltpu.VMEM((1, slots), I32),
            pltpu.VMEM(krylov.shape, F32),
            pltpu.SemaphoreType.DMA((6,)),
            pltpu.SemaphoreType.DMA,
        ],
    )(near_tiles, far_blocks, far_pairs.T, far_mask[None], near_pairs.T, near_mask[None], krylov)
    before, after = group_shift(bundle, 1), group_shift(bundle, -1)

    coeffs = call(coeffs_body, sds((DEVS, 128), BF16), [VMEM])(gathered)
    coeffs_before, coeffs_after = group_shift(coeffs, 1), group_shift(coeffs, -1)
    near = call(near_body, sds((DEVS * 8, 128), F32), [VMEM] * 4)(gathered, gather, scatter, tiles)
    far = call(far_own_body, sds((DEVS, 128), F32), [SMEM] + [VMEM] * 4)(
        place, bundle, coeffs, take, give
    )
    parts = call(far_body, sds((DEVS, 24, 128), BF16), [SMEM] + [VMEM] * 9)(
        place, near, far, bundle, before, after, coeffs_before, coeffs_after, take, give
    )
    product, copies = call(
        product_body, [sds((8, 128), F32), sds((GROUPS, 1, 128), F32)], [VMEM] * 4
    )(to_all(parts, "dev"), rank_rows, krylov, gram)
    first, second = all_reduce_sets()
    copies = call(spread_body, sds((DEVS, 1, 128), F32), [VMEM])(
        to_all(copies, ("group", "dev"), first)
    )
    pieces = to_all(copies, ("group", "dev"), second)
    count = float(panels * DEVS * GROUPS)

    def finish(*refs):
        last_body(count, *refs)

    next_vector, projections = call(finish, [sds((8, 128), F32), sds((1, 8), F32)], [VMEM] * 3)(
        pieces, product, krylov
    )
    return (next_vector.reshape(-1), projections.reshape(-1))


def solution(mesh):
    in_specs = (
        P(("group", "dev")),
        P(None, ("group", "dev")),
        P(("group", "dev"), None, None),
        P(("group", "dev"), None, None),
        P(("group", "dev"), None),
        P(("group", "dev")),
        P(("group", "dev"), None),
        P(("group", "dev"), None),
        P(("group", "dev")),
    )
    out_specs = (P(("group", "dev")), P())
    return jax.shard_map(local, mesh=mesh, in_specs=in_specs, out_specs=out_specs, check_vma=False)
```

```python
import jax
import jax.numpy as jnp
from jax import lax
from jax.experimental import pallas as pl
from jax.experimental.pallas import tpu as pltpu
from jax.sharding import PartitionSpec as P

F32 = jnp.float32
BF16 = jnp.bfloat16
I32 = jnp.int32
NX, NZ, NY = 4, 8, 8
DEVS, GROUPS = NZ * NX, 2 * NY
VMEM = pl.BlockSpec(memory_space=pltpu.VMEM)
HBM = pl.BlockSpec(memory_space=pltpu.HBM)
sds = jax.ShapeDtypeStruct


def call(body, outs, specs, scratch=()):
    kernel = pl.pallas_call(
        body,
        out_shape=outs,
        in_specs=specs,
        out_specs=jax.tree.map(lambda _: VMEM, outs),
        scratch_shapes=list(scratch),
        compiler_params=pltpu.CompilerParams(vmem_limit_bytes=24 * 1024 * 1024),
    )

    def run(*args):
        return kernel(
            *(
                pltpu.with_memory_space_constraint(arg, pltpu.HBM) if spec is HBM else arg
                for arg, spec in zip(args, specs, strict=True)
            )
        )

    return run


def iota(shape, dim):
    return lax.broadcasted_iota(I32, shape, dim)


def mm(a, b):
    return lax.dot_general(a, b, (((1,), (0,)), ((), ())), preferred_element_type=F32)


def mm_t(a, b):
    return lax.dot_general(a, b, (((1,), (1,)), ((), ())), preferred_element_type=F32)


def mm_exact(a, b, dims):
    return lax.dot_general(
        a, b, (dims, ((), ())), precision=lax.Precision.HIGHEST, preferred_element_type=F32
    )


def halves(value):
    high = value.astype(BF16)
    return high, (value - high.astype(F32)).astype(BF16)


def one_hot(mask):
    return mask.astype(F32).astype(BF16)


def small(rows):
    return rows.astype(F32).astype(BF16)


def columns(rows):
    width = rows.shape[1]
    same = one_hot(iota((width, width), 0) == iota((width, width), 1))
    return mm_t(same, small(rows)).astype(I32)


def to_all(value, axis):
    return lax.all_to_all(value, axis, split_axis=0, concat_axis=0, tiled=True)


def group_shift(value, step):
    return lax.ppermute(value, "group", [(g, (g + step) % GROUPS) for g in range(GROUPS)])


def started(ends, sems):
    copies = [pltpu.make_async_copy(*end, sems.at[k]) for k, end in enumerate(ends)]
    for copy in copies:
        copy.start()
    return copies


def pack_body(direction_hbm, bases_hbm, out_ref, direction_ref, bases_ref, sems):
    for copy in started(((direction_hbm, direction_ref), (bases_hbm, bases_ref)), sems):
        copy.wait()
    xb = direction_ref[...].astype(BF16)
    rank_rows = bases_ref[...]
    low = mm_t(xb, rank_rows[:, :128])
    high = mm_t(xb, rank_rows[:, 128:])
    row = iota((8, 128), 0)
    twice = (iota((8, 128), 1) >> 5) * 2
    kept = jnp.where(row == twice, low, 0.0) + jnp.where(row == twice + 1, high, 0.0)
    coeffs = jnp.sum(kept, axis=0, keepdims=True)
    packed = jnp.concatenate([xb, jnp.where(row == 0, coeffs, 0.0).astype(BF16)], axis=0)
    for d in range(DEVS):
        out_ref[d] = packed


def prep_body(tiles_hbm, blocks_hbm, pairs_hbm, mask_hbm, near_pairs_hbm, near_mask_hbm, krylov_hbm,
              out_ref, tiles_ref, gather_ref, scatter_ref, gram_ref,
              pairs_ref, mask_ref, near_pairs_ref, near_mask_ref, krylov_ref, sems, tile_sem):
    fetched = pltpu.make_async_copy(tiles_hbm, tiles_ref, tile_sem)
    slots = blocks_hbm.shape[0]
    ends = (
        (blocks_hbm, out_ref.at[0:slots]),
        (pairs_hbm, pairs_ref),
        (mask_hbm, mask_ref),
        (near_pairs_hbm, near_pairs_ref),
        (near_mask_hbm, near_mask_ref),
        (krylov_hbm, krylov_ref),
    )
    copies = started(ends, sems)
    fetched.start()
    for copy in copies:
        copy.wait()
    i_row, j_row = pairs_ref[0:1, :], pairs_ref[1:2, :]
    step = ((j_row >> 7) - (i_row >> 7)) & (GROUPS - 1)
    which = jnp.where(step == 0, 0, jnp.where(step == 1, 2, 1))
    live = mask_ref[...]
    both = jnp.where(i_row == j_row, 0, live)
    row = iota((16, slots), 0)
    digits = jnp.zeros((16, slots), I32)
    for k, value in enumerate((i_row & 127, j_row & 127, which, live, both)):
        digits = jnp.where(row == k, value, digits)
    out_ref[slots : slots + 16, :] = jnp.zeros((16, out_ref.shape[1]), BF16)
    out_ref[slots : slots + 16, 0:slots] = small(digits)
    near = near_pairs_ref[...]
    live = near_mask_ref[...]
    near_slots = near.shape[1]
    row = iota((8, near_slots), 0)
    info = jnp.where(row == 0, near[0:1, :], jnp.where(row == 1, near[1:2, :], live))
    m = iota((64, near_slots), 0)
    pick = one_hot((m & 15) == iota((64, near_slots), 1))
    info_cols = mm_t(pick, small(info)).astype(I32)
    i_col, j_col = info_cols[:, 0:1], info_cols[:, 1:2]
    m = iota((64, 1), 0) >> 4
    c = jnp.where(m < 2, j_col, i_col)
    place = (c >> 2) * 16 + (c & 3) * 2 + (m & 1)
    gather_ref[...] = one_hot(iota((64, DEVS * 16), 1) == place)
    lane = iota((near_slots, 128), 1)
    pick = one_hot((lane & 15) == iota((near_slots, 128), 0))
    info_lanes = mm(small(info), pick).astype(I32)
    i_lane, j_lane, live_lane = (info_lanes[k : k + 1, :] for k in range(3))
    kind = (iota((1, 128), 1) >> 4) & 3
    used = (live_lane == 1) & ((kind < 2) | (i_lane != j_lane))
    target = jnp.where(kind < 2, i_lane, j_lane) * 2 + (kind & 1)
    target = jnp.where(used, target, -1)
    scatter_ref[...] = one_hot(iota((DEVS * 8, 128), 0) == target)
    rows = krylov_ref[...]
    gram = mm_exact(rows, rows, ((1,), (1,)))
    lane, row = iota((8, 128), 1) - 8, iota((8, 128), 0)
    inside = (lane >= 0) & (lane < 64)
    wide = mm_exact(gram, jnp.where(inside & ((lane & 7) == row), 1.0, 0.0), ((1,), (0,)))
    gram_ref[...] = jnp.sum(
        jnp.where(inside & ((lane >> 3) == row), wide, 0.0), axis=0, keepdims=True
    )
    fetched.wait()


def coeffs_body(gathered_ref, out_ref):
    rows = iota((DEVS, DEVS * 16), 0) * 16 + 8
    pick = one_hot(iota((DEVS, DEVS * 16), 1) == rows)
    out_ref[...] = mm(pick, gathered_ref[...]).astype(BF16)


def near_body(gathered_ref, gather_ref, scatter_ref, tiles_ref, out_ref):
    taken = mm(gather_ref[...], gathered_ref[...])
    right = jnp.concatenate([taken[0:16], taken[16:32]], axis=1).astype(BF16)
    left = jnp.concatenate([taken[32:48], taken[48:64]], axis=1).astype(BF16)
    slot = iota((16, 256), 0)
    forward = jnp.zeros((16, 256), F32)
    backward = jnp.zeros((16, 256), F32)
    for s in range(tiles_ref.shape[0]):
        tile = tiles_ref[s]
        forward = jnp.where(slot == s, mm_t(right, tile), forward)
        backward = jnp.where(slot == s, mm(left, tile), backward)
    values = jnp.concatenate(
        [forward[:, :128], forward[:, 128:], backward[:, :128], backward[:, 128:]], axis=0
    )
    out_ref[...] = mm(scatter_ref[...], jnp.concatenate(halves(values), axis=0))


def far_body(near_ref, own_ref, before_ref, after_ref, own_coef_ref, before_coef_ref,
             after_coef_ref, out_ref):
    bundles = (own_ref, before_ref, after_ref)
    slots = own_ref.shape[0] - 16
    total_slots = 3 * slots
    rows = [b[slots : slots + 16, 0:slots].astype(F32).astype(I32) for b in bundles]
    cols = jnp.concatenate([columns(r) for r in rows], axis=0)
    i_low, j_low, which, live, both = (cols[:, k : k + 1] for k in range(5))
    coeffs = jnp.concatenate([own_coef_ref[...], before_coef_ref[...], after_coef_ref[...]], axis=0)

    def gather(index, low):
        n = low.shape[0]
        taken = mm(one_hot(iota((n, 3 * DEVS), 1) == index), coeffs)
        return jnp.where((iota((n, 128), 1) >> 5) == (low & 3), taken, 0.0).astype(BF16)

    slot = iota((total_slots, 1), 0)
    source = jnp.where(slot < slots, 0, jnp.where(slot < 2 * slots, 1, 2))
    right = gather(which[0:slots] * DEVS + (j_low[0:slots] >> 2), j_low[0:slots])
    left = gather(source * DEVS + (i_low >> 2), i_low)
    sub, lane = iota((128, 128), 0), iota((128, 128), 1)
    tiled = mm(right, one_hot((sub & 31) == (lane & 31)))
    forward = jnp.zeros((slots, 128), F32)
    backward = jnp.zeros((total_slots, 128), F32)
    for k in range(8):
        parts = [b[0:slots, k * 128 : k * 128 + 128] for b in bundles]
        part = jnp.concatenate(parts, axis=0).astype(F32)
        backward = backward + part * mm(left, one_hot((sub & 31) == 4 * k + (lane >> 5)))
        give = one_hot((lane & 31) == 4 * k + (sub >> 5))
        for piece in halves(part[0:slots] * tiled):
            forward = forward + mm(piece, give)
    backward = backward + pltpu.roll(backward, 64, 1)
    backward = backward + pltpu.roll(backward, 32, 1)
    lane_block = iota((total_slots, 128), 1) >> 5
    forward = jnp.where(
        (live[0:slots] == 1) & (lane_block[0:slots] == (i_low[0:slots] & 3)), forward, 0.0
    )
    wanted = jnp.where(source == 0, 0, jnp.where(source == 1, 2, 1))
    mine = (both == 1) & (which == wanted)
    backward = jnp.where(mine & (lane_block == (j_low & 3)), backward, 0.0)
    owner = iota((DEVS, slots), 0)
    total = jnp.zeros((DEVS, 128), F32)
    pick = one_hot(owner == (rows[0][0:1, :] >> 2))
    for part in halves(forward):
        total = total + mm(pick, part)
    for k in range(3):
        pick = one_hot(owner == (rows[k][1:2, :] >> 2))
        for part in halves(backward[k * slots : k * slots + slots]):
            total = total + mm(pick, part)
    row = iota((8, 128), 0)
    for d in range(DEVS):
        near = near_ref[d * 8 : d * 8 + 8, :]
        near_high = near.astype(BF16).astype(F32)
        far = total[d : d + 1, :]
        far_high = far.astype(BF16).astype(F32)
        tail = jnp.where(row == 0, far_high, jnp.where(row == 1, far - far_high, 0.0))
        out_ref[d] = jnp.concatenate([near_high, near - near_high, tail], axis=0).astype(BF16)


def product_body(pieces_ref, bases_ref, krylov_ref, gram_ref, product_ref, copies_ref):
    total = jnp.sum(pieces_ref[...].astype(F32), axis=0)
    near = total[0:8, :] + total[8:16, :]
    coef = (total[16:17, :] + total[17:18, :]).astype(BF16).astype(F32)
    row, lane = iota((8, 128), 0), iota((8, 128), 1)
    spread = jnp.where((lane >> 5) == (row >> 1), coef, 0.0).astype(BF16)
    low = mm(spread, bases_ref[:, :128])
    high = mm(spread, bases_ref[:, 128:])
    product = near + jnp.where((row & 1) == 0, low, high)
    product_ref[...] = product
    acc = jnp.zeros((8, 128), F32)
    for r in range(8):
        acc = acc + krylov_ref[:, r * 128 : r * 128 + 128] * product[r : r + 1, :]
    proj = jnp.sum(acc, axis=1, keepdims=True)
    square = jnp.sum(product * product, axis=1, keepdims=True)
    values = jnp.where(lane == row, proj, 0.0) + jnp.where(lane == 72, square, 0.0)
    payload = jnp.sum(values, axis=0, keepdims=True) + gram_ref[...]
    for d in range(copies_ref.shape[0]):
        copies_ref[d] = payload


def spread_body(pieces_ref, out_ref):
    total = jnp.sum(pieces_ref[...], axis=0)
    for d in range(out_ref.shape[0]):
        out_ref[d] = total


def last_body(count, pieces_ref, product_ref, krylov_ref, next_ref, proj_ref):
    total = jnp.sum(pieces_ref[...], axis=0)
    row, lane = iota((8, 128), 0), iota((8, 128), 1)
    proj = jnp.sum(jnp.where(lane == row, total, 0.0), axis=1, keepdims=True)
    inside = (lane >= 8) & (lane < 72)
    first = jnp.sum(jnp.where(inside & (((lane - 8) >> 3) == row), proj, 0.0), axis=0, keepdims=True)
    second = jnp.sum(jnp.where(inside & ((lane & 7) == row), proj, 0.0), axis=0, keepdims=True)
    lane = iota((1, 128), 1)
    terms = total * jnp.where(lane < 8, -2.0 * total, first * second)
    terms = jnp.where(lane == 72, total, jnp.where(lane < 72, terms, 0.0))
    length_sq = jnp.sum(terms, axis=1, keepdims=True)
    scale = 1.0 / jnp.sqrt(jnp.maximum(length_sq, 0.0) / count)
    for r in range(8):
        taken = jnp.sum(proj * krylov_ref[:, r * 128 : r * 128 + 128], axis=0, keepdims=True)
        next_ref[r : r + 1, :] = (product_ref[r : r + 1, :] - taken) * scale
    proj_ref[...] = total[:, 0:8]


def local(
    direction, krylov, bases, near_tiles, near_pairs, near_mask, far_blocks, far_pairs, far_mask
):
    panels = direction.shape[0]
    rank_rows = bases.reshape(-1, bases.shape[2])
    slots, far_slots = near_tiles.shape[0], far_blocks.shape[0]

    copies = call(
        pack_body,
        pltpu.VMEM((DEVS, 16, 128), BF16),
        [HBM, HBM],
        [pltpu.VMEM((8, 128), F32), pltpu.VMEM(rank_rows.shape, BF16), pltpu.SemaphoreType.DMA((2,))],
    )(direction.reshape(8, 128), rank_rows)
    gathered = to_all(copies, "dev").reshape(-1, 128)
    bundle, tiles, gather, scatter, gram = call(
        prep_body,
        [
            sds((far_slots + 16, far_blocks.shape[1]), BF16),
            pltpu.VMEM(near_tiles.shape, BF16),
            sds((64, DEVS * 16), BF16),
            sds((DEVS * 8, 128), BF16),
            sds((1, 128), F32),
        ],
        [HBM] * 7,
        [
            pltpu.VMEM((2, far_slots), I32),
            pltpu.VMEM((1, far_slots), I32),
            pltpu.VMEM((2, slots), I32),
            pltpu.VMEM((1, slots), I32),
            pltpu.VMEM(krylov.shape, F32),
            pltpu.SemaphoreType.DMA((6,)),
            pltpu.SemaphoreType.DMA,
        ],
    )(near_tiles, far_blocks, far_pairs.T, far_mask[None], near_pairs.T, near_mask[None], krylov)
    before, after = group_shift(bundle, 1), group_shift(bundle, -1)

    coeffs = call(coeffs_body, sds((DEVS, 128), BF16), [VMEM])(gathered)
    coeffs_before, coeffs_after = group_shift(coeffs, 1), group_shift(coeffs, -1)
    near = call(near_body, sds((DEVS * 8, 128), F32), [VMEM] * 4)(gathered, gather, scatter, tiles)
    parts = call(far_body, sds((DEVS, 24, 128), BF16), [VMEM] * 7)(
        near, bundle, before, after, coeffs, coeffs_before, coeffs_after
    )
    product, copies = call(
        product_body, [sds((8, 128), F32), sds((GROUPS, 1, 128), F32)], [VMEM] * 4
    )(to_all(parts, "dev"), rank_rows, krylov, gram)
    copies = call(spread_body, sds((DEVS, 1, 128), F32), [VMEM])(to_all(copies, "group"))
    pieces = to_all(copies, "dev")
    count = float(panels * DEVS * GROUPS)

    def finish(*refs):
        last_body(count, *refs)

    next_vector, projections = call(finish, [sds((8, 128), F32), sds((1, 8), F32)], [VMEM] * 3)(
        pieces, product, krylov
    )
    return (next_vector.reshape(-1), projections.reshape(-1))


def solution(mesh):
    in_specs = (
        P(("group", "dev")),
        P(None, ("group", "dev")),
        P(("group", "dev"), None, None),
        P(("group", "dev"), None, None),
        P(("group", "dev"), None),
        P(("group", "dev")),
        P(("group", "dev"), None),
        P(("group", "dev"), None),
        P(("group", "dev")),
    )
    out_specs = (P(("group", "dev")), P())
    return jax.shard_map(local, mesh=mesh, in_specs=in_specs, out_specs=out_specs, check_vma=False)
```

```python
import jax
import jax.numpy as jnp
from jax import lax
from jax.experimental import pallas as pl
from jax.experimental.pallas import tpu as pltpu
from jax.sharding import PartitionSpec as P

F32 = jnp.float32
BF16 = jnp.bfloat16
I32 = jnp.int32
NX, NZ, NY = 4, 8, 8
DEVS, GROUPS = NZ * NX, 2 * NY
VMEM = pl.BlockSpec(memory_space=pltpu.VMEM)
HBM = pl.BlockSpec(memory_space=pltpu.HBM)
sds = jax.ShapeDtypeStruct


def call(body, outs, specs, scratch=()):
    kernel = pl.pallas_call(
        body,
        out_shape=outs,
        in_specs=specs,
        out_specs=jax.tree.map(lambda _: VMEM, outs),
        scratch_shapes=list(scratch),
        compiler_params=pltpu.CompilerParams(vmem_limit_bytes=24 * 1024 * 1024),
    )

    def run(*args):
        return kernel(
            *(
                pltpu.with_memory_space_constraint(arg, pltpu.HBM) if spec is HBM else arg
                for arg, spec in zip(args, specs, strict=True)
            )
        )

    return run


def iota(shape, dim):
    return lax.broadcasted_iota(I32, shape, dim)


def mm(a, b):
    return lax.dot_general(a, b, (((1,), (0,)), ((), ())), preferred_element_type=F32)


def mm_t(a, b):
    return lax.dot_general(a, b, (((1,), (1,)), ((), ())), preferred_element_type=F32)


def mm_exact(a, b, dims):
    return lax.dot_general(
        a, b, (dims, ((), ())), precision=lax.Precision.HIGHEST, preferred_element_type=F32
    )


def halves(value):
    high = value.astype(BF16)
    return high, (value - high.astype(F32)).astype(BF16)


def one_hot(mask):
    return mask.astype(F32).astype(BF16)


def small(rows):
    return rows.astype(F32).astype(BF16)


def columns(rows):
    width = rows.shape[1]
    same = one_hot(iota((width, width), 0) == iota((width, width), 1))
    return mm_t(same, small(rows)).astype(I32)


def to_all(value, axis):
    return lax.all_to_all(value, axis, split_axis=0, concat_axis=0, tiled=True)


def group_shift(value, step):
    return lax.ppermute(value, "group", [(g, (g + step) % GROUPS) for g in range(GROUPS)])


def started(ends, sems):
    copies = [pltpu.make_async_copy(*end, sems.at[k]) for k, end in enumerate(ends)]
    for copy in copies:
        copy.start()
    return copies


def pack_body(direction_hbm, bases_hbm, out_ref, direction_ref, bases_ref, sems):
    for copy in started(((direction_hbm, direction_ref), (bases_hbm, bases_ref)), sems):
        copy.wait()
    xb = direction_ref[...].astype(BF16)
    rank_rows = bases_ref[...]
    low = mm_t(xb, rank_rows[:, :128])
    high = mm_t(xb, rank_rows[:, 128:])
    row = iota((8, 128), 0)
    twice = (iota((8, 128), 1) >> 5) * 2
    kept = jnp.where(row == twice, low, 0.0) + jnp.where(row == twice + 1, high, 0.0)
    coeffs = jnp.sum(kept, axis=0, keepdims=True)
    packed = jnp.concatenate([xb, jnp.where(row == 0, coeffs, 0.0).astype(BF16)], axis=0)
    for d in range(DEVS):
        out_ref[d] = packed


def prep_body(tiles_hbm, blocks_hbm, pairs_hbm, mask_hbm, near_pairs_hbm, near_mask_hbm, krylov_hbm,
              out_ref, tiles_ref, gather_ref, scatter_ref, gram_ref,
              pairs_ref, mask_ref, near_pairs_ref, near_mask_ref, krylov_ref, sems, tile_sem):
    fetched = pltpu.make_async_copy(tiles_hbm, tiles_ref, tile_sem)
    slots = blocks_hbm.shape[0]
    ends = (
        (blocks_hbm, out_ref.at[0:slots]),
        (pairs_hbm, pairs_ref),
        (mask_hbm, mask_ref),
        (near_pairs_hbm, near_pairs_ref),
        (near_mask_hbm, near_mask_ref),
        (krylov_hbm, krylov_ref),
    )
    copies = started(ends, sems)
    fetched.start()
    for copy in copies:
        copy.wait()
    i_row, j_row = pairs_ref[0:1, :], pairs_ref[1:2, :]
    step = ((j_row >> 7) - (i_row >> 7)) & (GROUPS - 1)
    which = jnp.where(step == 0, 0, jnp.where(step == 1, 2, 1))
    live = mask_ref[...]
    both = jnp.where(i_row == j_row, 0, live)
    row = iota((16, slots), 0)
    digits = jnp.zeros((16, slots), I32)
    for k, value in enumerate((i_row & 127, j_row & 127, which, live, both)):
        digits = jnp.where(row == k, value, digits)
    out_ref[slots : slots + 16, :] = jnp.zeros((16, out_ref.shape[1]), BF16)
    out_ref[slots : slots + 16, 0:slots] = small(digits)
    near = near_pairs_ref[...]
    live = near_mask_ref[...]
    near_slots = near.shape[1]
    row = iota((8, near_slots), 0)
    info = jnp.where(row == 0, near[0:1, :], jnp.where(row == 1, near[1:2, :], live))
    m = iota((64, near_slots), 0)
    pick = one_hot((m & 15) == iota((64, near_slots), 1))
    info_cols = mm_t(pick, small(info)).astype(I32)
    i_col, j_col = info_cols[:, 0:1], info_cols[:, 1:2]
    m = iota((64, 1), 0) >> 4
    c = jnp.where(m < 2, j_col, i_col)
    place = (c >> 2) * 16 + (c & 3) * 2 + (m & 1)
    gather_ref[...] = one_hot(iota((64, DEVS * 16), 1) == place)
    lane = iota((near_slots, 128), 1)
    pick = one_hot((lane & 15) == iota((near_slots, 128), 0))
    info_lanes = mm(small(info), pick).astype(I32)
    i_lane, j_lane, live_lane = (info_lanes[k : k + 1, :] for k in range(3))
    kind = (iota((1, 128), 1) >> 4) & 3
    used = (live_lane == 1) & ((kind < 2) | (i_lane != j_lane))
    target = jnp.where(kind < 2, i_lane, j_lane) * 2 + (kind & 1)
    target = jnp.where(used, target, -1)
    scatter_ref[...] = one_hot(iota((DEVS * 8, 128), 0) == target)
    rows = krylov_ref[...]
    gram = mm_exact(rows, rows, ((1,), (1,)))
    lane, row = iota((8, 128), 1) - 8, iota((8, 128), 0)
    inside = (lane >= 0) & (lane < 64)
    wide = mm_exact(gram, jnp.where(inside & ((lane & 7) == row), 1.0, 0.0), ((1,), (0,)))
    gram_ref[...] = jnp.sum(
        jnp.where(inside & ((lane >> 3) == row), wide, 0.0), axis=0, keepdims=True
    )
    fetched.wait()


def coeffs_body(gathered_ref, out_ref):
    rows = iota((DEVS, DEVS * 16), 0) * 16 + 8
    pick = one_hot(iota((DEVS, DEVS * 16), 1) == rows)
    out_ref[...] = mm(pick, gathered_ref[...]).astype(BF16)


def near_body(gathered_ref, gather_ref, scatter_ref, tiles_ref, out_ref):
    taken = mm(gather_ref[...], gathered_ref[...])
    right = jnp.concatenate([taken[0:16], taken[16:32]], axis=1).astype(BF16)
    left = jnp.concatenate([taken[32:48], taken[48:64]], axis=1).astype(BF16)
    slot = iota((16, 256), 0)
    forward = jnp.zeros((16, 256), F32)
    backward = jnp.zeros((16, 256), F32)
    for s in range(tiles_ref.shape[0]):
        tile = tiles_ref[s]
        forward = jnp.where(slot == s, mm_t(right, tile), forward)
        backward = jnp.where(slot == s, mm(left, tile), backward)
    values = jnp.concatenate(
        [forward[:, :128], forward[:, 128:], backward[:, :128], backward[:, 128:]], axis=0
    )
    out_ref[...] = mm(scatter_ref[...], jnp.concatenate(halves(values), axis=0))


def far_prep_body(own_ref, before_ref, after_ref, pick_ref, lanes_ref, keep_ref, owner_ref,
                  take_ref, give_ref):
    slots = own_ref.shape[0] - 16
    rows = [
        ref[slots : slots + 16, 0:slots].astype(F32).astype(I32)
        for ref in (own_ref, before_ref, after_ref)
    ]
    cols = jnp.concatenate([columns(r) for r in [rows[0]] + rows], axis=0)
    i_low, j_low, which, live, both = (cols[:, k : k + 1] for k in range(5))
    slot = iota((4 * slots, 1), 0) // slots
    ahead = slot == 0
    low = jnp.where(ahead, j_low, i_low)
    source = jnp.where(ahead, which, slot - 1)
    pick_ref[...] = one_hot(iota((4 * slots, 3 * DEVS), 1) == source * DEVS + (low >> 2))
    block = iota((4 * slots, 128), 1) >> 5
    lanes_ref[...] = jnp.where(block == (low & 3), 1.0, 0.0)
    wanted = jnp.where(slot == 2, 2, jnp.where(slot == 3, 1, 0))
    used = jnp.where(ahead, live, jnp.where(which == wanted, both, 0))
    target = jnp.where(ahead, i_low, j_low)
    keep_ref[...] = jnp.where((used == 1) & (block == (target & 3)), 1.0, 0.0)
    owner = iota((DEVS, slots), 0)
    for k, row in enumerate([rows[0][0:1, :]] + [r[1:2, :] for r in rows]):
        owner_ref[k] = one_hot(owner == (row >> 2))
    for k in range(8):
        sub, lane = iota((128, 128), 0), iota((128, 128), 1)
        take_ref[k] = one_hot((sub & 31) == 4 * k + (lane >> 5))
        give_ref[k] = one_hot((lane & 31) == 4 * k + (sub >> 5))


def far_body(near_ref, own_ref, before_ref, after_ref, own_coef_ref, before_coef_ref,
             after_coef_ref, pick_ref, lanes_ref, keep_ref, owner_ref, take_ref, give_ref, out_ref):
    bundles = (own_ref, before_ref, after_ref)
    slots = own_ref.shape[0] - 16
    coeffs = jnp.concatenate([own_coef_ref[...], before_coef_ref[...], after_coef_ref[...]], axis=0)
    taken = (mm(pick_ref[...], coeffs) * lanes_ref[...]).astype(BF16)
    right, left = taken[0:slots], taken[slots:]
    sub, lane = iota((128, 128), 0), iota((128, 128), 1)
    tiled = mm(right, one_hot((sub & 31) == (lane & 31)))
    forward = jnp.zeros((slots, 128), F32)
    backward = jnp.zeros(left.shape, F32)
    for k in range(8):
        parts = [b[0:slots, k * 128 : k * 128 + 128] for b in bundles]
        part = jnp.concatenate(parts, axis=0).astype(F32)
        backward = backward + part * mm(left, take_ref[k])
        for piece in halves(part[0:slots] * tiled):
            forward = forward + mm(piece, give_ref[k])
    backward = backward + pltpu.roll(backward, 64, 1)
    backward = backward + pltpu.roll(backward, 32, 1)
    sums = jnp.concatenate([forward, backward], axis=0) * keep_ref[...]
    total = jnp.zeros((DEVS, 128), F32)
    for k in range(4):
        for part in halves(sums[k * slots : k * slots + slots]):
            total = total + mm(owner_ref[k], part)
    row = iota((8, 128), 0)
    for d in range(DEVS):
        near = near_ref[d * 8 : d * 8 + 8, :]
        low = jnp.where(row == 7, total[d : d + 1, :], near - near.astype(BF16).astype(F32))
        out_ref[d] = jnp.concatenate([near, low], axis=0).astype(BF16)


def product_body(pieces_ref, bases_ref, krylov_ref, gram_ref, product_ref, copies_ref):
    total = jnp.sum(pieces_ref[...].astype(F32), axis=0)
    row, lane = iota((8, 128), 0), iota((8, 128), 1)
    near = total[0:8, :] + jnp.where(row == 7, 0.0, total[8:16, :])
    coef = total[15:16, :].astype(BF16).astype(F32)
    spread = jnp.where((lane >> 5) == (row >> 1), coef, 0.0).astype(BF16)
    low = mm(spread, bases_ref[:, :128])
    high = mm(spread, bases_ref[:, 128:])
    product = near + jnp.where((row & 1) == 0, low, high)
    product_ref[...] = product
    acc = jnp.zeros((8, 128), F32)
    for r in range(8):
        acc = acc + krylov_ref[:, r * 128 : r * 128 + 128] * product[r : r + 1, :]
    proj = jnp.sum(acc, axis=1, keepdims=True)
    square = jnp.sum(product * product, axis=1, keepdims=True)
    values = jnp.where(lane == row, proj, 0.0) + jnp.where(lane == 72, square, 0.0)
    payload = jnp.sum(values, axis=0, keepdims=True) + gram_ref[...]
    for d in range(copies_ref.shape[0]):
        copies_ref[d] = payload


def spread_body(pieces_ref, out_ref):
    total = jnp.sum(pieces_ref[...], axis=0)
    for d in range(out_ref.shape[0]):
        out_ref[d] = total


def last_body(count, pieces_ref, product_ref, krylov_ref, next_ref, proj_ref):
    total = jnp.sum(pieces_ref[...], axis=0)
    row, lane = iota((8, 128), 0), iota((8, 128), 1)
    proj = jnp.sum(jnp.where(lane == row, total, 0.0), axis=1, keepdims=True)
    inside = (lane >= 8) & (lane < 72)
    first = jnp.sum(jnp.where(inside & (((lane - 8) >> 3) == row), proj, 0.0), axis=0, keepdims=True)
    second = jnp.sum(jnp.where(inside & ((lane & 7) == row), proj, 0.0), axis=0, keepdims=True)
    lane = iota((1, 128), 1)
    terms = total * jnp.where(lane < 8, -2.0 * total, first * second)
    terms = jnp.where(lane == 72, total, jnp.where(lane < 72, terms, 0.0))
    length_sq = jnp.sum(terms, axis=1, keepdims=True)
    scale = 1.0 / jnp.sqrt(jnp.maximum(length_sq, 0.0) / count)
    for r in range(8):
        taken = jnp.sum(proj * krylov_ref[:, r * 128 : r * 128 + 128], axis=0, keepdims=True)
        next_ref[r : r + 1, :] = (product_ref[r : r + 1, :] - taken) * scale
    proj_ref[...] = total[:, 0:8]


def local(
    direction, krylov, bases, near_tiles, near_pairs, near_mask, far_blocks, far_pairs, far_mask
):
    panels = direction.shape[0]
    rank_rows = bases.reshape(-1, bases.shape[2])
    slots, far_slots = near_tiles.shape[0], far_blocks.shape[0]

    copies = call(
        pack_body,
        sds((DEVS, 16, 128), BF16),
        [HBM, HBM],
        [pltpu.VMEM((8, 128), F32), pltpu.VMEM(rank_rows.shape, BF16), pltpu.SemaphoreType.DMA((2,))],
    )(direction.reshape(8, 128), rank_rows)
    gathered = to_all(copies, "dev").reshape(-1, 128)
    bundle, tiles, gather, scatter, gram = call(
        prep_body,
        [
            sds((far_slots + 16, far_blocks.shape[1]), BF16),
            pltpu.VMEM(near_tiles.shape, BF16),
            sds((64, DEVS * 16), BF16),
            sds((DEVS * 8, 128), BF16),
            sds((1, 128), F32),
        ],
        [HBM] * 7,
        [
            pltpu.VMEM((2, far_slots), I32),
            pltpu.VMEM((1, far_slots), I32),
            pltpu.VMEM((2, slots), I32),
            pltpu.VMEM((1, slots), I32),
            pltpu.VMEM(krylov.shape, F32),
            pltpu.SemaphoreType.DMA((6,)),
            pltpu.SemaphoreType.DMA,
        ],
    )(near_tiles, far_blocks, far_pairs.T, far_mask[None], near_pairs.T, near_mask[None], krylov)
    before, after = group_shift(bundle, 1), group_shift(bundle, -1)

    coeffs = call(coeffs_body, sds((DEVS, 128), BF16), [VMEM])(gathered)
    coeffs_before, coeffs_after = group_shift(coeffs, 1), group_shift(coeffs, -1)
    near = call(near_body, sds((DEVS * 8, 128), F32), [VMEM] * 4)(gathered, gather, scatter, tiles)
    far_prep = call(
        far_prep_body,
        [
            pltpu.VMEM((4 * far_slots, 3 * DEVS), BF16),
            pltpu.VMEM((4 * far_slots, 128), F32),
            pltpu.VMEM((4 * far_slots, 128), F32),
            pltpu.VMEM((4, DEVS, far_slots), BF16),
            pltpu.VMEM((8, 128, 128), BF16),
            pltpu.VMEM((8, 128, 128), BF16),
        ],
        [VMEM] * 3,
    )(bundle, before, after)
    parts = call(far_body, sds((DEVS, 16, 128), BF16), [VMEM] * 13)(
        near, bundle, before, after, coeffs, coeffs_before, coeffs_after, *far_prep
    )
    product, copies = call(
        product_body, [sds((8, 128), F32), sds((GROUPS, 1, 128), F32)], [VMEM] * 4
    )(to_all(parts, "dev"), rank_rows, krylov, gram)
    copies = call(spread_body, sds((DEVS, 1, 128), F32), [VMEM])(to_all(copies, "group"))
    pieces = to_all(copies, "dev")
    count = float(panels * DEVS * GROUPS)

    def finish(*refs):
        last_body(count, *refs)

    next_vector, projections = call(finish, [sds((8, 128), F32), sds((1, 8), F32)], [VMEM] * 3)(
        pieces, product, krylov
    )
    return (next_vector.reshape(-1), projections.reshape(-1))


def solution(mesh):
    in_specs = (
        P(("group", "dev")),
        P(None, ("group", "dev")),
        P(("group", "dev"), None, None),
        P(("group", "dev"), None, None),
        P(("group", "dev"), None),
        P(("group", "dev")),
        P(("group", "dev"), None),
        P(("group", "dev"), None),
        P(("group", "dev")),
    )
    out_specs = (P(("group", "dev")), P())
    return jax.shard_map(local, mesh=mesh, in_specs=in_specs, out_specs=out_specs, check_vma=False)
```

```python
import jax
import jax.numpy as jnp
from jax import lax
from jax.experimental import pallas as pl
from jax.experimental.pallas import tpu as pltpu
from jax.sharding import PartitionSpec as P

F32 = jnp.float32
BF16 = jnp.bfloat16
I32 = jnp.int32
NX, NZ, NY = 4, 8, 8
DEVS, GROUPS = NZ * NX, 2 * NY
VMEM = pl.BlockSpec(memory_space=pltpu.VMEM)
HBM = pl.BlockSpec(memory_space=pltpu.HBM)
sds = jax.ShapeDtypeStruct


def call(body, outs, specs, scratch=()):
    kernel = pl.pallas_call(
        body,
        out_shape=outs,
        in_specs=specs,
        out_specs=jax.tree.map(lambda _: VMEM, outs),
        scratch_shapes=list(scratch),
        compiler_params=pltpu.CompilerParams(vmem_limit_bytes=24 * 1024 * 1024),
    )

    def run(*args):
        return kernel(
            *(
                pltpu.with_memory_space_constraint(arg, pltpu.HBM) if spec is HBM else arg
                for arg, spec in zip(args, specs, strict=True)
            )
        )

    return run


def iota(shape, dim):
    return lax.broadcasted_iota(I32, shape, dim)


def mm(a, b):
    return lax.dot_general(a, b, (((1,), (0,)), ((), ())), preferred_element_type=F32)


def mm_t(a, b):
    return lax.dot_general(a, b, (((1,), (1,)), ((), ())), preferred_element_type=F32)


def mm_exact(a, b, dims):
    return lax.dot_general(
        a, b, (dims, ((), ())), precision=lax.Precision.HIGHEST, preferred_element_type=F32
    )


def halves(value):
    high = value.astype(BF16)
    return high, (value - high.astype(F32)).astype(BF16)


def one_hot(mask):
    return mask.astype(F32).astype(BF16)


def small(rows):
    return rows.astype(F32).astype(BF16)


def columns(rows):
    width = rows.shape[1]
    same = one_hot(iota((width, width), 0) == iota((width, width), 1))
    return mm_t(same, small(rows)).astype(I32)


def to_all(value, axis):
    return lax.all_to_all(value, axis, split_axis=0, concat_axis=0, tiled=True)


def group_shift(value, step):
    return lax.ppermute(value, "group", [(g, (g + step) % GROUPS) for g in range(GROUPS)])


def started(ends, sems):
    copies = [pltpu.make_async_copy(*end, sems.at[k]) for k, end in enumerate(ends)]
    for copy in copies:
        copy.start()
    return copies


def pack_body(direction_hbm, bases_hbm, out_ref, direction_ref, bases_ref, sems):
    for copy in started(((direction_hbm, direction_ref), (bases_hbm, bases_ref)), sems):
        copy.wait()
    xb = direction_ref[...].astype(BF16)
    rank_rows = bases_ref[...]
    low = mm_t(xb, rank_rows[:, :128])
    high = mm_t(xb, rank_rows[:, 128:])
    row = iota((8, 128), 0)
    twice = (iota((8, 128), 1) >> 5) * 2
    kept = jnp.where(row == twice, low, 0.0) + jnp.where(row == twice + 1, high, 0.0)
    coeffs = jnp.sum(kept, axis=0, keepdims=True)
    packed = jnp.concatenate([xb, jnp.where(row == 0, coeffs, 0.0).astype(BF16)], axis=0)
    for d in range(DEVS):
        out_ref[d] = packed


def prep_body(tiles_hbm, blocks_hbm, pairs_hbm, mask_hbm, near_pairs_hbm, near_mask_hbm, krylov_hbm,
              out_ref, tiles_ref, gather_ref, scatter_ref, gram_ref,
              pairs_ref, mask_ref, near_pairs_ref, near_mask_ref, krylov_ref, sems, tile_sem):
    fetched = pltpu.make_async_copy(tiles_hbm, tiles_ref, tile_sem)
    slots = blocks_hbm.shape[0]
    ends = (
        (blocks_hbm, out_ref.at[0:slots]),
        (pairs_hbm, pairs_ref),
        (mask_hbm, mask_ref),
        (near_pairs_hbm, near_pairs_ref),
        (near_mask_hbm, near_mask_ref),
        (krylov_hbm, krylov_ref),
    )
    copies = started(ends, sems)
    fetched.start()
    for copy in copies:
        copy.wait()
    i_row, j_row = pairs_ref[0:1, :], pairs_ref[1:2, :]
    step = ((j_row >> 7) - (i_row >> 7)) & (GROUPS - 1)
    which = jnp.where(step == 0, 0, jnp.where(step == 1, 2, 1))
    live = mask_ref[...]
    both = jnp.where(i_row == j_row, 0, live)
    row = iota((16, slots), 0)
    digits = jnp.zeros((16, slots), I32)
    for k, value in enumerate((i_row & 127, j_row & 127, which, live, both)):
        digits = jnp.where(row == k, value, digits)
    out_ref[slots : slots + 16, :] = jnp.zeros((16, out_ref.shape[1]), BF16)
    out_ref[slots : slots + 16, 0:slots] = small(digits)
    near = near_pairs_ref[...]
    live = near_mask_ref[...]
    near_slots = near.shape[1]
    row = iota((8, near_slots), 0)
    info = jnp.where(row == 0, near[0:1, :], jnp.where(row == 1, near[1:2, :], live))
    m = iota((64, near_slots), 0)
    pick = one_hot((m & 15) == iota((64, near_slots), 1))
    info_cols = mm_t(pick, small(info)).astype(I32)
    i_col, j_col = info_cols[:, 0:1], info_cols[:, 1:2]
    m = iota((64, 1), 0) >> 4
    c = jnp.where(m < 2, j_col, i_col)
    place = (c >> 2) * 16 + (c & 3) * 2 + (m & 1)
    gather_ref[...] = one_hot(iota((64, DEVS * 16), 1) == place)
    lane = iota((near_slots, 128), 1)
    pick = one_hot((lane & 15) == iota((near_slots, 128), 0))
    info_lanes = mm(small(info), pick).astype(I32)
    i_lane, j_lane, live_lane = (info_lanes[k : k + 1, :] for k in range(3))
    kind = (iota((1, 128), 1) >> 4) & 3
    used = (live_lane == 1) & ((kind < 2) | (i_lane != j_lane))
    target = jnp.where(kind < 2, i_lane, j_lane) * 2 + (kind & 1)
    target = jnp.where(used, target, -1)
    scatter_ref[...] = one_hot(iota((DEVS * 8, 128), 0) == target)
    rows = krylov_ref[...]
    gram = mm_exact(rows, rows, ((1,), (1,)))
    lane, row = iota((8, 128), 1) - 8, iota((8, 128), 0)
    inside = (lane >= 0) & (lane < 64)
    wide = mm_exact(gram, jnp.where(inside & ((lane & 7) == row), 1.0, 0.0), ((1,), (0,)))
    gram_ref[...] = jnp.sum(
        jnp.where(inside & ((lane >> 3) == row), wide, 0.0), axis=0, keepdims=True
    )
    fetched.wait()


def coeffs_body(gathered_ref, out_ref):
    rows = iota((DEVS, DEVS * 16), 0) * 16 + 8
    pick = one_hot(iota((DEVS, DEVS * 16), 1) == rows)
    out_ref[...] = mm(pick, gathered_ref[...]).astype(BF16)


def near_body(gathered_ref, gather_ref, scatter_ref, tiles_ref, own_ref, before_ref, after_ref,
              out_ref, *far_refs):
    far_prep(own_ref, before_ref, after_ref, *far_refs)
    taken = mm(gather_ref[...], gathered_ref[...])
    right = jnp.concatenate([taken[0:16], taken[16:32]], axis=1).astype(BF16)
    left = jnp.concatenate([taken[32:48], taken[48:64]], axis=1).astype(BF16)
    slot = iota((16, 256), 0)
    forward = jnp.zeros((16, 256), F32)
    backward = jnp.zeros((16, 256), F32)
    for s in range(tiles_ref.shape[0]):
        tile = tiles_ref[s]
        forward = jnp.where(slot == s, mm_t(right, tile), forward)
        backward = jnp.where(slot == s, mm(left, tile), backward)
    values = jnp.concatenate(
        [forward[:, :128], forward[:, 128:], backward[:, :128], backward[:, 128:]], axis=0
    )
    out_ref[...] = mm(scatter_ref[...], jnp.concatenate(halves(values), axis=0))


def far_prep(own_ref, before_ref, after_ref, pick_ref, lanes_ref, keep_ref, owner_ref, take_ref,
             give_ref):
    slots = own_ref.shape[0] - 16
    rows = [
        ref[slots : slots + 16, 0:slots].astype(F32).astype(I32)
        for ref in (own_ref, before_ref, after_ref)
    ]
    cols = jnp.concatenate([columns(r) for r in [rows[0]] + rows], axis=0)
    i_low, j_low, which, live, both = (cols[:, k : k + 1] for k in range(5))
    slot = iota((4 * slots, 1), 0) // slots
    ahead = slot == 0
    low = jnp.where(ahead, j_low, i_low)
    source = jnp.where(ahead, which, slot - 1)
    pick_ref[...] = one_hot(iota((4 * slots, 3 * DEVS), 1) == source * DEVS + (low >> 2))
    block = iota((4 * slots, 128), 1) >> 5
    lanes_ref[...] = jnp.where(block == (low & 3), 1.0, 0.0)
    wanted = jnp.where(slot == 2, 2, jnp.where(slot == 3, 1, 0))
    used = jnp.where(ahead, live, jnp.where(which == wanted, both, 0))
    target = jnp.where(ahead, i_low, j_low)
    keep_ref[...] = jnp.where((used == 1) & (block == (target & 3)), 1.0, 0.0)
    owner = iota((DEVS, slots), 0)
    for k, row in enumerate([rows[0][0:1, :]] + [r[1:2, :] for r in rows]):
        owner_ref[k] = one_hot(owner == (row >> 2))
    for k in range(8):
        sub, lane = iota((128, 128), 0), iota((128, 128), 1)
        take_ref[k] = one_hot((sub & 31) == 4 * k + (lane >> 5))
        give_ref[k] = one_hot((lane & 31) == 4 * k + (sub >> 5))


def far_body(near_ref, own_ref, before_ref, after_ref, own_coef_ref, before_coef_ref,
             after_coef_ref, pick_ref, lanes_ref, keep_ref, owner_ref, take_ref, give_ref, out_ref):
    bundles = (own_ref, before_ref, after_ref)
    slots = own_ref.shape[0] - 16
    coeffs = jnp.concatenate([own_coef_ref[...], before_coef_ref[...], after_coef_ref[...]], axis=0)
    taken = (mm(pick_ref[...], coeffs) * lanes_ref[...]).astype(BF16)
    right, left = taken[0:slots], taken[slots:]
    sub, lane = iota((128, 128), 0), iota((128, 128), 1)
    tiled = mm(right, one_hot((sub & 31) == (lane & 31)))
    forward = jnp.zeros((slots, 128), F32)
    backward = jnp.zeros(left.shape, F32)
    for k in range(8):
        parts = [b[0:slots, k * 128 : k * 128 + 128] for b in bundles]
        part = jnp.concatenate(parts, axis=0).astype(F32)
        backward = backward + part * mm(left, take_ref[k])
        for piece in halves(part[0:slots] * tiled):
            forward = forward + mm(piece, give_ref[k])
    backward = backward + pltpu.roll(backward, 64, 1)
    backward = backward + pltpu.roll(backward, 32, 1)
    sums = jnp.concatenate([forward, backward], axis=0) * keep_ref[...]
    total = jnp.zeros((DEVS, 128), F32)
    for k in range(4):
        for part in halves(sums[k * slots : k * slots + slots]):
            total = total + mm(owner_ref[k], part)
    row = iota((8, 128), 0)
    for d in range(DEVS):
        near = near_ref[d * 8 : d * 8 + 8, :]
        low = jnp.where(row == 7, total[d : d + 1, :], near - near.astype(BF16).astype(F32))
        out_ref[d] = jnp.concatenate([near, low], axis=0).astype(BF16)


def product_body(pieces_ref, bases_ref, krylov_ref, gram_ref, product_ref, copies_ref):
    total = jnp.sum(pieces_ref[...].astype(F32), axis=0)
    row, lane = iota((8, 128), 0), iota((8, 128), 1)
    near = total[0:8, :] + jnp.where(row == 7, 0.0, total[8:16, :])
    coef = total[15:16, :].astype(BF16).astype(F32)
    spread = jnp.where((lane >> 5) == (row >> 1), coef, 0.0).astype(BF16)
    low = mm(spread, bases_ref[:, :128])
    high = mm(spread, bases_ref[:, 128:])
    product = near + jnp.where((row & 1) == 0, low, high)
    product_ref[...] = product
    acc = jnp.zeros((8, 128), F32)
    for r in range(8):
        acc = acc + krylov_ref[:, r * 128 : r * 128 + 128] * product[r : r + 1, :]
    proj = jnp.sum(acc, axis=1, keepdims=True)
    square = jnp.sum(product * product, axis=1, keepdims=True)
    values = jnp.where(lane == row, proj, 0.0) + jnp.where(lane == 72, square, 0.0)
    payload = jnp.sum(values, axis=0, keepdims=True) + gram_ref[...]
    for d in range(copies_ref.shape[0]):
        copies_ref[d] = payload


def spread_body(pieces_ref, out_ref):
    total = jnp.sum(pieces_ref[...], axis=0)
    for d in range(out_ref.shape[0]):
        out_ref[d] = total


def last_body(count, pieces_ref, product_ref, krylov_ref, next_ref, proj_ref):
    total = jnp.sum(pieces_ref[...], axis=0)
    row, lane = iota((8, 128), 0), iota((8, 128), 1)
    proj = jnp.sum(jnp.where(lane == row, total, 0.0), axis=1, keepdims=True)
    inside = (lane >= 8) & (lane < 72)
    first = jnp.sum(jnp.where(inside & (((lane - 8) >> 3) == row), proj, 0.0), axis=0, keepdims=True)
    second = jnp.sum(jnp.where(inside & ((lane & 7) == row), proj, 0.0), axis=0, keepdims=True)
    lane = iota((1, 128), 1)
    terms = total * jnp.where(lane < 8, -2.0 * total, first * second)
    terms = jnp.where(lane == 72, total, jnp.where(lane < 72, terms, 0.0))
    length_sq = jnp.sum(terms, axis=1, keepdims=True)
    scale = 1.0 / jnp.sqrt(jnp.maximum(length_sq, 0.0) / count)
    for r in range(8):
        taken = jnp.sum(proj * krylov_ref[:, r * 128 : r * 128 + 128], axis=0, keepdims=True)
        next_ref[r : r + 1, :] = (product_ref[r : r + 1, :] - taken) * scale
    proj_ref[...] = total[:, 0:8]


def local(
    direction, krylov, bases, near_tiles, near_pairs, near_mask, far_blocks, far_pairs, far_mask
):
    panels = direction.shape[0]
    rank_rows = bases.reshape(-1, bases.shape[2])
    slots, far_slots = near_tiles.shape[0], far_blocks.shape[0]

    copies = call(
        pack_body,
        sds((DEVS, 16, 128), BF16),
        [HBM, HBM],
        [pltpu.VMEM((8, 128), F32), pltpu.VMEM(rank_rows.shape, BF16), pltpu.SemaphoreType.DMA((2,))],
    )(direction.reshape(8, 128), rank_rows)
    gathered = to_all(copies, "dev").reshape(-1, 128)
    bundle, tiles, gather, scatter, gram = call(
        prep_body,
        [
            sds((far_slots + 16, far_blocks.shape[1]), BF16),
            pltpu.VMEM(near_tiles.shape, BF16),
            sds((64, DEVS * 16), BF16),
            sds((DEVS * 8, 128), BF16),
            sds((1, 128), F32),
        ],
        [HBM] * 7,
        [
            pltpu.VMEM((2, far_slots), I32),
            pltpu.VMEM((1, far_slots), I32),
            pltpu.VMEM((2, slots), I32),
            pltpu.VMEM((1, slots), I32),
            pltpu.VMEM(krylov.shape, F32),
            pltpu.SemaphoreType.DMA((6,)),
            pltpu.SemaphoreType.DMA,
        ],
    )(near_tiles, far_blocks, far_pairs.T, far_mask[None], near_pairs.T, near_mask[None], krylov)
    before, after = group_shift(bundle, 1), group_shift(bundle, -1)

    coeffs = call(coeffs_body, sds((DEVS, 128), BF16), [VMEM])(gathered)
    coeffs_before, coeffs_after = group_shift(coeffs, 1), group_shift(coeffs, -1)
    near, *far_prepared = call(
        near_body,
        [
            sds((DEVS * 8, 128), F32),
            pltpu.VMEM((4 * far_slots, 3 * DEVS), BF16),
            pltpu.VMEM((4 * far_slots, 128), F32),
            pltpu.VMEM((4 * far_slots, 128), F32),
            pltpu.VMEM((4, DEVS, far_slots), BF16),
            pltpu.VMEM((8, 128, 128), BF16),
            pltpu.VMEM((8, 128, 128), BF16),
        ],
        [VMEM] * 7,
    )(gathered, gather, scatter, tiles, bundle, before, after)
    parts = call(far_body, sds((DEVS, 16, 128), BF16), [VMEM] * 13)(
        near, bundle, before, after, coeffs, coeffs_before, coeffs_after, *far_prepared
    )
    product, copies = call(
        product_body, [sds((8, 128), F32), sds((GROUPS, 1, 128), F32)], [VMEM] * 4
    )(to_all(parts, "dev"), rank_rows, krylov, gram)
    copies = call(spread_body, sds((DEVS, 1, 128), F32), [VMEM])(to_all(copies, "group"))
    pieces = to_all(copies, "dev")
    count = float(panels * DEVS * GROUPS)

    def finish(*refs):
        last_body(count, *refs)

    next_vector, projections = call(finish, [sds((8, 128), F32), sds((1, 8), F32)], [VMEM] * 3)(
        pieces, product, krylov
    )
    return (next_vector.reshape(-1), projections.reshape(-1))


def solution(mesh):
    in_specs = (
        P(("group", "dev")),
        P(None, ("group", "dev")),
        P(("group", "dev"), None, None),
        P(("group", "dev"), None, None),
        P(("group", "dev"), None),
        P(("group", "dev")),
        P(("group", "dev"), None),
        P(("group", "dev"), None),
        P(("group", "dev")),
    )
    out_specs = (P(("group", "dev")), P())
    return jax.shard_map(local, mesh=mesh, in_specs=in_specs, out_specs=out_specs, check_vma=False)
```

```python
import jax
import jax.numpy as jnp
from jax import lax
from jax.experimental import pallas as pl
from jax.experimental.pallas import tpu as pltpu
from jax.sharding import PartitionSpec as P

F32 = jnp.float32
BF16 = jnp.bfloat16
I32 = jnp.int32
NX, NZ, NY = 4, 8, 8
DEVS, GROUPS = NZ * NX, 2 * NY
VMEM = pl.BlockSpec(memory_space=pltpu.VMEM)
HBM = pl.BlockSpec(memory_space=pltpu.HBM)
SMEM = pl.BlockSpec(memory_space=pltpu.SMEM)
sds = jax.ShapeDtypeStruct


def call(body, outs, specs, scratch=()):
    kernel = pl.pallas_call(
        body,
        out_shape=outs,
        in_specs=specs,
        out_specs=jax.tree.map(lambda _: VMEM, outs),
        scratch_shapes=list(scratch),
        compiler_params=pltpu.CompilerParams(vmem_limit_bytes=24 * 1024 * 1024),
    )

    def run(*args):
        return kernel(
            *(
                pltpu.with_memory_space_constraint(arg, pltpu.HBM) if spec is HBM else arg
                for arg, spec in zip(args, specs, strict=True)
            )
        )

    return run


def iota(shape, dim):
    return lax.broadcasted_iota(I32, shape, dim)


def mm(a, b):
    return lax.dot_general(a, b, (((1,), (0,)), ((), ())), preferred_element_type=F32)


def mm_t(a, b):
    return lax.dot_general(a, b, (((1,), (1,)), ((), ())), preferred_element_type=F32)


def mm_exact(a, b, dims):
    return lax.dot_general(
        a, b, (dims, ((), ())), precision=lax.Precision.HIGHEST, preferred_element_type=F32
    )


def halves(value):
    high = value.astype(BF16)
    return high, (value - high.astype(F32)).astype(BF16)


def thirds(value):
    first = value.astype(BF16).astype(F32)
    second = (value - first).astype(BF16).astype(F32)
    return first, second, (value - first - second).astype(BF16).astype(F32)


def one_hot(mask):
    return mask.astype(F32).astype(BF16)


def small(rows):
    return rows.astype(F32).astype(BF16)


def columns(rows):
    width = rows.shape[1]
    same = one_hot(iota((width, width), 0) == iota((width, width), 1))
    return mm_t(same, small(rows)).astype(I32)


def to_all(value, axis, index_groups=None):
    return lax.all_to_all(
        value, axis, split_axis=0, concat_axis=0, tiled=True, axis_index_groups=index_groups
    )


def group_shift(value, step):
    return lax.ppermute(value, "group", [(g, (g + step) % GROUPS) for g in range(GROUPS)])


def started(ends, sems):
    copies = [pltpu.make_async_copy(*end, sems.at[k]) for k, end in enumerate(ends)]
    for copy in copies:
        copy.start()
    return copies


def pack_body(direction_hbm, bases_hbm, out_ref, direction_ref, bases_ref, sems):
    for copy in started(((direction_hbm, direction_ref), (bases_hbm, bases_ref)), sems):
        copy.wait()
    xb = direction_ref[...].astype(BF16)
    rank_rows = bases_ref[...]
    low = mm_t(xb, rank_rows[:, :128])
    high = mm_t(xb, rank_rows[:, 128:])
    row = iota((8, 128), 0)
    twice = (iota((8, 128), 1) >> 5) * 2
    kept = jnp.where(row == twice, low, 0.0) + jnp.where(row == twice + 1, high, 0.0)
    coeffs = jnp.sum(kept, axis=0, keepdims=True)
    packed = jnp.concatenate([xb, jnp.where(row == 0, coeffs, 0.0).astype(BF16)], axis=0)
    for d in range(DEVS):
        out_ref[d] = packed


def prep_body(x_ref, tiles_hbm, blocks_hbm, pairs_hbm, mask_hbm, near_pairs_hbm, near_mask_hbm,
              krylov_hbm, bases_hbm, out_ref, tiles_ref, gather_ref, scatter_ref, row_ref, here_ref,
              pairs_ref, mask_ref, near_pairs_ref, near_mask_ref, krylov_ref, sems, tile_sem):
    fetched = pltpu.make_async_copy(tiles_hbm, tiles_ref, tile_sem)
    slots = blocks_hbm.shape[0]
    ends = (
        (blocks_hbm, out_ref.at[0:slots]),
        (pairs_hbm, pairs_ref),
        (mask_hbm, mask_ref),
        (near_pairs_hbm, near_pairs_ref),
        (near_mask_hbm, near_mask_ref),
        (krylov_hbm, krylov_ref),
        (bases_hbm, row_ref.at[0:128]),
    )
    copies = started(ends, sems)
    fetched.start()
    for copy in copies:
        copy.wait()
    i_row, j_row = pairs_ref[0:1, :], pairs_ref[1:2, :]
    step = ((j_row >> 7) - (i_row >> 7)) & (GROUPS - 1)
    which = jnp.where(step == 0, 0, jnp.where(step == 1, 2, 1))
    live = mask_ref[...]
    both = jnp.where(i_row == j_row, 0, live)
    row = iota((16, slots), 0)
    digits = jnp.zeros((16, slots), I32)
    for k, value in enumerate((i_row & 127, j_row & 127, which, live, both)):
        digits = jnp.where(row == k, value, digits)
    out_ref[slots : slots + 16, :] = jnp.zeros((16, out_ref.shape[1]), BF16)
    out_ref[slots : slots + 16, 0:slots] = small(digits)
    near = near_pairs_ref[...]
    live = near_mask_ref[...]
    near_slots = near.shape[1]
    row = iota((8, near_slots), 0)
    info = jnp.where(row == 0, near[0:1, :], jnp.where(row == 1, near[1:2, :], live))
    m = iota((64, near_slots), 0)
    pick = one_hot((m & 15) == iota((64, near_slots), 1))
    info_cols = mm_t(pick, small(info)).astype(I32)
    i_col, j_col = info_cols[:, 0:1], info_cols[:, 1:2]
    m = iota((64, 1), 0) >> 4
    c = jnp.where(m < 2, j_col, i_col)
    place = (c >> 2) * 16 + (c & 3) * 2 + (m & 1)
    gather_ref[...] = one_hot(iota((64, DEVS * 16), 1) == place)
    lane = iota((near_slots, 128), 1)
    pick = one_hot((lane & 15) == iota((near_slots, 128), 0))
    info_lanes = mm(small(info), pick).astype(I32)
    i_lane, j_lane, live_lane = (info_lanes[k : k + 1, :] for k in range(3))
    kind = (iota((1, 128), 1) >> 4) & 3
    used = (live_lane == 1) & ((kind < 2) | (i_lane != j_lane))
    target = jnp.where(kind < 2, i_lane, j_lane) * 2 + (kind & 1)
    target = jnp.where(used, target, -1)
    scatter_ref[...] = one_hot(iota((DEVS * 8, 128), 0) == target)
    rows = krylov_ref[...]
    gram = mm_exact(rows, rows, ((1,), (1,)))
    lane, row = iota((8, 128), 1) - 8, iota((8, 128), 0)
    inside = (lane >= 0) & (lane < 64)
    wide = mm_exact(gram, jnp.where(inside & ((lane & 7) == row), 1.0, 0.0), ((1,), (0,)))
    gram = jnp.sum(jnp.where(inside & ((lane >> 3) == row), wide, 0.0), axis=0, keepdims=True)
    for t, part in enumerate(thirds(rows)):
        for b in range(2):
            left, right = part[:, b * 512 : b * 512 + 256], part[:, b * 512 + 256 : b * 512 + 512]
            at = 128 + t * 32 + b * 16
            row_ref[at : at + 16, :] = jnp.concatenate([left, right], axis=0).astype(BF16)
    row = iota((16, 128), 0)
    tail = jnp.zeros((16, 128), F32)
    for t, part in enumerate(thirds(gram)):
        tail = jnp.where(row == t, part, tail)
    row_ref[224:240, 0:128] = tail.astype(BF16)
    row_ref[224:240, 128:256] = jnp.zeros((16, 128), BF16)
    here_ref[...] = jnp.where(iota((NX, 8, 128), 0) == x_ref[0], 1.0, 0.0)
    fetched.wait()


def coeffs_body(gathered_ref, out_ref):
    rows = iota((DEVS, DEVS * 16), 0) * 16 + 8
    pick = one_hot(iota((DEVS, DEVS * 16), 1) == rows)
    out_ref[...] = mm(pick, gathered_ref[...]).astype(BF16)


def near_body(gathered_ref, gather_ref, scatter_ref, tiles_ref, own_ref, before_ref, after_ref,
              out_ref, *far_refs):
    far_prep(own_ref, before_ref, after_ref, *far_refs)
    taken = mm(gather_ref[...], gathered_ref[...])
    right = jnp.concatenate([taken[0:16], taken[16:32]], axis=1).astype(BF16)
    left = jnp.concatenate([taken[32:48], taken[48:64]], axis=1).astype(BF16)
    slot = iota((16, 256), 0)
    forward = jnp.zeros((16, 256), F32)
    backward = jnp.zeros((16, 256), F32)
    for s in range(tiles_ref.shape[0]):
        tile = tiles_ref[s]
        forward = jnp.where(slot == s, mm_t(right, tile), forward)
        backward = jnp.where(slot == s, mm(left, tile), backward)
    values = jnp.concatenate(
        [forward[:, :128], forward[:, 128:], backward[:, :128], backward[:, 128:]], axis=0
    )
    out_ref[...] = mm(scatter_ref[...], jnp.concatenate(halves(values), axis=0))


def far_prep(own_ref, before_ref, after_ref, pick_ref, lanes_ref, keep_ref, owner_ref, take_ref,
             give_ref):
    slots = own_ref.shape[0] - 16
    rows = [
        ref[slots : slots + 16, 0:slots].astype(F32).astype(I32)
        for ref in (own_ref, before_ref, after_ref)
    ]
    cols = jnp.concatenate([columns(r) for r in [rows[0]] + rows], axis=0)
    i_low, j_low, which, live, both = (cols[:, k : k + 1] for k in range(5))
    slot = iota((4 * slots, 1), 0) // slots
    ahead = slot == 0
    low = jnp.where(ahead, j_low, i_low)
    source = jnp.where(ahead, which, slot - 1)
    pick_ref[...] = one_hot(iota((4 * slots, 3 * DEVS), 1) == source * DEVS + (low >> 2))
    block = iota((4 * slots, 128), 1) >> 5
    lanes_ref[...] = jnp.where(block == (low & 3), 1.0, 0.0)
    wanted = jnp.where(slot == 2, 2, jnp.where(slot == 3, 1, 0))
    used = jnp.where(ahead, live, jnp.where(which == wanted, both, 0))
    target = jnp.where(ahead, i_low, j_low)
    keep_ref[...] = jnp.where((used == 1) & (block == (target & 3)), 1.0, 0.0)
    owner = iota((DEVS, slots), 0)
    for k, row in enumerate([rows[0][0:1, :]] + [r[1:2, :] for r in rows]):
        owner_ref[k] = one_hot(owner == (row >> 2))
    for k in range(8):
        sub, lane = iota((128, 128), 0), iota((128, 128), 1)
        take_ref[k] = one_hot((sub & 31) == 4 * k + (lane >> 5))
        give_ref[k] = one_hot((lane & 31) == 4 * k + (sub >> 5))


def far_body(near_ref, own_ref, before_ref, after_ref, own_coef_ref, before_coef_ref,
             after_coef_ref, pick_ref, lanes_ref, keep_ref, owner_ref, take_ref, give_ref, row_ref, out_ref,
             rows_ref):
    bundles = (own_ref, before_ref, after_ref)
    slots = own_ref.shape[0] - 16
    coeffs = jnp.concatenate([own_coef_ref[...], before_coef_ref[...], after_coef_ref[...]], axis=0)
    taken = (mm(pick_ref[...], coeffs) * lanes_ref[...]).astype(BF16)
    right, left = taken[0:slots], taken[slots:]
    sub, lane = iota((128, 128), 0), iota((128, 128), 1)
    tiled = mm(right, one_hot((sub & 31) == (lane & 31)))
    forward = jnp.zeros((slots, 128), F32)
    backward = jnp.zeros(left.shape, F32)
    for k in range(8):
        parts = [b[0:slots, k * 128 : k * 128 + 128] for b in bundles]
        part = jnp.concatenate(parts, axis=0).astype(F32)
        backward = backward + part * mm(left, take_ref[k])
        for piece in halves(part[0:slots] * tiled):
            forward = forward + mm(piece, give_ref[k])
    backward = backward + pltpu.roll(backward, 64, 1)
    backward = backward + pltpu.roll(backward, 32, 1)
    sums = jnp.concatenate([forward, backward], axis=0) * keep_ref[...]
    total = jnp.zeros((DEVS, 128), F32)
    for k in range(4):
        for part in halves(sums[k * slots : k * slots + slots]):
            total = total + mm(owner_ref[k], part)
    row = iota((8, 128), 0)
    for d in range(DEVS):
        near = near_ref[d * 8 : d * 8 + 8, :]
        low = jnp.where(row == 7, total[d : d + 1, :], near - near.astype(BF16).astype(F32))
        at = d % NX * 16
        out_ref[d // NX, at : at + 16, :] = jnp.concatenate([near, low], axis=0).astype(BF16)
    for x in range(NX):
        rows_ref[x] = row_ref[...]


def middle_body(pieces_ref, out_ref):
    total = jnp.sum(pieces_ref[...].astype(F32), axis=0)
    row = iota((8, 128), 0)
    nears = []
    fars = jnp.zeros((8, 128), F32)
    for x in range(NX):
        high, low = total[x * 16 : x * 16 + 8, :], total[x * 16 + 8 : x * 16 + 16, :]
        nears.append(high + jnp.where(row == 7, 0.0, low))
        fars = jnp.where(row == x, low[7:8, :], fars)
    both = jnp.concatenate(nears + [fars], axis=0)
    for x in range(NX):
        out_ref[x] = both


def product_body(pieces_ref, rows_ref, here_ref, product_ref, copies_ref):
    total = jnp.sum(pieces_ref[...], axis=0)
    row, lane = iota((8, 128), 0), iota((8, 128), 1)
    acc, square, own = (jnp.zeros((8, 128), F32) for _ in range(3))
    gram = jnp.zeros((1, 128), F32)
    for m in range(NX):
        coef = total[32 + m : 33 + m, :].astype(BF16).astype(F32)
        spread = jnp.where((lane >> 5) == (row >> 1), coef, 0.0).astype(BF16)
        low = mm(spread, rows_ref[m, 0:128, 0:128])
        high = mm(spread, rows_ref[m, 0:128, 128:256])
        product = total[m * 8 : m * 8 + 8, :] + jnp.where((row & 1) == 0, low, high)
        own = jnp.where(here_ref[m] > 0.5, product, own)
        square = square + product * product
        for b in range(2):
            parts = [
                rows_ref[m, 128 + t * 32 + b * 16 : 144 + t * 32 + b * 16, :].astype(F32)
                for t in range(3)
            ]
            krylov = (parts[0] + parts[1]) + parts[2]
            for r in range(4):
                at = (r >> 1) * 8, (r & 1) * 128
                part = krylov[at[0] : at[0] + 8, at[1] : at[1] + 128]
                acc = acc + part * product[b * 4 + r : b * 4 + r + 1, :]
        parts = rows_ref[m, 224:240, 0:128].astype(F32)
        gram = gram + ((parts[0:1, :] + parts[1:2, :]) + parts[2:3, :])
    product_ref[...] = own
    proj = jnp.sum(acc, axis=1, keepdims=True)
    square = jnp.sum(square, axis=1, keepdims=True)
    values = jnp.where(lane == row, proj, 0.0) + jnp.where(lane == 72, square, 0.0)
    payload = jnp.sum(values, axis=0, keepdims=True) + gram
    for d in range(copies_ref.shape[0]):
        copies_ref[d] = payload


def spread_body(pieces_ref, out_ref):
    total = jnp.sum(pieces_ref[...], axis=0)
    for d in range(out_ref.shape[0]):
        out_ref[d] = total


def last_body(count, pieces_ref, product_ref, krylov_ref, next_ref, proj_ref):
    total = jnp.sum(pieces_ref[...], axis=0)
    row, lane = iota((8, 128), 0), iota((8, 128), 1)
    proj = jnp.sum(jnp.where(lane == row, total, 0.0), axis=1, keepdims=True)
    inside = (lane >= 8) & (lane < 72)
    first = jnp.sum(jnp.where(inside & (((lane - 8) >> 3) == row), proj, 0.0), axis=0, keepdims=True)
    second = jnp.sum(jnp.where(inside & ((lane & 7) == row), proj, 0.0), axis=0, keepdims=True)
    lane = iota((1, 128), 1)
    terms = total * jnp.where(lane < 8, -2.0 * total, first * second)
    terms = jnp.where(lane == 72, total, jnp.where(lane < 72, terms, 0.0))
    length_sq = jnp.sum(terms, axis=1, keepdims=True)
    scale = 1.0 / jnp.sqrt(jnp.maximum(length_sq, 0.0) / count)
    for r in range(8):
        taken = jnp.sum(proj * krylov_ref[:, r * 128 : r * 128 + 128], axis=0, keepdims=True)
        next_ref[r : r + 1, :] = (product_ref[r : r + 1, :] - taken) * scale
    proj_ref[...] = total[:, 0:8]


def local(
    direction, krylov, bases, near_tiles, near_pairs, near_mask, far_blocks, far_pairs, far_mask
):
    panels = direction.shape[0]
    rank_rows = bases.reshape(-1, bases.shape[2])
    slots, far_slots = near_tiles.shape[0], far_blocks.shape[0]

    copies = call(
        pack_body,
        sds((DEVS, 16, 128), BF16),
        [HBM, HBM],
        [pltpu.VMEM((8, 128), F32), pltpu.VMEM(rank_rows.shape, BF16), pltpu.SemaphoreType.DMA((2,))],
    )(direction.reshape(8, 128), rank_rows)
    gathered = to_all(copies, "dev").reshape(-1, 128)
    x = (lax.axis_index("dev") & (NX - 1)).astype(I32)[None]
    bundle, tiles, gather, scatter, row, here = call(
        prep_body,
        [
            sds((far_slots + 16, far_blocks.shape[1]), BF16),
            pltpu.VMEM(near_tiles.shape, BF16),
            sds((64, DEVS * 16), BF16),
            sds((DEVS * 8, 128), BF16),
            sds((240, 256), BF16),
            pltpu.VMEM((NX, 8, 128), F32),
        ],
        [SMEM] + [HBM] * 8,
        [
            pltpu.VMEM((2, far_slots), I32),
            pltpu.VMEM((1, far_slots), I32),
            pltpu.VMEM((2, slots), I32),
            pltpu.VMEM((1, slots), I32),
            pltpu.VMEM(krylov.shape, F32),
            pltpu.SemaphoreType.DMA((7,)),
            pltpu.SemaphoreType.DMA,
        ],
    )(
        x, near_tiles, far_blocks, far_pairs.T, far_mask[None], near_pairs.T, near_mask[None], krylov,
        rank_rows,
    )
    before, after = group_shift(bundle, 1), group_shift(bundle, -1)

    coeffs = call(coeffs_body, sds((DEVS, 128), BF16), [VMEM])(gathered)
    coeffs_before, coeffs_after = group_shift(coeffs, 1), group_shift(coeffs, -1)
    near, *far_prepared = call(
        near_body,
        [
            sds((DEVS * 8, 128), F32),
            pltpu.VMEM((4 * far_slots, 3 * DEVS), BF16),
            pltpu.VMEM((4 * far_slots, 128), F32),
            pltpu.VMEM((4 * far_slots, 128), F32),
            pltpu.VMEM((4, DEVS, far_slots), BF16),
            pltpu.VMEM((8, 128, 128), BF16),
            pltpu.VMEM((8, 128, 128), BF16),
        ],
        [VMEM] * 7,
    )(gathered, gather, scatter, tiles, bundle, before, after)
    parts, rows = call(
        far_body,
        [sds((NZ, NX * 16, 128), BF16), sds((NX, 240, 256), BF16)],
        [VMEM] * 14,
    )(near, bundle, before, after, coeffs, coeffs_before, coeffs_after, *far_prepared, row)
    along_x = [[z * NX + x for x in range(NX)] for z in range(NZ)]
    along_z = [[z * NX + x for z in range(NZ)] for x in range(NX)]
    parts = to_all(parts, "dev", along_z)
    rows = to_all(rows, "dev", along_x)
    parts = call(middle_body, sds((NX, 40, 128), F32), [VMEM])(parts)
    product, copies = call(
        product_body, [sds((8, 128), F32), sds((GROUPS, 1, 128), F32)], [VMEM] * 3
    )(to_all(parts, "dev", along_x), rows, here)
    copies = call(spread_body, sds((NZ, 1, 128), F32), [VMEM])(to_all(copies, "group"))
    pieces = to_all(copies, "dev", along_z)
    count = float(panels * DEVS * GROUPS)

    def finish(*refs):
        last_body(count, *refs)

    next_vector, projections = call(finish, [sds((8, 128), F32), sds((1, 8), F32)], [VMEM] * 3)(
        pieces, product, krylov
    )
    return (next_vector.reshape(-1), projections.reshape(-1))


def solution(mesh):
    in_specs = (
        P(("group", "dev")),
        P(None, ("group", "dev")),
        P(("group", "dev"), None, None),
        P(("group", "dev"), None, None),
        P(("group", "dev"), None),
        P(("group", "dev")),
        P(("group", "dev"), None),
        P(("group", "dev"), None),
        P(("group", "dev")),
    )
    out_specs = (P(("group", "dev")), P())
    return jax.shard_map(local, mesh=mesh, in_specs=in_specs, out_specs=out_specs, check_vma=False)
```

```python
import jax
import jax.numpy as jnp
from jax import lax
from jax.experimental import pallas as pl
from jax.experimental.pallas import tpu as pltpu
from jax.sharding import PartitionSpec as P

F32 = jnp.float32
BF16 = jnp.bfloat16
I32 = jnp.int32
NX, NZ, NY = 4, 8, 8
DEVS, GROUPS = NZ * NX, 2 * NY
VMEM = pl.BlockSpec(memory_space=pltpu.VMEM)
HBM = pl.BlockSpec(memory_space=pltpu.HBM)
sds = jax.ShapeDtypeStruct


def call(body, outs, specs, scratch=()):
    kernel = pl.pallas_call(
        body,
        out_shape=outs,
        in_specs=specs,
        out_specs=jax.tree.map(lambda _: VMEM, outs),
        scratch_shapes=list(scratch),
        compiler_params=pltpu.CompilerParams(vmem_limit_bytes=24 * 1024 * 1024),
    )

    def run(*args):
        return kernel(
            *(
                pltpu.with_memory_space_constraint(arg, pltpu.HBM) if spec is HBM else arg
                for arg, spec in zip(args, specs, strict=True)
            )
        )

    return run


def iota(shape, dim):
    return lax.broadcasted_iota(I32, shape, dim)


def mm(a, b):
    return lax.dot_general(a, b, (((1,), (0,)), ((), ())), preferred_element_type=F32)


def mm_t(a, b):
    return lax.dot_general(a, b, (((1,), (1,)), ((), ())), preferred_element_type=F32)


def mm_exact(a, b, dims):
    return lax.dot_general(
        a, b, (dims, ((), ())), precision=lax.Precision.HIGHEST, preferred_element_type=F32
    )


def halves(value):
    high = value.astype(BF16)
    return high, (value - high.astype(F32)).astype(BF16)


def one_hot(mask):
    return mask.astype(F32).astype(BF16)


def small(rows):
    return rows.astype(F32).astype(BF16)


def columns(rows):
    width = rows.shape[1]
    same = one_hot(iota((width, width), 0) == iota((width, width), 1))
    return mm_t(same, small(rows)).astype(I32)


def snake(dev):
    return dev ^ (((dev >> 2) & 1) * (NX - 1))


def to_all(value, axis):
    order = [[snake(k) for k in range(DEVS)]] if axis == "dev" else None
    return lax.all_to_all(
        value, axis, split_axis=0, concat_axis=0, tiled=True, axis_index_groups=order
    )


def group_shift(value, step):
    return lax.ppermute(value, "group", [(g, (g + step) % GROUPS) for g in range(GROUPS)])


def started(ends, sems):
    copies = [pltpu.make_async_copy(*end, sems.at[k]) for k, end in enumerate(ends)]
    for copy in copies:
        copy.start()
    return copies


def pack_body(direction_hbm, bases_hbm, out_ref, direction_ref, bases_ref, sems):
    for copy in started(((direction_hbm, direction_ref), (bases_hbm, bases_ref)), sems):
        copy.wait()
    xb = direction_ref[...].astype(BF16)
    rank_rows = bases_ref[...]
    low = mm_t(xb, rank_rows[:, :128])
    high = mm_t(xb, rank_rows[:, 128:])
    row = iota((8, 128), 0)
    twice = (iota((8, 128), 1) >> 5) * 2
    kept = jnp.where(row == twice, low, 0.0) + jnp.where(row == twice + 1, high, 0.0)
    coeffs = jnp.sum(kept, axis=0, keepdims=True)
    packed = jnp.concatenate([xb, jnp.where(row == 0, coeffs, 0.0).astype(BF16)], axis=0)
    for d in range(DEVS):
        out_ref[d] = packed


def prep_body(tiles_hbm, blocks_hbm, pairs_hbm, mask_hbm, near_pairs_hbm, near_mask_hbm, krylov_hbm,
              out_ref, tiles_ref, gather_ref, scatter_ref, gram_ref,
              pairs_ref, mask_ref, near_pairs_ref, near_mask_ref, krylov_ref, sems, tile_sem):
    fetched = pltpu.make_async_copy(tiles_hbm, tiles_ref, tile_sem)
    slots = blocks_hbm.shape[0]
    ends = (
        (blocks_hbm, out_ref.at[0:slots]),
        (pairs_hbm, pairs_ref),
        (mask_hbm, mask_ref),
        (near_pairs_hbm, near_pairs_ref),
        (near_mask_hbm, near_mask_ref),
        (krylov_hbm, krylov_ref),
    )
    copies = started(ends, sems)
    fetched.start()
    for copy in copies:
        copy.wait()
    i_row, j_row = pairs_ref[0:1, :], pairs_ref[1:2, :]
    step = ((j_row >> 7) - (i_row >> 7)) & (GROUPS - 1)
    which = jnp.where(step == 0, 0, jnp.where(step == 1, 2, 1))
    live = mask_ref[...]
    both = jnp.where(i_row == j_row, 0, live)
    row = iota((16, slots), 0)
    digits = jnp.zeros((16, slots), I32)
    for k, value in enumerate((i_row & 127, j_row & 127, which, live, both)):
        digits = jnp.where(row == k, value, digits)
    out_ref[slots : slots + 16, :] = jnp.zeros((16, out_ref.shape[1]), BF16)
    out_ref[slots : slots + 16, 0:slots] = small(digits)
    near = near_pairs_ref[...]
    live = near_mask_ref[...]
    near_slots = near.shape[1]
    row = iota((8, near_slots), 0)
    info = jnp.where(row == 0, near[0:1, :], jnp.where(row == 1, near[1:2, :], live))
    m = iota((64, near_slots), 0)
    pick = one_hot((m & 15) == iota((64, near_slots), 1))
    info_cols = mm_t(pick, small(info)).astype(I32)
    i_col, j_col = info_cols[:, 0:1], info_cols[:, 1:2]
    m = iota((64, 1), 0) >> 4
    c = jnp.where(m < 2, j_col, i_col)
    place = snake(c >> 2) * 16 + (c & 3) * 2 + (m & 1)
    gather_ref[...] = one_hot(iota((64, DEVS * 16), 1) == place)
    lane = iota((near_slots, 128), 1)
    pick = one_hot((lane & 15) == iota((near_slots, 128), 0))
    info_lanes = mm(small(info), pick).astype(I32)
    i_lane, j_lane, live_lane = (info_lanes[k : k + 1, :] for k in range(3))
    kind = (iota((1, 128), 1) >> 4) & 3
    used = (live_lane == 1) & ((kind < 2) | (i_lane != j_lane))
    target = jnp.where(kind < 2, i_lane, j_lane) * 2 + (kind & 1)
    target = jnp.where(used, target, -1)
    scatter_ref[...] = one_hot(iota((DEVS * 8, 128), 0) == target)
    rows = krylov_ref[...]
    gram = mm_exact(rows, rows, ((1,), (1,)))
    lane, row = iota((8, 128), 1) - 8, iota((8, 128), 0)
    inside = (lane >= 0) & (lane < 64)
    wide = mm_exact(gram, jnp.where(inside & ((lane & 7) == row), 1.0, 0.0), ((1,), (0,)))
    gram_ref[...] = jnp.sum(
        jnp.where(inside & ((lane >> 3) == row), wide, 0.0), axis=0, keepdims=True
    )
    fetched.wait()


def coeffs_body(gathered_ref, out_ref):
    rows = snake(iota((DEVS, DEVS * 16), 0)) * 16 + 8
    pick = one_hot(iota((DEVS, DEVS * 16), 1) == rows)
    out_ref[...] = mm(pick, gathered_ref[...]).astype(BF16)


def near_body(gathered_ref, gather_ref, scatter_ref, tiles_ref, own_ref, before_ref, after_ref,
              out_ref, *far_refs):
    far_prep(own_ref, before_ref, after_ref, *far_refs)
    taken = mm(gather_ref[...], gathered_ref[...])
    right = jnp.concatenate([taken[0:16], taken[16:32]], axis=1).astype(BF16)
    left = jnp.concatenate([taken[32:48], taken[48:64]], axis=1).astype(BF16)
    slot = iota((16, 256), 0)
    forward = jnp.zeros((16, 256), F32)
    backward = jnp.zeros((16, 256), F32)
    for s in range(tiles_ref.shape[0]):
        tile = tiles_ref[s]
        forward = jnp.where(slot == s, mm_t(right, tile), forward)
        backward = jnp.where(slot == s, mm(left, tile), backward)
    values = jnp.concatenate(
        [forward[:, :128], forward[:, 128:], backward[:, :128], backward[:, 128:]], axis=0
    )
    out_ref[...] = mm(scatter_ref[...], jnp.concatenate(halves(values), axis=0))


def far_prep(own_ref, before_ref, after_ref, pick_ref, lanes_ref, keep_ref, owner_ref, take_ref,
             give_ref):
    slots = own_ref.shape[0] - 16
    rows = [
        ref[slots : slots + 16, 0:slots].astype(F32).astype(I32)
        for ref in (own_ref, before_ref, after_ref)
    ]
    cols = jnp.concatenate([columns(r) for r in [rows[0]] + rows], axis=0)
    i_low, j_low, which, live, both = (cols[:, k : k + 1] for k in range(5))
    slot = iota((4 * slots, 1), 0) // slots
    ahead = slot == 0
    low = jnp.where(ahead, j_low, i_low)
    source = jnp.where(ahead, which, slot - 1)
    pick_ref[...] = one_hot(iota((4 * slots, 3 * DEVS), 1) == source * DEVS + (low >> 2))
    block = iota((4 * slots, 128), 1) >> 5
    lanes_ref[...] = jnp.where(block == (low & 3), 1.0, 0.0)
    wanted = jnp.where(slot == 2, 2, jnp.where(slot == 3, 1, 0))
    used = jnp.where(ahead, live, jnp.where(which == wanted, both, 0))
    target = jnp.where(ahead, i_low, j_low)
    keep_ref[...] = jnp.where((used == 1) & (block == (target & 3)), 1.0, 0.0)
    owner = iota((DEVS, slots), 0)
    for k, row in enumerate([rows[0][0:1, :]] + [r[1:2, :] for r in rows]):
        owner_ref[k] = one_hot(owner == (row >> 2))
    for k in range(8):
        sub, lane = iota((128, 128), 0), iota((128, 128), 1)
        take_ref[k] = one_hot((sub & 31) == 4 * k + (lane >> 5))
        give_ref[k] = one_hot((lane & 31) == 4 * k + (sub >> 5))


def far_body(near_ref, own_ref, before_ref, after_ref, own_coef_ref, before_coef_ref,
             after_coef_ref, pick_ref, lanes_ref, keep_ref, owner_ref, take_ref, give_ref, out_ref):
    bundles = (own_ref, before_ref, after_ref)
    slots = own_ref.shape[0] - 16
    coeffs = jnp.concatenate([own_coef_ref[...], before_coef_ref[...], after_coef_ref[...]], axis=0)
    taken = (mm(pick_ref[...], coeffs) * lanes_ref[...]).astype(BF16)
    right, left = taken[0:slots], taken[slots:]
    sub, lane = iota((128, 128), 0), iota((128, 128), 1)
    tiled = mm(right, one_hot((sub & 31) == (lane & 31)))
    forward = jnp.zeros((slots, 128), F32)
    backward = jnp.zeros(left.shape, F32)
    for k in range(8):
        parts = [b[0:slots, k * 128 : k * 128 + 128] for b in bundles]
        part = jnp.concatenate(parts, axis=0).astype(F32)
        backward = backward + part * mm(left, take_ref[k])
        for piece in halves(part[0:slots] * tiled):
            forward = forward + mm(piece, give_ref[k])
    backward = backward + pltpu.roll(backward, 64, 1)
    backward = backward + pltpu.roll(backward, 32, 1)
    sums = jnp.concatenate([forward, backward], axis=0) * keep_ref[...]
    total = jnp.zeros((DEVS, 128), F32)
    for k in range(4):
        for part in halves(sums[k * slots : k * slots + slots]):
            total = total + mm(owner_ref[k], part)
    row = iota((8, 128), 0)
    for d in range(DEVS):
        near = near_ref[d * 8 : d * 8 + 8, :]
        low = jnp.where(row == 7, total[d : d + 1, :], near - near.astype(BF16).astype(F32))
        out_ref[snake(d)] = jnp.concatenate([near, low], axis=0).astype(BF16)


def product_body(pieces_ref, bases_ref, krylov_ref, gram_ref, product_ref, copies_ref):
    total = jnp.sum(pieces_ref[...].astype(F32), axis=0)
    row, lane = iota((8, 128), 0), iota((8, 128), 1)
    near = total[0:8, :] + jnp.where(row == 7, 0.0, total[8:16, :])
    coef = total[15:16, :].astype(BF16).astype(F32)
    spread = jnp.where((lane >> 5) == (row >> 1), coef, 0.0).astype(BF16)
    low = mm(spread, bases_ref[:, :128])
    high = mm(spread, bases_ref[:, 128:])
    product = near + jnp.where((row & 1) == 0, low, high)
    product_ref[...] = product
    acc = jnp.zeros((8, 128), F32)
    for r in range(8):
        acc = acc + krylov_ref[:, r * 128 : r * 128 + 128] * product[r : r + 1, :]
    proj = jnp.sum(acc, axis=1, keepdims=True)
    square = jnp.sum(product * product, axis=1, keepdims=True)
    values = jnp.where(lane == row, proj, 0.0) + jnp.where(lane == 72, square, 0.0)
    payload = jnp.sum(values, axis=0, keepdims=True) + gram_ref[...]
    for d in range(copies_ref.shape[0]):
        copies_ref[d] = payload


def spread_body(pieces_ref, out_ref):
    total = jnp.sum(pieces_ref[...], axis=0)
    for d in range(out_ref.shape[0]):
        out_ref[d] = total


def last_body(count, pieces_ref, product_ref, krylov_ref, next_ref, proj_ref):
    total = jnp.sum(pieces_ref[...], axis=0)
    row, lane = iota((8, 128), 0), iota((8, 128), 1)
    proj = jnp.sum(jnp.where(lane == row, total, 0.0), axis=1, keepdims=True)
    inside = (lane >= 8) & (lane < 72)
    first = jnp.sum(jnp.where(inside & (((lane - 8) >> 3) == row), proj, 0.0), axis=0, keepdims=True)
    second = jnp.sum(jnp.where(inside & ((lane & 7) == row), proj, 0.0), axis=0, keepdims=True)
    lane = iota((1, 128), 1)
    terms = total * jnp.where(lane < 8, -2.0 * total, first * second)
    terms = jnp.where(lane == 72, total, jnp.where(lane < 72, terms, 0.0))
    length_sq = jnp.sum(terms, axis=1, keepdims=True)
    scale = 1.0 / jnp.sqrt(jnp.maximum(length_sq, 0.0) / count)
    for r in range(8):
        taken = jnp.sum(proj * krylov_ref[:, r * 128 : r * 128 + 128], axis=0, keepdims=True)
        next_ref[r : r + 1, :] = (product_ref[r : r + 1, :] - taken) * scale
    proj_ref[...] = total[:, 0:8]


def local(
    direction, krylov, bases, near_tiles, near_pairs, near_mask, far_blocks, far_pairs, far_mask
):
    panels = direction.shape[0]
    rank_rows = bases.reshape(-1, bases.shape[2])
    slots, far_slots = near_tiles.shape[0], far_blocks.shape[0]

    copies = call(
        pack_body,
        sds((DEVS, 16, 128), BF16),
        [HBM, HBM],
        [pltpu.VMEM((8, 128), F32), pltpu.VMEM(rank_rows.shape, BF16), pltpu.SemaphoreType.DMA((2,))],
    )(direction.reshape(8, 128), rank_rows)
    gathered = to_all(copies, "dev").reshape(-1, 128)
    bundle, tiles, gather, scatter, gram = call(
        prep_body,
        [
            sds((far_slots + 16, far_blocks.shape[1]), BF16),
            pltpu.VMEM(near_tiles.shape, BF16),
            sds((64, DEVS * 16), BF16),
            sds((DEVS * 8, 128), BF16),
            sds((1, 128), F32),
        ],
        [HBM] * 7,
        [
            pltpu.VMEM((2, far_slots), I32),
            pltpu.VMEM((1, far_slots), I32),
            pltpu.VMEM((2, slots), I32),
            pltpu.VMEM((1, slots), I32),
            pltpu.VMEM(krylov.shape, F32),
            pltpu.SemaphoreType.DMA((6,)),
            pltpu.SemaphoreType.DMA,
        ],
    )(near_tiles, far_blocks, far_pairs.T, far_mask[None], near_pairs.T, near_mask[None], krylov)
    before, after = group_shift(bundle, 1), group_shift(bundle, -1)

    coeffs = call(coeffs_body, sds((DEVS, 128), BF16), [VMEM])(gathered)
    coeffs_before, coeffs_after = group_shift(coeffs, 1), group_shift(coeffs, -1)
    near, *far_prepared = call(
        near_body,
        [
            sds((DEVS * 8, 128), F32),
            pltpu.VMEM((4 * far_slots, 3 * DEVS), BF16),
            pltpu.VMEM((4 * far_slots, 128), F32),
            pltpu.VMEM((4 * far_slots, 128), F32),
            pltpu.VMEM((4, DEVS, far_slots), BF16),
            pltpu.VMEM((8, 128, 128), BF16),
            pltpu.VMEM((8, 128, 128), BF16),
        ],
        [VMEM] * 7,
    )(gathered, gather, scatter, tiles, bundle, before, after)
    parts = call(far_body, sds((DEVS, 16, 128), BF16), [VMEM] * 13)(
        near, bundle, before, after, coeffs, coeffs_before, coeffs_after, *far_prepared
    )
    product, copies = call(
        product_body, [sds((8, 128), F32), sds((GROUPS, 1, 128), F32)], [VMEM] * 4
    )(to_all(parts, "dev"), rank_rows, krylov, gram)
    copies = call(spread_body, sds((DEVS, 1, 128), F32), [VMEM])(to_all(copies, "group"))
    pieces = to_all(copies, "dev")
    count = float(panels * DEVS * GROUPS)

    def finish(*refs):
        last_body(count, *refs)

    next_vector, projections = call(finish, [sds((8, 128), F32), sds((1, 8), F32)], [VMEM] * 3)(
        pieces, product, krylov
    )
    return (next_vector.reshape(-1), projections.reshape(-1))


def solution(mesh):
    in_specs = (
        P(("group", "dev")),
        P(None, ("group", "dev")),
        P(("group", "dev"), None, None),
        P(("group", "dev"), None, None),
        P(("group", "dev"), None),
        P(("group", "dev")),
        P(("group", "dev"), None),
        P(("group", "dev"), None),
        P(("group", "dev")),
    )
    out_specs = (P(("group", "dev")), P())
    return jax.shard_map(local, mesh=mesh, in_specs=in_specs, out_specs=out_specs, check_vma=False)
```

```python
import jax
import jax.numpy as jnp
from jax import lax
from jax.experimental import pallas as pl
from jax.experimental.pallas import tpu as pltpu
from jax.sharding import PartitionSpec as P

F32 = jnp.float32
BF16 = jnp.bfloat16
I32 = jnp.int32
NX, NZ, NY = 4, 8, 8
DEVS, GROUPS = NZ * NX, 2 * NY
VMEM = pl.BlockSpec(memory_space=pltpu.VMEM)
HBM = pl.BlockSpec(memory_space=pltpu.HBM)
sds = jax.ShapeDtypeStruct


def call(body, outs, specs, scratch=()):
    kernel = pl.pallas_call(
        body,
        out_shape=outs,
        in_specs=specs,
        out_specs=jax.tree.map(lambda _: VMEM, outs),
        scratch_shapes=list(scratch),
        compiler_params=pltpu.CompilerParams(vmem_limit_bytes=24 * 1024 * 1024),
    )

    def run(*args):
        return kernel(
            *(
                pltpu.with_memory_space_constraint(arg, pltpu.HBM) if spec is HBM else arg
                for arg, spec in zip(args, specs, strict=True)
            )
        )

    return run


def iota(shape, dim):
    return lax.broadcasted_iota(I32, shape, dim)


def mm(a, b):
    return lax.dot_general(a, b, (((1,), (0,)), ((), ())), preferred_element_type=F32)


def mm_t(a, b):
    return lax.dot_general(a, b, (((1,), (1,)), ((), ())), preferred_element_type=F32)


def mm_exact(a, b, dims):
    return lax.dot_general(
        a, b, (dims, ((), ())), precision=lax.Precision.HIGHEST, preferred_element_type=F32
    )


def halves(value):
    high = value.astype(BF16)
    return high, (value - high.astype(F32)).astype(BF16)


def one_hot(mask):
    return mask.astype(F32).astype(BF16)


def small(rows):
    return rows.astype(F32).astype(BF16)


def columns(rows):
    width = rows.shape[1]
    same = one_hot(iota((width, width), 0) == iota((width, width), 1))
    return mm_t(same, small(rows)).astype(I32)


def to_all(value, axis):
    return lax.all_to_all(value, axis, split_axis=0, concat_axis=0, tiled=True)


def group_shift(value, step):
    return lax.ppermute(value, "group", [(g, (g + step) % GROUPS) for g in range(GROUPS)])


def started(ends, sems):
    copies = [pltpu.make_async_copy(*end, sems.at[k]) for k, end in enumerate(ends)]
    for copy in copies:
        copy.start()
    return copies


def pack_body(direction_hbm, bases_hbm, out_ref, direction_ref, bases_ref, sems):
    for copy in started(((direction_hbm, direction_ref), (bases_hbm, bases_ref)), sems):
        copy.wait()
    xb = direction_ref[...].astype(BF16)
    rank_rows = bases_ref[...]
    low = mm_t(xb, rank_rows[:, :128])
    high = mm_t(xb, rank_rows[:, 128:])
    row = iota((8, 128), 0)
    twice = (iota((8, 128), 1) >> 5) * 2
    kept = jnp.where(row == twice, low, 0.0) + jnp.where(row == twice + 1, high, 0.0)
    coeffs = jnp.sum(kept, axis=0, keepdims=True)
    packed = jnp.concatenate([xb, jnp.where(row == 0, coeffs, 0.0).astype(BF16)], axis=0)
    for d in range(DEVS):
        out_ref[d] = packed


def prep_body(tiles_hbm, blocks_hbm, pairs_hbm, mask_hbm, near_pairs_hbm, near_mask_hbm, krylov_hbm,
              out_ref, tiles_ref, gather_ref, scatter_ref, gram_ref,
              pairs_ref, mask_ref, near_pairs_ref, near_mask_ref, krylov_ref, sems, tile_sem):
    fetched = pltpu.make_async_copy(tiles_hbm, tiles_ref, tile_sem)
    slots = blocks_hbm.shape[0]
    ends = (
        (blocks_hbm, out_ref.at[0:slots]),
        (pairs_hbm, pairs_ref),
        (mask_hbm, mask_ref),
        (near_pairs_hbm, near_pairs_ref),
        (near_mask_hbm, near_mask_ref),
        (krylov_hbm, krylov_ref),
    )
    copies = started(ends, sems)
    fetched.start()
    for copy in copies:
        copy.wait()
    i_row, j_row = pairs_ref[0:1, :], pairs_ref[1:2, :]
    step = ((j_row >> 7) - (i_row >> 7)) & (GROUPS - 1)
    which = jnp.where(step == 0, 0, jnp.where(step == 1, 2, 1))
    live = mask_ref[...]
    both = jnp.where(i_row == j_row, 0, live)
    row = iota((16, slots), 0)
    digits = jnp.zeros((16, slots), I32)
    for k, value in enumerate((i_row & 127, j_row & 127, which, live, both)):
        digits = jnp.where(row == k, value, digits)
    out_ref[slots : slots + 16, :] = jnp.zeros((16, out_ref.shape[1]), BF16)
    out_ref[slots : slots + 16, 0:slots] = small(digits)
    near = near_pairs_ref[...]
    live = near_mask_ref[...]
    near_slots = near.shape[1]
    row = iota((8, near_slots), 0)
    info = jnp.where(row == 0, near[0:1, :], jnp.where(row == 1, near[1:2, :], live))
    m = iota((64, near_slots), 0)
    pick = one_hot((m & 15) == iota((64, near_slots), 1))
    info_cols = mm_t(pick, small(info)).astype(I32)
    i_col, j_col = info_cols[:, 0:1], info_cols[:, 1:2]
    m = iota((64, 1), 0) >> 4
    c = jnp.where(m < 2, j_col, i_col)
    place = (c >> 2) * 16 + (c & 3) * 2 + (m & 1)
    gather_ref[...] = one_hot(iota((64, DEVS * 16), 1) == place)
    lane = iota((near_slots, 128), 1)
    pick = one_hot((lane & 15) == iota((near_slots, 128), 0))
    info_lanes = mm(small(info), pick).astype(I32)
    i_lane, j_lane, live_lane = (info_lanes[k : k + 1, :] for k in range(3))
    kind = (iota((1, 128), 1) >> 4) & 3
    used = (live_lane == 1) & ((kind < 2) | (i_lane != j_lane))
    target = jnp.where(kind < 2, i_lane, j_lane) * 2 + (kind & 1)
    target = jnp.where(used, target, -1)
    scatter_ref[...] = one_hot(iota((DEVS * 8, 128), 0) == target)
    rows = krylov_ref[...]
    gram = mm_exact(rows, rows, ((1,), (1,)))
    lane, row = iota((8, 128), 1) - 8, iota((8, 128), 0)
    inside = (lane >= 0) & (lane < 64)
    wide = mm_exact(gram, jnp.where(inside & ((lane & 7) == row), 1.0, 0.0), ((1,), (0,)))
    gram_ref[...] = jnp.sum(
        jnp.where(inside & ((lane >> 3) == row), wide, 0.0), axis=0, keepdims=True
    )
    fetched.wait()


def coeffs_body(gathered_ref, out_ref):
    rows = iota((DEVS, DEVS * 16), 0) * 16 + 8
    pick = one_hot(iota((DEVS, DEVS * 16), 1) == rows)
    out_ref[...] = mm(pick, gathered_ref[...]).astype(BF16)


def near_body(gathered_ref, gather_ref, scatter_ref, tiles_ref, own_ref, after_ref, before_ref,
              out_ref, *far_refs):
    far_prep(own_ref, before_ref, after_ref, *far_refs)
    taken = mm(gather_ref[...], gathered_ref[...])
    right = jnp.concatenate([taken[0:16], taken[16:32]], axis=1).astype(BF16)
    left = jnp.concatenate([taken[32:48], taken[48:64]], axis=1).astype(BF16)
    slot = iota((16, 256), 0)
    forward = jnp.zeros((16, 256), F32)
    backward = jnp.zeros((16, 256), F32)
    for s in range(tiles_ref.shape[0]):
        tile = tiles_ref[s]
        forward = jnp.where(slot == s, mm_t(right, tile), forward)
        backward = jnp.where(slot == s, mm(left, tile), backward)
    values = jnp.concatenate(
        [forward[:, :128], forward[:, 128:], backward[:, :128], backward[:, 128:]], axis=0
    )
    out_ref[...] = mm(scatter_ref[...], jnp.concatenate(halves(values), axis=0))


def far_prep(own_ref, before_ref, after_ref, pick_ref, lanes_ref, keep_ref, owner_ref, take_ref,
             give_ref):
    slots = own_ref.shape[0] - 16
    rows = [
        ref[slots : slots + 16, 0:slots].astype(F32).astype(I32)
        for ref in (own_ref, before_ref, after_ref)
    ]
    cols = jnp.concatenate([columns(r) for r in [rows[0]] + rows], axis=0)
    i_low, j_low, which, live, both = (cols[:, k : k + 1] for k in range(5))
    slot = iota((4 * slots, 1), 0) // slots
    ahead = slot == 0
    low = jnp.where(ahead, j_low, i_low)
    source = jnp.where(ahead, which, slot - 1)
    pick_ref[...] = one_hot(iota((4 * slots, 3 * DEVS), 1) == source * DEVS + (low >> 2))
    block = iota((4 * slots, 128), 1) >> 5
    lanes_ref[...] = jnp.where(block == (low & 3), 1.0, 0.0)
    wanted = jnp.where(slot == 2, 2, jnp.where(slot == 3, 1, 0))
    used = jnp.where(ahead, live, jnp.where(which == wanted, both, 0))
    target = jnp.where(ahead, i_low, j_low)
    keep_ref[...] = jnp.where((used == 1) & (block == (target & 3)), 1.0, 0.0)
    owner = iota((DEVS, slots), 0)
    for k, row in enumerate([rows[0][0:1, :]] + [r[1:2, :] for r in rows]):
        owner_ref[k] = one_hot(owner == (row >> 2))
    for k in range(8):
        sub, lane = iota((128, 128), 0), iota((128, 128), 1)
        take_ref[k] = one_hot((sub & 31) == 4 * k + (lane >> 5))
        give_ref[k] = one_hot((lane & 31) == 4 * k + (sub >> 5))


def far_body(near_ref, own_ref, after_ref, before_ref, own_coef_ref, after_coef_ref,
             before_coef_ref, pick_ref, lanes_ref, keep_ref, owner_ref, take_ref, give_ref, out_ref):
    bundles = (own_ref, before_ref, after_ref)
    slots = own_ref.shape[0] - 16
    coeffs = jnp.concatenate([own_coef_ref[...], before_coef_ref[...], after_coef_ref[...]], axis=0)
    taken = (mm(pick_ref[...], coeffs) * lanes_ref[...]).astype(BF16)
    right, left = taken[0:slots], taken[slots:]
    sub, lane = iota((128, 128), 0), iota((128, 128), 1)
    tiled = mm(right, one_hot((sub & 31) == (lane & 31)))
    forward = jnp.zeros((slots, 128), F32)
    backward = jnp.zeros(left.shape, F32)
    for k in range(8):
        parts = [b[0:slots, k * 128 : k * 128 + 128] for b in bundles]
        part = jnp.concatenate(parts, axis=0).astype(F32)
        backward = backward + part * mm(left, take_ref[k])
        for piece in halves(part[0:slots] * tiled):
            forward = forward + mm(piece, give_ref[k])
    backward = backward + pltpu.roll(backward, 64, 1)
    backward = backward + pltpu.roll(backward, 32, 1)
    sums = jnp.concatenate([forward, backward], axis=0) * keep_ref[...]
    total = jnp.zeros((DEVS, 128), F32)
    for k in range(4):
        for part in halves(sums[k * slots : k * slots + slots]):
            total = total + mm(owner_ref[k], part)
    row = iota((8, 128), 0)
    for d in range(DEVS):
        near = near_ref[d * 8 : d * 8 + 8, :]
        low = jnp.where(row == 7, total[d : d + 1, :], near - near.astype(BF16).astype(F32))
        out_ref[d] = jnp.concatenate([near, low], axis=0).astype(BF16)


def product_body(pieces_ref, bases_ref, krylov_ref, gram_ref, product_ref, copies_ref):
    total = jnp.sum(pieces_ref[...].astype(F32), axis=0)
    row, lane = iota((8, 128), 0), iota((8, 128), 1)
    near = total[0:8, :] + jnp.where(row == 7, 0.0, total[8:16, :])
    coef = total[15:16, :].astype(BF16).astype(F32)
    spread = jnp.where((lane >> 5) == (row >> 1), coef, 0.0).astype(BF16)
    low = mm(spread, bases_ref[:, :128])
    high = mm(spread, bases_ref[:, 128:])
    product = near + jnp.where((row & 1) == 0, low, high)
    product_ref[...] = product
    acc = jnp.zeros((8, 128), F32)
    for r in range(8):
        acc = acc + krylov_ref[:, r * 128 : r * 128 + 128] * product[r : r + 1, :]
    proj = jnp.sum(acc, axis=1, keepdims=True)
    square = jnp.sum(product * product, axis=1, keepdims=True)
    values = jnp.where(lane == row, proj, 0.0) + jnp.where(lane == 72, square, 0.0)
    payload = jnp.sum(values, axis=0, keepdims=True) + gram_ref[...]
    for d in range(copies_ref.shape[0]):
        copies_ref[d] = payload


def spread_body(pieces_ref, out_ref):
    total = jnp.sum(pieces_ref[...], axis=0)
    for d in range(out_ref.shape[0]):
        out_ref[d] = total


def last_body(count, pieces_ref, product_ref, krylov_ref, next_ref, proj_ref):
    total = jnp.sum(pieces_ref[...], axis=0)
    row, lane = iota((8, 128), 0), iota((8, 128), 1)
    proj = jnp.sum(jnp.where(lane == row, total, 0.0), axis=1, keepdims=True)
    inside = (lane >= 8) & (lane < 72)
    first = jnp.sum(jnp.where(inside & (((lane - 8) >> 3) == row), proj, 0.0), axis=0, keepdims=True)
    second = jnp.sum(jnp.where(inside & ((lane & 7) == row), proj, 0.0), axis=0, keepdims=True)
    lane = iota((1, 128), 1)
    terms = total * jnp.where(lane < 8, -2.0 * total, first * second)
    terms = jnp.where(lane == 72, total, jnp.where(lane < 72, terms, 0.0))
    length_sq = jnp.sum(terms, axis=1, keepdims=True)
    scale = 1.0 / jnp.sqrt(jnp.maximum(length_sq, 0.0) / count)
    for r in range(8):
        taken = jnp.sum(proj * krylov_ref[:, r * 128 : r * 128 + 128], axis=0, keepdims=True)
        next_ref[r : r + 1, :] = (product_ref[r : r + 1, :] - taken) * scale
    proj_ref[...] = total[:, 0:8]


def local(
    direction, krylov, bases, near_tiles, near_pairs, near_mask, far_blocks, far_pairs, far_mask
):
    panels = direction.shape[0]
    rank_rows = bases.reshape(-1, bases.shape[2])
    slots, far_slots = near_tiles.shape[0], far_blocks.shape[0]

    copies = call(
        pack_body,
        sds((DEVS, 16, 128), BF16),
        [HBM, HBM],
        [pltpu.VMEM((8, 128), F32), pltpu.VMEM(rank_rows.shape, BF16), pltpu.SemaphoreType.DMA((2,))],
    )(direction.reshape(8, 128), rank_rows)
    gathered = to_all(copies, "dev").reshape(-1, 128)
    bundle, tiles, gather, scatter, gram = call(
        prep_body,
        [
            sds((far_slots + 16, far_blocks.shape[1]), BF16),
            pltpu.VMEM(near_tiles.shape, BF16),
            sds((64, DEVS * 16), BF16),
            sds((DEVS * 8, 128), BF16),
            sds((1, 128), F32),
        ],
        [HBM] * 7,
        [
            pltpu.VMEM((2, far_slots), I32),
            pltpu.VMEM((1, far_slots), I32),
            pltpu.VMEM((2, slots), I32),
            pltpu.VMEM((1, slots), I32),
            pltpu.VMEM(krylov.shape, F32),
            pltpu.SemaphoreType.DMA((6,)),
            pltpu.SemaphoreType.DMA,
        ],
    )(near_tiles, far_blocks, far_pairs.T, far_mask[None], near_pairs.T, near_mask[None], krylov)
    after, before = group_shift(bundle, -1), group_shift(bundle, 1)

    coeffs = call(coeffs_body, sds((DEVS, 128), BF16), [VMEM])(gathered)
    coeffs_after, coeffs_before = group_shift(coeffs, -1), group_shift(coeffs, 1)
    near, *far_prepared = call(
        near_body,
        [
            sds((DEVS * 8, 128), F32),
            pltpu.VMEM((4 * far_slots, 3 * DEVS), BF16),
            pltpu.VMEM((4 * far_slots, 128), F32),
            pltpu.VMEM((4 * far_slots, 128), F32),
            pltpu.VMEM((4, DEVS, far_slots), BF16),
            pltpu.VMEM((8, 128, 128), BF16),
            pltpu.VMEM((8, 128, 128), BF16),
        ],
        [VMEM] * 7,
    )(gathered, gather, scatter, tiles, bundle, after, before)
    parts = call(far_body, sds((DEVS, 16, 128), BF16), [VMEM] * 13)(
        near, bundle, after, before, coeffs, coeffs_after, coeffs_before, *far_prepared
    )
    product, copies = call(
        product_body, [sds((8, 128), F32), sds((GROUPS, 1, 128), F32)], [VMEM] * 4
    )(to_all(parts, "dev"), rank_rows, krylov, gram)
    copies = call(spread_body, sds((DEVS, 1, 128), F32), [VMEM])(to_all(copies, "group"))
    pieces = to_all(copies, "dev")
    count = float(panels * DEVS * GROUPS)

    def finish(*refs):
        last_body(count, *refs)

    next_vector, projections = call(finish, [sds((8, 128), F32), sds((1, 8), F32)], [VMEM] * 3)(
        pieces, product, krylov
    )
    return (next_vector.reshape(-1), projections.reshape(-1))


def solution(mesh):
    in_specs = (
        P(("group", "dev")),
        P(None, ("group", "dev")),
        P(("group", "dev"), None, None),
        P(("group", "dev"), None, None),
        P(("group", "dev"), None),
        P(("group", "dev")),
        P(("group", "dev"), None),
        P(("group", "dev"), None),
        P(("group", "dev")),
    )
    out_specs = (P(("group", "dev")), P())
    return jax.shard_map(local, mesh=mesh, in_specs=in_specs, out_specs=out_specs, check_vma=False)
```

```python
import jax
import jax.numpy as jnp
from jax import lax
from jax.experimental import pallas as pl
from jax.experimental.pallas import tpu as pltpu
from jax.sharding import PartitionSpec as P

F32 = jnp.float32
BF16 = jnp.bfloat16
I32 = jnp.int32
NX, NZ, NY = 4, 8, 8
DEVS, GROUPS = NZ * NX, 2 * NY
VMEM = pl.BlockSpec(memory_space=pltpu.VMEM)
HBM = pl.BlockSpec(memory_space=pltpu.HBM)
sds = jax.ShapeDtypeStruct


def call(body, outs, specs, scratch=()):
    kernel = pl.pallas_call(
        body,
        out_shape=outs,
        in_specs=specs,
        out_specs=jax.tree.map(lambda _: VMEM, outs),
        scratch_shapes=list(scratch),
        compiler_params=pltpu.CompilerParams(vmem_limit_bytes=24 * 1024 * 1024),
    )

    def run(*args):
        return kernel(
            *(
                pltpu.with_memory_space_constraint(arg, pltpu.HBM) if spec is HBM else arg
                for arg, spec in zip(args, specs, strict=True)
            )
        )

    return run


def iota(shape, dim):
    return lax.broadcasted_iota(I32, shape, dim)


def mm(a, b):
    return lax.dot_general(a, b, (((1,), (0,)), ((), ())), preferred_element_type=F32)


def mm_t(a, b):
    return lax.dot_general(a, b, (((1,), (1,)), ((), ())), preferred_element_type=F32)


def mm_exact(a, b, dims):
    return lax.dot_general(
        a, b, (dims, ((), ())), precision=lax.Precision.HIGHEST, preferred_element_type=F32
    )


def halves(value):
    high = value.astype(BF16)
    return high, (value - high.astype(F32)).astype(BF16)


def one_hot(mask):
    return mask.astype(F32).astype(BF16)


def small(rows):
    return rows.astype(F32).astype(BF16)


def columns(rows):
    width = rows.shape[1]
    same = one_hot(iota((width, width), 0) == iota((width, width), 1))
    return mm_t(same, small(rows)).astype(I32)


def to_all(value, axis):
    return lax.all_to_all(value, axis, split_axis=0, concat_axis=0, tiled=True)


def group_shift(value, step):
    return lax.ppermute(value, "group", [(g, (g + step) % GROUPS) for g in range(GROUPS)])


def started(ends, sems):
    copies = [pltpu.make_async_copy(*end, sems.at[k]) for k, end in enumerate(ends)]
    for copy in copies:
        copy.start()
    return copies


def pack_body(direction_hbm, bases_hbm, out_ref, direction_ref, bases_ref, sems):
    for copy in started(((direction_hbm, direction_ref), (bases_hbm, bases_ref)), sems):
        copy.wait()
    xb = direction_ref[...].astype(BF16)
    rank_rows = bases_ref[...]
    low = mm_t(xb, rank_rows[:, :128])
    high = mm_t(xb, rank_rows[:, 128:])
    row = iota((8, 128), 0)
    twice = (iota((8, 128), 1) >> 5) * 2
    kept = jnp.where(row == twice, low, 0.0) + jnp.where(row == twice + 1, high, 0.0)
    coeffs = jnp.sum(kept, axis=0, keepdims=True)
    packed = jnp.concatenate([xb, jnp.where(row == 0, coeffs, 0.0).astype(BF16)], axis=0)
    for d in range(DEVS):
        out_ref[d] = packed


def prep_body(tiles_hbm, blocks_hbm, pairs_hbm, mask_hbm, near_pairs_hbm, near_mask_hbm, krylov_hbm,
              out_ref, tiles_ref, gather_ref, scatter_ref, gram_ref,
              pairs_ref, mask_ref, near_pairs_ref, near_mask_ref, krylov_ref, sems, tile_sem):
    fetched = pltpu.make_async_copy(tiles_hbm, tiles_ref, tile_sem)
    slots = blocks_hbm.shape[0]
    ends = (
        (blocks_hbm, out_ref.at[0:slots]),
        (pairs_hbm, pairs_ref),
        (mask_hbm, mask_ref),
        (near_pairs_hbm, near_pairs_ref),
        (near_mask_hbm, near_mask_ref),
        (krylov_hbm, krylov_ref),
    )
    copies = started(ends, sems)
    fetched.start()
    for copy in copies:
        copy.wait()
    i_row, j_row = pairs_ref[0:1, :], pairs_ref[1:2, :]
    step = ((j_row >> 7) - (i_row >> 7)) & (GROUPS - 1)
    which = jnp.where(step == 0, 0, jnp.where(step == 1, 2, 1))
    live = mask_ref[...]
    both = jnp.where(i_row == j_row, 0, live)
    row = iota((16, slots), 0)
    digits = jnp.zeros((16, slots), I32)
    for k, value in enumerate((i_row & 127, j_row & 127, which, live, both)):
        digits = jnp.where(row == k, value, digits)
    out_ref[slots : slots + 16, :] = jnp.zeros((16, out_ref.shape[1]), BF16)
    out_ref[slots : slots + 16, 0:slots] = small(digits)
    near = near_pairs_ref[...]
    live = near_mask_ref[...]
    near_slots = near.shape[1]
    row = iota((8, near_slots), 0)
    info = jnp.where(row == 0, near[0:1, :], jnp.where(row == 1, near[1:2, :], live))
    m = iota((64, near_slots), 0)
    pick = one_hot((m & 15) == iota((64, near_slots), 1))
    info_cols = mm_t(pick, small(info)).astype(I32)
    i_col, j_col = info_cols[:, 0:1], info_cols[:, 1:2]
    m = iota((64, 1), 0) >> 4
    c = jnp.where(m < 2, j_col, i_col)
    place = (c >> 2) * 16 + (c & 3) * 2 + (m & 1)
    gather_ref[...] = one_hot(iota((64, DEVS * 16), 1) == place)
    lane = iota((near_slots, 128), 1)
    pick = one_hot((lane & 15) == iota((near_slots, 128), 0))
    info_lanes = mm(small(info), pick).astype(I32)
    i_lane, j_lane, live_lane = (info_lanes[k : k + 1, :] for k in range(3))
    kind = (iota((1, 128), 1) >> 4) & 3
    used = (live_lane == 1) & ((kind < 2) | (i_lane != j_lane))
    target = jnp.where(kind < 2, i_lane, j_lane) * 2 + (kind & 1)
    target = jnp.where(used, target, -1)
    scatter_ref[...] = one_hot(iota((DEVS * 8, 128), 0) == target)
    rows = krylov_ref[...]
    gram = mm_exact(rows, rows, ((1,), (1,)))
    lane, row = iota((8, 128), 1) - 8, iota((8, 128), 0)
    inside = (lane >= 0) & (lane < 64)
    wide = mm_exact(gram, jnp.where(inside & ((lane & 7) == row), 1.0, 0.0), ((1,), (0,)))
    gram_ref[...] = jnp.sum(
        jnp.where(inside & ((lane >> 3) == row), wide, 0.0), axis=0, keepdims=True
    )
    fetched.wait()


def coeffs_body(gathered_ref, out_ref):
    rows = iota((DEVS, DEVS * 16), 0) * 16 + 8
    pick = one_hot(iota((DEVS, DEVS * 16), 1) == rows)
    out_ref[...] = mm(pick, gathered_ref[...]).astype(BF16)


def near_body(gathered_ref, gather_ref, scatter_ref, tiles_ref, own_ref, before_ref, after_ref,
              out_ref, *far_refs):
    far_prep(own_ref, before_ref, after_ref, *far_refs)
    taken = mm(gather_ref[...], gathered_ref[...])
    right = jnp.concatenate([taken[0:16], taken[16:32]], axis=1).astype(BF16)
    left = jnp.concatenate([taken[32:48], taken[48:64]], axis=1).astype(BF16)
    slot = iota((16, 256), 0)
    forward = jnp.zeros((16, 256), F32)
    backward = jnp.zeros((16, 256), F32)
    for s in range(tiles_ref.shape[0]):
        tile = tiles_ref[s]
        forward = jnp.where(slot == s, mm_t(right, tile), forward)
        backward = jnp.where(slot == s, mm(left, tile), backward)
    values = jnp.concatenate(
        [forward[:, :128], forward[:, 128:], backward[:, :128], backward[:, 128:]], axis=0
    )
    out_ref[...] = mm(scatter_ref[...], jnp.concatenate(halves(values), axis=0))


def far_prep(own_ref, before_ref, after_ref, pick_ref, lanes_ref, keep_ref, owner_ref, take_ref,
             give_ref):
    slots = own_ref.shape[0] - 16
    rows = [
        ref[slots : slots + 16, 0:slots].astype(F32).astype(I32)
        for ref in (own_ref, before_ref, after_ref)
    ]
    cols = jnp.concatenate([columns(r) for r in [rows[0]] + rows], axis=0)
    i_low, j_low, which, live, both = (cols[:, k : k + 1] for k in range(5))
    slot = iota((4 * slots, 1), 0) // slots
    ahead = slot == 0
    low = jnp.where(ahead, j_low, i_low)
    source = jnp.where(ahead, which, slot - 1)
    pick_ref[...] = one_hot(iota((4 * slots, 3 * DEVS), 1) == source * DEVS + (low >> 2))
    block = iota((4 * slots, 128), 1) >> 5
    lanes_ref[...] = jnp.where(block == (low & 3), 1.0, 0.0)
    wanted = jnp.where(slot == 2, 2, jnp.where(slot == 3, 1, 0))
    used = jnp.where(ahead, live, jnp.where(which == wanted, both, 0))
    target = jnp.where(ahead, i_low, j_low)
    keep_ref[...] = jnp.where((used == 1) & (block == (target & 3)), 1.0, 0.0)
    owner = iota((DEVS, slots), 0)
    for k, row in enumerate([rows[0][0:1, :]] + [r[1:2, :] for r in rows]):
        owner_ref[k] = one_hot(owner == (row >> 2))
    for k in range(8):
        sub, lane = iota((128, 128), 0), iota((128, 128), 1)
        take_ref[k] = one_hot((sub & 31) == 4 * k + (lane >> 5))
        give_ref[k] = one_hot((lane & 31) == 4 * k + (sub >> 5))


def far_body(near_ref, own_ref, before_ref, after_ref, own_coef_ref, before_coef_ref,
             after_coef_ref, pick_ref, lanes_ref, keep_ref, owner_ref, take_ref, give_ref, out_ref):
    bundles = (own_ref, before_ref, after_ref)
    slots = own_ref.shape[0] - 16
    coeffs = jnp.concatenate([own_coef_ref[...], before_coef_ref[...], after_coef_ref[...]], axis=0)
    taken = mm(pick_ref[...], coeffs) * lanes_ref[...]
    right, left = taken[0:slots], taken[slots:].astype(BF16)
    tiled = right + pltpu.roll(right, 64, 1)
    tiled = tiled + pltpu.roll(tiled, 32, 1)
    forward = jnp.zeros((slots, 128), F32)
    backward = jnp.zeros(left.shape, F32)
    for k in range(8):
        parts = [b[0:slots, k * 128 : k * 128 + 128] for b in bundles]
        part = jnp.concatenate(parts, axis=0).astype(F32)
        backward = backward + part * mm(left, take_ref[k])
        for piece in halves(part[0:slots] * tiled):
            forward = forward + mm(piece, give_ref[k])
    backward = backward + pltpu.roll(backward, 64, 1)
    backward = backward + pltpu.roll(backward, 32, 1)
    sums = jnp.concatenate([forward, backward], axis=0) * keep_ref[...]
    total = jnp.zeros((DEVS, 128), F32)
    for k in range(4):
        for part in halves(sums[k * slots : k * slots + slots]):
            total = total + mm(owner_ref[k], part)
    row = iota((8, 128), 0)
    far_high = total.astype(BF16).astype(F32)
    far_low = total - far_high
    for d in range(DEVS):
        near = near_ref[d * 8 : d * 8 + 8, :]
        near_low = near - near.astype(BF16).astype(F32)
        tail = jnp.where(row == 0, far_high[d : d + 1, :], far_low[d : d + 1, :])
        out_ref[d] = jnp.concatenate([near, near_low, tail], axis=0).astype(BF16)


def product_body(pieces_ref, bases_ref, krylov_ref, gram_ref, product_ref, copies_ref):
    total = jnp.sum(pieces_ref[...].astype(F32), axis=0)
    row, lane = iota((8, 128), 0), iota((8, 128), 1)
    near = total[0:8, :] + total[8:16, :]
    coef = (total[16:17, :] + total[17:18, :]).astype(BF16).astype(F32)
    spread = jnp.where((lane >> 5) == (row >> 1), coef, 0.0).astype(BF16)
    low = mm(spread, bases_ref[:, :128])
    high = mm(spread, bases_ref[:, 128:])
    product = near + jnp.where((row & 1) == 0, low, high)
    product_ref[...] = product
    acc = jnp.zeros((8, 128), F32)
    for r in range(8):
        acc = acc + krylov_ref[:, r * 128 : r * 128 + 128] * product[r : r + 1, :]
    proj = jnp.sum(acc, axis=1, keepdims=True)
    square = jnp.sum(product * product, axis=1, keepdims=True)
    values = jnp.where(lane == row, proj, 0.0) + jnp.where(lane == 72, square, 0.0)
    payload = jnp.sum(values, axis=0, keepdims=True) + gram_ref[...]
    for d in range(copies_ref.shape[0]):
        copies_ref[d] = payload


def spread_body(pieces_ref, out_ref):
    total = jnp.sum(pieces_ref[...], axis=0)
    for d in range(out_ref.shape[0]):
        out_ref[d] = total


def last_body(count, pieces_ref, product_ref, krylov_ref, next_ref, proj_ref):
    total = jnp.sum(pieces_ref[...], axis=0)
    row, lane = iota((8, 128), 0), iota((8, 128), 1)
    proj = jnp.sum(jnp.where(lane == row, total, 0.0), axis=1, keepdims=True)
    inside = (lane >= 8) & (lane < 72)
    first = jnp.sum(jnp.where(inside & (((lane - 8) >> 3) == row), proj, 0.0), axis=0, keepdims=True)
    second = jnp.sum(jnp.where(inside & ((lane & 7) == row), proj, 0.0), axis=0, keepdims=True)
    lane = iota((1, 128), 1)
    terms = total * jnp.where(lane < 8, -2.0 * total, first * second)
    terms = jnp.where(lane == 72, total, jnp.where(lane < 72, terms, 0.0))
    length_sq = jnp.sum(terms, axis=1, keepdims=True)
    scale = 1.0 / jnp.sqrt(jnp.maximum(length_sq, 0.0) / count)
    for r in range(8):
        taken = jnp.sum(proj * krylov_ref[:, r * 128 : r * 128 + 128], axis=0, keepdims=True)
        next_ref[r : r + 1, :] = (product_ref[r : r + 1, :] - taken) * scale
    proj_ref[...] = total[:, 0:8]


def local(
    direction, krylov, bases, near_tiles, near_pairs, near_mask, far_blocks, far_pairs, far_mask
):
    panels = direction.shape[0]
    rank_rows = bases.reshape(-1, bases.shape[2])
    slots, far_slots = near_tiles.shape[0], far_blocks.shape[0]

    copies = call(
        pack_body,
        sds((DEVS, 16, 128), BF16),
        [HBM, HBM],
        [pltpu.VMEM((8, 128), F32), pltpu.VMEM(rank_rows.shape, BF16), pltpu.SemaphoreType.DMA((2,))],
    )(direction.reshape(8, 128), rank_rows)
    gathered = to_all(copies, "dev").reshape(-1, 128)
    bundle, tiles, gather, scatter, gram = call(
        prep_body,
        [
            sds((far_slots + 16, far_blocks.shape[1]), BF16),
            pltpu.VMEM(near_tiles.shape, BF16),
            sds((64, DEVS * 16), BF16),
            sds((DEVS * 8, 128), BF16),
            sds((1, 128), F32),
        ],
        [HBM] * 7,
        [
            pltpu.VMEM((2, far_slots), I32),
            pltpu.VMEM((1, far_slots), I32),
            pltpu.VMEM((2, slots), I32),
            pltpu.VMEM((1, slots), I32),
            pltpu.VMEM(krylov.shape, F32),
            pltpu.SemaphoreType.DMA((6,)),
            pltpu.SemaphoreType.DMA,
        ],
    )(near_tiles, far_blocks, far_pairs.T, far_mask[None], near_pairs.T, near_mask[None], krylov)
    before, after = group_shift(bundle, 1), group_shift(bundle, -1)

    coeffs = call(coeffs_body, sds((DEVS, 128), BF16), [VMEM])(gathered)
    coeffs_before, coeffs_after = group_shift(coeffs, 1), group_shift(coeffs, -1)
    near, *far_prepared = call(
        near_body,
        [
            sds((DEVS * 8, 128), F32),
            pltpu.VMEM((4 * far_slots, 3 * DEVS), BF16),
            pltpu.VMEM((4 * far_slots, 128), F32),
            pltpu.VMEM((4 * far_slots, 128), F32),
            pltpu.VMEM((4, DEVS, far_slots), BF16),
            pltpu.VMEM((8, 128, 128), BF16),
            pltpu.VMEM((8, 128, 128), BF16),
        ],
        [VMEM] * 7,
    )(gathered, gather, scatter, tiles, bundle, before, after)
    parts = call(far_body, sds((DEVS, 24, 128), BF16), [VMEM] * 13)(
        near, bundle, before, after, coeffs, coeffs_before, coeffs_after, *far_prepared
    )
    product, copies = call(
        product_body, [sds((8, 128), F32), sds((GROUPS, 1, 128), F32)], [VMEM] * 4
    )(to_all(parts, "dev"), rank_rows, krylov, gram)
    copies = call(spread_body, sds((DEVS, 1, 128), F32), [VMEM])(to_all(copies, "group"))
    pieces = to_all(copies, "dev")
    count = float(panels * DEVS * GROUPS)

    def finish(*refs):
        last_body(count, *refs)

    next_vector, projections = call(finish, [sds((8, 128), F32), sds((1, 8), F32)], [VMEM] * 3)(
        pieces, product, krylov
    )
    return (next_vector.reshape(-1), projections.reshape(-1))


def solution(mesh):
    in_specs = (
        P(("group", "dev")),
        P(None, ("group", "dev")),
        P(("group", "dev"), None, None),
        P(("group", "dev"), None, None),
        P(("group", "dev"), None),
        P(("group", "dev")),
        P(("group", "dev"), None),
        P(("group", "dev"), None),
        P(("group", "dev")),
    )
    out_specs = (P(("group", "dev")), P())
    return jax.shard_map(local, mesh=mesh, in_specs=in_specs, out_specs=out_specs, check_vma=False)
```

```python
import jax
import jax.numpy as jnp
from jax import lax
from jax.experimental import pallas as pl
from jax.experimental.pallas import tpu as pltpu
from jax.sharding import PartitionSpec as P

F32 = jnp.float32
BF16 = jnp.bfloat16
I32 = jnp.int32
NX, NZ, NY = 4, 8, 8
DEVS, GROUPS = NZ * NX, 2 * NY
VMEM = pl.BlockSpec(memory_space=pltpu.VMEM)
HBM = pl.BlockSpec(memory_space=pltpu.HBM)
sds = jax.ShapeDtypeStruct


def call(body, outs, specs, scratch=()):
    kernel = pl.pallas_call(
        body,
        out_shape=outs,
        in_specs=specs,
        out_specs=jax.tree.map(lambda _: VMEM, outs),
        scratch_shapes=list(scratch),
        compiler_params=pltpu.CompilerParams(vmem_limit_bytes=24 * 1024 * 1024),
    )

    def run(*args):
        return kernel(
            *(
                pltpu.with_memory_space_constraint(arg, pltpu.HBM) if spec is HBM else arg
                for arg, spec in zip(args, specs, strict=True)
            )
        )

    return run


def iota(shape, dim):
    return lax.broadcasted_iota(I32, shape, dim)


def mm(a, b):
    return lax.dot_general(a, b, (((1,), (0,)), ((), ())), preferred_element_type=F32)


def mm_t(a, b):
    return lax.dot_general(a, b, (((1,), (1,)), ((), ())), preferred_element_type=F32)


def mm_exact(a, b, dims):
    return lax.dot_general(
        a, b, (dims, ((), ())), precision=lax.Precision.HIGHEST, preferred_element_type=F32
    )


def halves(value):
    high = value.astype(BF16)
    return high, (value - high.astype(F32)).astype(BF16)


def one_hot(mask):
    return mask.astype(F32).astype(BF16)


def small(rows):
    return rows.astype(F32).astype(BF16)


def columns(rows):
    width = rows.shape[1]
    same = one_hot(iota((width, width), 0) == iota((width, width), 1))
    return mm_t(same, small(rows)).astype(I32)


def to_all(value, axis):
    return lax.all_to_all(value, axis, split_axis=0, concat_axis=0, tiled=True)


def group_shift(value, step):
    return lax.ppermute(value, "group", [(g, (g + step) % GROUPS) for g in range(GROUPS)])


def started(ends, sems):
    copies = [pltpu.make_async_copy(*end, sems.at[k]) for k, end in enumerate(ends)]
    for copy in copies:
        copy.start()
    return copies


def pack_body(direction_hbm, bases_hbm, out_ref, direction_ref, bases_ref, sems):
    for copy in started(((direction_hbm, direction_ref), (bases_hbm, bases_ref)), sems):
        copy.wait()
    xb = direction_ref[...].astype(BF16)
    rank_rows = bases_ref[...]
    low = mm_t(xb, rank_rows[:, :128])
    high = mm_t(xb, rank_rows[:, 128:])
    row = iota((8, 128), 0)
    twice = (iota((8, 128), 1) >> 5) * 2
    kept = jnp.where(row == twice, low, 0.0) + jnp.where(row == twice + 1, high, 0.0)
    coeffs = jnp.sum(kept, axis=0, keepdims=True)
    packed = jnp.concatenate([xb, jnp.where(row == 0, coeffs, 0.0).astype(BF16)], axis=0)
    for d in range(DEVS):
        out_ref[d] = packed


def prep_body(tiles_hbm, blocks_hbm, pairs_hbm, mask_hbm, near_pairs_hbm, near_mask_hbm, krylov_hbm,
              out_ref, tiles_ref, gather_ref, scatter_ref, gram_ref,
              pairs_ref, mask_ref, near_pairs_ref, near_mask_ref, krylov_ref, sems, tile_sem):
    fetched = pltpu.make_async_copy(tiles_hbm, tiles_ref, tile_sem)
    slots = blocks_hbm.shape[0]
    ends = (
        (blocks_hbm, out_ref.at[0:slots]),
        (pairs_hbm, pairs_ref),
        (mask_hbm, mask_ref),
        (near_pairs_hbm, near_pairs_ref),
        (near_mask_hbm, near_mask_ref),
        (krylov_hbm, krylov_ref),
    )
    copies = started(ends, sems)
    fetched.start()
    for copy in copies:
        copy.wait()
    i_row, j_row = pairs_ref[0:1, :], pairs_ref[1:2, :]
    step = ((j_row >> 7) - (i_row >> 7)) & (GROUPS - 1)
    which = jnp.where(step == 0, 0, jnp.where(step == 1, 2, 1))
    live = mask_ref[...]
    both = jnp.where(i_row == j_row, 0, live)
    row = iota((16, slots), 0)
    digits = jnp.zeros((16, slots), I32)
    for k, value in enumerate((i_row & 127, j_row & 127, which, live, both)):
        digits = jnp.where(row == k, value, digits)
    out_ref[slots : slots + 16, :] = jnp.zeros((16, out_ref.shape[1]), BF16)
    out_ref[slots : slots + 16, 0:slots] = small(digits)
    near = near_pairs_ref[...]
    live = near_mask_ref[...]
    near_slots = near.shape[1]
    row = iota((8, near_slots), 0)
    info = jnp.where(row == 0, near[0:1, :], jnp.where(row == 1, near[1:2, :], live))
    m = iota((64, near_slots), 0)
    pick = one_hot((m & 15) == iota((64, near_slots), 1))
    info_cols = mm_t(pick, small(info)).astype(I32)
    i_col, j_col = info_cols[:, 0:1], info_cols[:, 1:2]
    m = iota((64, 1), 0) >> 4
    c = jnp.where(m < 2, j_col, i_col)
    place = (c >> 2) * 16 + (c & 3) * 2 + (m & 1)
    gather_ref[...] = one_hot(iota((64, DEVS * 16), 1) == place)
    lane = iota((near_slots, 128), 1)
    pick = one_hot((lane & 15) == iota((near_slots, 128), 0))
    info_lanes = mm(small(info), pick).astype(I32)
    i_lane, j_lane, live_lane = (info_lanes[k : k + 1, :] for k in range(3))
    kind = (iota((1, 128), 1) >> 4) & 3
    used = (live_lane == 1) & ((kind < 2) | (i_lane != j_lane))
    target = jnp.where(kind < 2, i_lane, j_lane) * 2 + (kind & 1)
    target = jnp.where(used, target, -1)
    scatter_ref[...] = one_hot(iota((DEVS * 8, 128), 0) == target)
    rows = krylov_ref[...]
    gram = mm_exact(rows, rows, ((1,), (1,)))
    lane, row = iota((8, 128), 1) - 8, iota((8, 128), 0)
    inside = (lane >= 0) & (lane < 64)
    wide = mm_exact(gram, jnp.where(inside & ((lane & 7) == row), 1.0, 0.0), ((1,), (0,)))
    gram_ref[...] = jnp.sum(
        jnp.where(inside & ((lane >> 3) == row), wide, 0.0), axis=0, keepdims=True
    )
    fetched.wait()


def coeffs_body(gathered_ref, out_ref):
    rows = iota((DEVS, DEVS * 16), 0) * 16 + 8
    pick = one_hot(iota((DEVS, DEVS * 16), 1) == rows)
    out_ref[...] = mm(pick, gathered_ref[...]).astype(BF16)


def near_body(gathered_ref, gather_ref, scatter_ref, tiles_ref, own_ref, before_ref, after_ref,
              out_ref, *far_refs):
    far_prep(own_ref, before_ref, after_ref, *far_refs)
    taken = mm(gather_ref[...], gathered_ref[...])
    right = jnp.concatenate([taken[0:16], taken[16:32]], axis=1).astype(BF16)
    left = jnp.concatenate([taken[32:48], taken[48:64]], axis=1).astype(BF16)
    slot = iota((16, 256), 0)
    forward = jnp.zeros((16, 256), F32)
    backward = jnp.zeros((16, 256), F32)
    for s in range(tiles_ref.shape[0]):
        tile = tiles_ref[s]
        forward = jnp.where(slot == s, mm_t(right, tile), forward)
        backward = jnp.where(slot == s, mm(left, tile), backward)
    values = jnp.concatenate(
        [forward[:, :128], forward[:, 128:], backward[:, :128], backward[:, 128:]], axis=0
    )
    out_ref[...] = mm(scatter_ref[...], jnp.concatenate(halves(values), axis=0))


def far_prep(own_ref, before_ref, after_ref, pick_ref, lanes_ref, keep_ref, owner_ref, take_ref,
             give_ref):
    slots = own_ref.shape[0] - 16
    rows = [
        ref[slots : slots + 16, 0:slots].astype(F32).astype(I32)
        for ref in (own_ref, before_ref, after_ref)
    ]
    cols = jnp.concatenate([columns(r) for r in [rows[0]] + rows], axis=0)
    i_low, j_low, which, live, both = (cols[:, k : k + 1] for k in range(5))
    slot = iota((4 * slots, 1), 0) // slots
    ahead = slot == 0
    low = jnp.where(ahead, j_low, i_low)
    source = jnp.where(ahead, which, slot - 1)
    pick_ref[...] = one_hot(iota((4 * slots, 3 * DEVS), 1) == source * DEVS + (low >> 2))
    block = iota((4 * slots, 128), 1) >> 5
    lanes_ref[...] = jnp.where(block == (low & 3), 1.0, 0.0)
    wanted = jnp.where(slot == 2, 2, jnp.where(slot == 3, 1, 0))
    used = jnp.where(ahead, live, jnp.where(which == wanted, both, 0))
    target = jnp.where(ahead, i_low, j_low)
    keep_ref[...] = jnp.where((used == 1) & (block == (target & 3)), 1.0, 0.0)
    owner = iota((DEVS, slots), 0)
    for k, row in enumerate([rows[0][0:1, :]] + [r[1:2, :] for r in rows]):
        owner_ref[k] = one_hot(owner == (row >> 2))
    for k in range(8):
        sub, lane = iota((128, 128), 0), iota((128, 128), 1)
        take_ref[k] = one_hot((sub & 31) == 4 * k + (lane >> 5))
        give_ref[k] = one_hot((lane & 31) == 4 * k + (sub >> 5))


def far_body(near_ref, own_ref, before_ref, after_ref, own_coef_ref, before_coef_ref,
             after_coef_ref, pick_ref, lanes_ref, keep_ref, owner_ref, take_ref, give_ref, out_ref):
    bundles = (own_ref, before_ref, after_ref)
    slots = own_ref.shape[0] - 16
    coeffs = jnp.concatenate([own_coef_ref[...], before_coef_ref[...], after_coef_ref[...]], axis=0)
    taken = (mm(pick_ref[...], coeffs) * lanes_ref[...]).astype(BF16)
    right, left = taken[0:slots], taken[slots:]
    sub, lane = iota((128, 128), 0), iota((128, 128), 1)
    tiled = mm(right, one_hot((sub & 31) == (lane & 31)))
    forward = jnp.zeros((slots, 128), F32)
    backward = jnp.zeros(left.shape, F32)
    for k in range(8):
        parts = [b[0:slots, k * 128 : k * 128 + 128] for b in bundles]
        part = jnp.concatenate(parts, axis=0).astype(F32)
        backward = backward + part * mm(left, take_ref[k])
        for piece in halves(part[0:slots] * tiled):
            forward = forward + mm(piece, give_ref[k])
    backward = backward + pltpu.roll(backward, 64, 1)
    backward = backward + pltpu.roll(backward, 32, 1)
    sums = jnp.concatenate([forward, backward], axis=0) * keep_ref[...]
    total = jnp.zeros((DEVS, 128), F32)
    for k in range(4):
        for part in halves(sums[k * slots : k * slots + slots]):
            total = total + mm(owner_ref[k], part)
    row = iota((8, 128), 0)
    far_high = total.astype(BF16).astype(F32)
    far_low = total - far_high
    for d in range(DEVS):
        near = near_ref[d * 8 : d * 8 + 8, :]
        low = jnp.where(row == 6, far_high[d : d + 1, :], near - near.astype(BF16).astype(F32))
        low = jnp.where(row == 7, far_low[d : d + 1, :], low)
        out_ref[d] = jnp.concatenate([near, low], axis=0).astype(BF16)


def product_body(pieces_ref, bases_ref, krylov_ref, gram_ref, product_ref, copies_ref):
    total = jnp.sum(pieces_ref[...].astype(F32), axis=0)
    row, lane = iota((8, 128), 0), iota((8, 128), 1)
    near = total[0:8, :] + jnp.where(row < 6, total[8:16, :], 0.0)
    coef = (total[14:15, :] + total[15:16, :]).astype(BF16).astype(F32)
    spread = jnp.where((lane >> 5) == (row >> 1), coef, 0.0).astype(BF16)
    low = mm(spread, bases_ref[:, :128])
    high = mm(spread, bases_ref[:, 128:])
    product = near + jnp.where((row & 1) == 0, low, high)
    product_ref[...] = product
    acc = jnp.zeros((8, 128), F32)
    for r in range(8):
        acc = acc + krylov_ref[:, r * 128 : r * 128 + 128] * product[r : r + 1, :]
    proj = jnp.sum(acc, axis=1, keepdims=True)
    square = jnp.sum(product * product, axis=1, keepdims=True)
    values = jnp.where(lane == row, proj, 0.0) + jnp.where(lane == 72, square, 0.0)
    payload = jnp.sum(values, axis=0, keepdims=True) + gram_ref[...]
    for d in range(copies_ref.shape[0]):
        copies_ref[d] = payload


def spread_body(pieces_ref, out_ref):
    total = jnp.sum(pieces_ref[...], axis=0)
    for d in range(out_ref.shape[0]):
        out_ref[d] = total


def last_body(count, pieces_ref, product_ref, krylov_ref, next_ref, proj_ref):
    total = jnp.sum(pieces_ref[...], axis=0)
    row, lane = iota((8, 128), 0), iota((8, 128), 1)
    proj = jnp.sum(jnp.where(lane == row, total, 0.0), axis=1, keepdims=True)
    inside = (lane >= 8) & (lane < 72)
    first = jnp.sum(jnp.where(inside & (((lane - 8) >> 3) == row), proj, 0.0), axis=0, keepdims=True)
    second = jnp.sum(jnp.where(inside & ((lane & 7) == row), proj, 0.0), axis=0, keepdims=True)
    lane = iota((1, 128), 1)
    terms = total * jnp.where(lane < 8, -2.0 * total, first * second)
    terms = jnp.where(lane == 72, total, jnp.where(lane < 72, terms, 0.0))
    length_sq = jnp.sum(terms, axis=1, keepdims=True)
    scale = 1.0 / jnp.sqrt(jnp.maximum(length_sq, 0.0) / count)
    for r in range(8):
        taken = jnp.sum(proj * krylov_ref[:, r * 128 : r * 128 + 128], axis=0, keepdims=True)
        next_ref[r : r + 1, :] = (product_ref[r : r + 1, :] - taken) * scale
    proj_ref[...] = total[:, 0:8]


def local(
    direction, krylov, bases, near_tiles, near_pairs, near_mask, far_blocks, far_pairs, far_mask
):
    panels = direction.shape[0]
    rank_rows = bases.reshape(-1, bases.shape[2])
    slots, far_slots = near_tiles.shape[0], far_blocks.shape[0]

    copies = call(
        pack_body,
        sds((DEVS, 16, 128), BF16),
        [HBM, HBM],
        [pltpu.VMEM((8, 128), F32), pltpu.VMEM(rank_rows.shape, BF16), pltpu.SemaphoreType.DMA((2,))],
    )(direction.reshape(8, 128), rank_rows)
    gathered = to_all(copies, "dev").reshape(-1, 128)
    bundle, tiles, gather, scatter, gram = call(
        prep_body,
        [
            sds((far_slots + 16, far_blocks.shape[1]), BF16),
            pltpu.VMEM(near_tiles.shape, BF16),
            sds((64, DEVS * 16), BF16),
            sds((DEVS * 8, 128), BF16),
            sds((1, 128), F32),
        ],
        [HBM] * 7,
        [
            pltpu.VMEM((2, far_slots), I32),
            pltpu.VMEM((1, far_slots), I32),
            pltpu.VMEM((2, slots), I32),
            pltpu.VMEM((1, slots), I32),
            pltpu.VMEM(krylov.shape, F32),
            pltpu.SemaphoreType.DMA((6,)),
            pltpu.SemaphoreType.DMA,
        ],
    )(near_tiles, far_blocks, far_pairs.T, far_mask[None], near_pairs.T, near_mask[None], krylov)
    before, after = group_shift(bundle, 1), group_shift(bundle, -1)

    coeffs = call(coeffs_body, sds((DEVS, 128), BF16), [VMEM])(gathered)
    coeffs_before, coeffs_after = group_shift(coeffs, 1), group_shift(coeffs, -1)
    near, *far_prepared = call(
        near_body,
        [
            sds((DEVS * 8, 128), F32),
            pltpu.VMEM((4 * far_slots, 3 * DEVS), BF16),
            pltpu.VMEM((4 * far_slots, 128), F32),
            pltpu.VMEM((4 * far_slots, 128), F32),
            pltpu.VMEM((4, DEVS, far_slots), BF16),
            pltpu.VMEM((8, 128, 128), BF16),
            pltpu.VMEM((8, 128, 128), BF16),
        ],
        [VMEM] * 7,
    )(gathered, gather, scatter, tiles, bundle, before, after)
    parts = call(far_body, sds((DEVS, 16, 128), BF16), [VMEM] * 13)(
        near, bundle, before, after, coeffs, coeffs_before, coeffs_after, *far_prepared
    )
    product, copies = call(
        product_body, [sds((8, 128), F32), sds((GROUPS, 1, 128), F32)], [VMEM] * 4
    )(to_all(parts, "dev"), rank_rows, krylov, gram)
    copies = call(spread_body, sds((DEVS, 1, 128), F32), [VMEM])(to_all(copies, "group"))
    pieces = to_all(copies, "dev")
    count = float(panels * DEVS * GROUPS)

    def finish(*refs):
        last_body(count, *refs)

    next_vector, projections = call(finish, [sds((8, 128), F32), sds((1, 8), F32)], [VMEM] * 3)(
        pieces, product, krylov
    )
    return (next_vector.reshape(-1), projections.reshape(-1))


def solution(mesh):
    in_specs = (
        P(("group", "dev")),
        P(None, ("group", "dev")),
        P(("group", "dev"), None, None),
        P(("group", "dev"), None, None),
        P(("group", "dev"), None),
        P(("group", "dev")),
        P(("group", "dev"), None),
        P(("group", "dev"), None),
        P(("group", "dev")),
    )
    out_specs = (P(("group", "dev")), P())
    return jax.shard_map(local, mesh=mesh, in_specs=in_specs, out_specs=out_specs, check_vma=False)
```

```python
import jax
import jax.numpy as jnp
from jax import lax
from jax.experimental import pallas as pl
from jax.experimental.pallas import tpu as pltpu
from jax.sharding import PartitionSpec as P

F32 = jnp.float32
BF16 = jnp.bfloat16
I32 = jnp.int32
NX, NZ, NY = 4, 8, 8
DEVS, GROUPS = NZ * NX, 2 * NY
VMEM = pl.BlockSpec(memory_space=pltpu.VMEM)
HBM = pl.BlockSpec(memory_space=pltpu.HBM)
sds = jax.ShapeDtypeStruct


def call(body, outs, specs, scratch=()):
    kernel = pl.pallas_call(
        body,
        out_shape=outs,
        in_specs=specs,
        out_specs=jax.tree.map(lambda _: VMEM, outs),
        scratch_shapes=list(scratch),
        compiler_params=pltpu.CompilerParams(vmem_limit_bytes=24 * 1024 * 1024),
    )

    def run(*args):
        return kernel(
            *(
                pltpu.with_memory_space_constraint(arg, pltpu.HBM) if spec is HBM else arg
                for arg, spec in zip(args, specs, strict=True)
            )
        )

    return run


def iota(shape, dim):
    return lax.broadcasted_iota(I32, shape, dim)


def mm(a, b):
    return lax.dot_general(a, b, (((1,), (0,)), ((), ())), preferred_element_type=F32)


def mm_t(a, b):
    return lax.dot_general(a, b, (((1,), (1,)), ((), ())), preferred_element_type=F32)


def mm_exact(a, b, dims):
    return lax.dot_general(
        a, b, (dims, ((), ())), precision=lax.Precision.HIGHEST, preferred_element_type=F32
    )


def halves(value):
    high = value.astype(BF16)
    return high, (value - high.astype(F32)).astype(BF16)


def one_hot(mask):
    return mask.astype(F32).astype(BF16)


def small(rows):
    return rows.astype(F32).astype(BF16)


def columns(rows):
    width = rows.shape[1]
    same = one_hot(iota((width, width), 0) == iota((width, width), 1))
    return mm_t(same, small(rows)).astype(I32)


def to_all(value, axis):
    return lax.all_to_all(value, axis, split_axis=0, concat_axis=0, tiled=True)


def group_shift(value, step):
    return lax.ppermute(value, "group", [(g, (g + step) % GROUPS) for g in range(GROUPS)])


def started(ends, sems):
    copies = [pltpu.make_async_copy(*end, sems.at[k]) for k, end in enumerate(ends)]
    for copy in copies:
        copy.start()
    return copies


def pack_body(direction_hbm, bases_hbm, out_ref, direction_ref, bases_ref, sems):
    for copy in started(((direction_hbm, direction_ref), (bases_hbm, bases_ref)), sems):
        copy.wait()
    xb = direction_ref[...].astype(BF16)
    rank_rows = bases_ref[...]
    low = mm_t(xb, rank_rows[:, :128])
    high = mm_t(xb, rank_rows[:, 128:])
    row = iota((8, 128), 0)
    twice = (iota((8, 128), 1) >> 5) * 2
    kept = jnp.where(row == twice, low, 0.0) + jnp.where(row == twice + 1, high, 0.0)
    coeffs = jnp.sum(kept, axis=0, keepdims=True)
    packed = jnp.concatenate([xb, jnp.where(row == 0, coeffs, 0.0).astype(BF16)], axis=0)
    for d in range(DEVS):
        out_ref[d] = packed


def prep_body(tiles_hbm, blocks_hbm, pairs_hbm, mask_hbm, near_pairs_hbm, near_mask_hbm, krylov_hbm,
              out_ref, tiles_ref, gather_ref, scatter_ref, gram_ref,
              pairs_ref, mask_ref, near_pairs_ref, near_mask_ref, krylov_ref, sems, tile_sem):
    fetched = pltpu.make_async_copy(tiles_hbm, tiles_ref, tile_sem)
    slots = blocks_hbm.shape[0]
    ends = (
        (blocks_hbm, out_ref.at[0:slots]),
        (pairs_hbm, pairs_ref),
        (mask_hbm, mask_ref),
        (near_pairs_hbm, near_pairs_ref),
        (near_mask_hbm, near_mask_ref),
        (krylov_hbm, krylov_ref),
    )
    copies = started(ends, sems)
    fetched.start()
    for copy in copies:
        copy.wait()
    i_row, j_row = pairs_ref[0:1, :], pairs_ref[1:2, :]
    step = ((j_row >> 7) - (i_row >> 7)) & (GROUPS - 1)
    which = jnp.where(step == 0, 0, jnp.where(step == 1, 2, 1))
    live = mask_ref[...]
    both = jnp.where(i_row == j_row, 0, live)
    row = iota((16, slots), 0)
    digits = jnp.zeros((16, slots), I32)
    for k, value in enumerate((i_row & 127, j_row & 127, which, live, both)):
        digits = jnp.where(row == k, value, digits)
    out_ref[slots : slots + 16, :] = jnp.zeros((16, out_ref.shape[1]), BF16)
    out_ref[slots : slots + 16, 0:slots] = small(digits)
    near = near_pairs_ref[...]
    live = near_mask_ref[...]
    near_slots = near.shape[1]
    row = iota((8, near_slots), 0)
    info = jnp.where(row == 0, near[0:1, :], jnp.where(row == 1, near[1:2, :], live))
    m = iota((64, near_slots), 0)
    pick = one_hot((m & 15) == iota((64, near_slots), 1))
    info_cols = mm_t(pick, small(info)).astype(I32)
    i_col, j_col = info_cols[:, 0:1], info_cols[:, 1:2]
    m = iota((64, 1), 0) >> 4
    c = jnp.where(m < 2, j_col, i_col)
    place = (c >> 2) * 16 + (c & 3) * 2 + (m & 1)
    gather_ref[...] = one_hot(iota((64, DEVS * 16), 1) == place)
    lane = iota((near_slots, 128), 1)
    pick = one_hot((lane & 15) == iota((near_slots, 128), 0))
    info_lanes = mm(small(info), pick).astype(I32)
    i_lane, j_lane, live_lane = (info_lanes[k : k + 1, :] for k in range(3))
    kind = (iota((1, 128), 1) >> 4) & 3
    used = (live_lane == 1) & ((kind < 2) | (i_lane != j_lane))
    target = jnp.where(kind < 2, i_lane, j_lane) * 2 + (kind & 1)
    target = jnp.where(used, target, -1)
    scatter_ref[...] = one_hot(iota((DEVS * 8, 128), 0) == target)
    rows = krylov_ref[...]
    gram = mm_exact(rows, rows, ((1,), (1,)))
    lane, row = iota((8, 128), 1) - 8, iota((8, 128), 0)
    inside = (lane >= 0) & (lane < 64)
    wide = mm_exact(gram, jnp.where(inside & ((lane & 7) == row), 1.0, 0.0), ((1,), (0,)))
    gram_ref[...] = jnp.sum(
        jnp.where(inside & ((lane >> 3) == row), wide, 0.0), axis=0, keepdims=True
    )
    fetched.wait()


def coeffs_body(gathered_ref, out_ref):
    parts = []
    for k in range(DEVS // 8):
        total = jnp.zeros((8, 128), F32)
        for r in range(8):
            at = (k * 8 + r) * 16
            tail = gathered_ref[at : at + 16, :].astype(F32)[8:16, :]
            total = total + (pltpu.roll(tail, r, 0) if r else tail)
        parts.append(total)
    out_ref[...] = jnp.concatenate(parts, axis=0).astype(BF16)


def near_body(gathered_ref, gather_ref, scatter_ref, tiles_ref, own_ref, before_ref, after_ref,
              out_ref, *far_refs):
    far_prep(own_ref, before_ref, after_ref, *far_refs)
    taken = mm(gather_ref[...], gathered_ref[...])
    right = jnp.concatenate([taken[0:16], taken[16:32]], axis=1).astype(BF16)
    left = jnp.concatenate([taken[32:48], taken[48:64]], axis=1).astype(BF16)
    slot = iota((16, 256), 0)
    forward = jnp.zeros((16, 256), F32)
    backward = jnp.zeros((16, 256), F32)
    for s in range(tiles_ref.shape[0]):
        tile = tiles_ref[s]
        forward = jnp.where(slot == s, mm_t(right, tile), forward)
        backward = jnp.where(slot == s, mm(left, tile), backward)
    values = jnp.concatenate(
        [forward[:, :128], forward[:, 128:], backward[:, :128], backward[:, 128:]], axis=0
    )
    out_ref[...] = mm(scatter_ref[...], jnp.concatenate(halves(values), axis=0))


def far_prep(own_ref, before_ref, after_ref, pick_ref, lanes_ref, keep_ref, owner_ref, take_ref,
             give_ref):
    slots = own_ref.shape[0] - 16
    rows = [
        ref[slots : slots + 16, 0:slots].astype(F32).astype(I32)
        for ref in (own_ref, before_ref, after_ref)
    ]
    cols = jnp.concatenate([columns(r) for r in [rows[0]] + rows], axis=0)
    i_low, j_low, which, live, both = (cols[:, k : k + 1] for k in range(5))
    slot = iota((4 * slots, 1), 0) // slots
    ahead = slot == 0
    low = jnp.where(ahead, j_low, i_low)
    source = jnp.where(ahead, which, slot - 1)
    pick_ref[...] = one_hot(iota((4 * slots, 3 * DEVS), 1) == source * DEVS + (low >> 2))
    block = iota((4 * slots, 128), 1) >> 5
    lanes_ref[...] = jnp.where(block == (low & 3), 1.0, 0.0)
    wanted = jnp.where(slot == 2, 2, jnp.where(slot == 3, 1, 0))
    used = jnp.where(ahead, live, jnp.where(which == wanted, both, 0))
    target = jnp.where(ahead, i_low, j_low)
    keep_ref[...] = jnp.where((used == 1) & (block == (target & 3)), 1.0, 0.0)
    owner = iota((DEVS, slots), 0)
    for k, row in enumerate([rows[0][0:1, :]] + [r[1:2, :] for r in rows]):
        owner_ref[k] = one_hot(owner == (row >> 2))
    for k in range(8):
        sub, lane = iota((128, 128), 0), iota((128, 128), 1)
        take_ref[k] = one_hot((sub & 31) == 4 * k + (lane >> 5))
        give_ref[k] = one_hot((lane & 31) == 4 * k + (sub >> 5))


def far_body(near_ref, own_ref, before_ref, after_ref, own_coef_ref, before_coef_ref,
             after_coef_ref, pick_ref, lanes_ref, keep_ref, owner_ref, take_ref, give_ref, out_ref):
    bundles = (own_ref, before_ref, after_ref)
    slots = own_ref.shape[0] - 16
    coeffs = jnp.concatenate([own_coef_ref[...], before_coef_ref[...], after_coef_ref[...]], axis=0)
    taken = (mm(pick_ref[...], coeffs) * lanes_ref[...]).astype(BF16)
    right, left = taken[0:slots], taken[slots:]
    sub, lane = iota((128, 128), 0), iota((128, 128), 1)
    tiled = mm(right, one_hot((sub & 31) == (lane & 31)))
    forward = jnp.zeros((slots, 128), F32)
    backward = jnp.zeros(left.shape, F32)
    for k in range(8):
        parts = [b[0:slots, k * 128 : k * 128 + 128] for b in bundles]
        part = jnp.concatenate(parts, axis=0).astype(F32)
        backward = backward + part * mm(left, take_ref[k])
        for piece in halves(part[0:slots] * tiled):
            forward = forward + mm(piece, give_ref[k])
    backward = backward + pltpu.roll(backward, 64, 1)
    backward = backward + pltpu.roll(backward, 32, 1)
    sums = jnp.concatenate([forward, backward], axis=0) * keep_ref[...]
    total = jnp.zeros((DEVS, 128), F32)
    for k in range(4):
        for part in halves(sums[k * slots : k * slots + slots]):
            total = total + mm(owner_ref[k], part)
    row = iota((8, 128), 0)
    far_high = total.astype(BF16).astype(F32)
    far_low = total - far_high
    for d in range(DEVS):
        near = near_ref[d * 8 : d * 8 + 8, :]
        low = jnp.where(row == 6, far_high[d : d + 1, :], near - near.astype(BF16).astype(F32))
        low = jnp.where(row == 7, far_low[d : d + 1, :], low)
        out_ref[d] = jnp.concatenate([near, low], axis=0).astype(BF16)


def product_body(pieces_ref, bases_ref, krylov_ref, gram_ref, product_ref, copies_ref):
    total = jnp.sum(pieces_ref[...].astype(F32), axis=0)
    row, lane = iota((8, 128), 0), iota((8, 128), 1)
    near = total[0:8, :] + jnp.where(row < 6, total[8:16, :], 0.0)
    coef = (total[14:15, :] + total[15:16, :]).astype(BF16).astype(F32)
    spread = jnp.where((lane >> 5) == (row >> 1), coef, 0.0).astype(BF16)
    low = mm(spread, bases_ref[:, :128])
    high = mm(spread, bases_ref[:, 128:])
    product = near + jnp.where((row & 1) == 0, low, high)
    product_ref[...] = product
    acc = jnp.zeros((8, 128), F32)
    for r in range(8):
        acc = acc + krylov_ref[:, r * 128 : r * 128 + 128] * product[r : r + 1, :]
    proj = jnp.sum(acc, axis=1, keepdims=True)
    square = jnp.sum(product * product, axis=1, keepdims=True)
    values = jnp.where(lane == row, proj, 0.0) + jnp.where(lane == 72, square, 0.0)
    payload = jnp.sum(values, axis=0, keepdims=True) + gram_ref[...]
    for d in range(copies_ref.shape[0]):
        copies_ref[d] = payload


def spread_body(pieces_ref, out_ref):
    total = jnp.sum(pieces_ref[...], axis=0)
    for d in range(out_ref.shape[0]):
        out_ref[d] = total


def last_body(count, pieces_ref, product_ref, krylov_ref, next_ref, proj_ref):
    total = jnp.sum(pieces_ref[...], axis=0)
    row, lane = iota((8, 128), 0), iota((8, 128), 1)
    proj = jnp.sum(jnp.where(lane == row, total, 0.0), axis=1, keepdims=True)
    inside = (lane >= 8) & (lane < 72)
    first = jnp.sum(jnp.where(inside & (((lane - 8) >> 3) == row), proj, 0.0), axis=0, keepdims=True)
    second = jnp.sum(jnp.where(inside & ((lane & 7) == row), proj, 0.0), axis=0, keepdims=True)
    lane = iota((1, 128), 1)
    terms = total * jnp.where(lane < 8, -2.0 * total, first * second)
    terms = jnp.where(lane == 72, total, jnp.where(lane < 72, terms, 0.0))
    length_sq = jnp.sum(terms, axis=1, keepdims=True)
    scale = 1.0 / jnp.sqrt(jnp.maximum(length_sq, 0.0) / count)
    for r in range(8):
        taken = jnp.sum(proj * krylov_ref[:, r * 128 : r * 128 + 128], axis=0, keepdims=True)
        next_ref[r : r + 1, :] = (product_ref[r : r + 1, :] - taken) * scale
    proj_ref[...] = total[:, 0:8]


def local(
    direction, krylov, bases, near_tiles, near_pairs, near_mask, far_blocks, far_pairs, far_mask
):
    panels = direction.shape[0]
    rank_rows = bases.reshape(-1, bases.shape[2])
    slots, far_slots = near_tiles.shape[0], far_blocks.shape[0]

    copies = call(
        pack_body,
        sds((DEVS, 16, 128), BF16),
        [HBM, HBM],
        [pltpu.VMEM((8, 128), F32), pltpu.VMEM(rank_rows.shape, BF16), pltpu.SemaphoreType.DMA((2,))],
    )(direction.reshape(8, 128), rank_rows)
    gathered = to_all(copies, "dev").reshape(-1, 128)
    bundle, tiles, gather, scatter, gram = call(
        prep_body,
        [
            sds((far_slots + 16, far_blocks.shape[1]), BF16),
            pltpu.VMEM(near_tiles.shape, BF16),
            sds((64, DEVS * 16), BF16),
            sds((DEVS * 8, 128), BF16),
            sds((1, 128), F32),
        ],
        [HBM] * 7,
        [
            pltpu.VMEM((2, far_slots), I32),
            pltpu.VMEM((1, far_slots), I32),
            pltpu.VMEM((2, slots), I32),
            pltpu.VMEM((1, slots), I32),
            pltpu.VMEM(krylov.shape, F32),
            pltpu.SemaphoreType.DMA((6,)),
            pltpu.SemaphoreType.DMA,
        ],
    )(near_tiles, far_blocks, far_pairs.T, far_mask[None], near_pairs.T, near_mask[None], krylov)
    before, after = group_shift(bundle, 1), group_shift(bundle, -1)

    coeffs = call(coeffs_body, sds((DEVS, 128), BF16), [VMEM])(gathered)
    coeffs_before, coeffs_after = group_shift(coeffs, 1), group_shift(coeffs, -1)
    near, *far_prepared = call(
        near_body,
        [
            sds((DEVS * 8, 128), F32),
            pltpu.VMEM((4 * far_slots, 3 * DEVS), BF16),
            pltpu.VMEM((4 * far_slots, 128), F32),
            pltpu.VMEM((4 * far_slots, 128), F32),
            pltpu.VMEM((4, DEVS, far_slots), BF16),
            pltpu.VMEM((8, 128, 128), BF16),
            pltpu.VMEM((8, 128, 128), BF16),
        ],
        [VMEM] * 7,
    )(gathered, gather, scatter, tiles, bundle, before, after)
    parts = call(far_body, sds((DEVS, 16, 128), BF16), [VMEM] * 13)(
        near, bundle, before, after, coeffs, coeffs_before, coeffs_after, *far_prepared
    )
    product, copies = call(
        product_body, [sds((8, 128), F32), sds((GROUPS, 1, 128), F32)], [VMEM] * 4
    )(to_all(parts, "dev"), rank_rows, krylov, gram)
    copies = call(spread_body, sds((DEVS, 1, 128), F32), [VMEM])(to_all(copies, "group"))
    pieces = to_all(copies, "dev")
    count = float(panels * DEVS * GROUPS)

    def finish(*refs):
        last_body(count, *refs)

    next_vector, projections = call(finish, [sds((8, 128), F32), sds((1, 8), F32)], [VMEM] * 3)(
        pieces, product, krylov
    )
    return (next_vector.reshape(-1), projections.reshape(-1))


def solution(mesh):
    in_specs = (
        P(("group", "dev")),
        P(None, ("group", "dev")),
        P(("group", "dev"), None, None),
        P(("group", "dev"), None, None),
        P(("group", "dev"), None),
        P(("group", "dev")),
        P(("group", "dev"), None),
        P(("group", "dev"), None),
        P(("group", "dev")),
    )
    out_specs = (P(("group", "dev")), P())
    return jax.shard_map(local, mesh=mesh, in_specs=in_specs, out_specs=out_specs, check_vma=False)
```

```python
import jax
import jax.numpy as jnp
from jax import lax
from jax.experimental import pallas as pl
from jax.experimental.pallas import tpu as pltpu
from jax.sharding import PartitionSpec as P

F32 = jnp.float32
BF16 = jnp.bfloat16
I32 = jnp.int32
NX, NZ, NY = 4, 8, 8
DEVS, GROUPS = NZ * NX, 2 * NY
VMEM = pl.BlockSpec(memory_space=pltpu.VMEM)
HBM = pl.BlockSpec(memory_space=pltpu.HBM)
sds = jax.ShapeDtypeStruct


def call(body, outs, specs, scratch=()):
    kernel = pl.pallas_call(
        body,
        out_shape=outs,
        in_specs=specs,
        out_specs=jax.tree.map(lambda _: VMEM, outs),
        scratch_shapes=list(scratch),
        compiler_params=pltpu.CompilerParams(vmem_limit_bytes=24 * 1024 * 1024),
    )

    def run(*args):
        return kernel(
            *(
                pltpu.with_memory_space_constraint(arg, pltpu.HBM) if spec is HBM else arg
                for arg, spec in zip(args, specs, strict=True)
            )
        )

    return run


def iota(shape, dim):
    return lax.broadcasted_iota(I32, shape, dim)


def mm(a, b):
    return lax.dot_general(a, b, (((1,), (0,)), ((), ())), preferred_element_type=F32)


def mm_t(a, b):
    return lax.dot_general(a, b, (((1,), (1,)), ((), ())), preferred_element_type=F32)


def mm_exact(a, b, dims):
    return lax.dot_general(
        a, b, (dims, ((), ())), precision=lax.Precision.HIGHEST, preferred_element_type=F32
    )


def halves(value):
    high = value.astype(BF16)
    return high, (value - high.astype(F32)).astype(BF16)


def one_hot(mask):
    return mask.astype(F32).astype(BF16)


def small(rows):
    return rows.astype(F32).astype(BF16)


def columns(rows):
    width = rows.shape[1]
    same = one_hot(iota((width, width), 0) == iota((width, width), 1))
    return mm_t(same, small(rows)).astype(I32)


def to_all(value, axis):
    return lax.all_to_all(value, axis, split_axis=0, concat_axis=0, tiled=True)


def group_shift(value, step):
    return lax.ppermute(value, "group", [(g, (g + step) % GROUPS) for g in range(GROUPS)])


def started(ends, sems):
    copies = [pltpu.make_async_copy(*end, sems.at[k]) for k, end in enumerate(ends)]
    for copy in copies:
        copy.start()
    return copies


def pack_body(direction_hbm, bases_hbm, out_ref, direction_ref, bases_ref, sems):
    for copy in started(((direction_hbm, direction_ref), (bases_hbm, bases_ref)), sems):
        copy.wait()
    xb = direction_ref[...].astype(BF16)
    rank_rows = bases_ref[...]
    low = mm_t(xb, rank_rows[:, :128])
    high = mm_t(xb, rank_rows[:, 128:])
    row = iota((8, 128), 0)
    twice = (iota((8, 128), 1) >> 5) * 2
    kept = jnp.where(row == twice, low, 0.0) + jnp.where(row == twice + 1, high, 0.0)
    coeffs = jnp.sum(kept, axis=0, keepdims=True)
    packed = jnp.concatenate([xb, jnp.where(row == 0, coeffs, 0.0).astype(BF16)], axis=0)
    for d in range(DEVS):
        out_ref[d] = packed


def prep_body(tiles_hbm, blocks_hbm, pairs_hbm, mask_hbm, near_pairs_hbm, near_mask_hbm, krylov_hbm,
              out_ref, tiles_ref, gather_ref, scatter_ref, gram_ref,
              pairs_ref, mask_ref, near_pairs_ref, near_mask_ref, krylov_ref, sems, tile_sem):
    fetched = pltpu.make_async_copy(tiles_hbm, tiles_ref, tile_sem)
    slots = blocks_hbm.shape[0]
    ends = (
        (blocks_hbm, out_ref.at[0:slots]),
        (pairs_hbm, pairs_ref),
        (mask_hbm, mask_ref),
        (near_pairs_hbm, near_pairs_ref),
        (near_mask_hbm, near_mask_ref),
        (krylov_hbm, krylov_ref),
    )
    copies = started(ends, sems)
    fetched.start()
    for copy in copies:
        copy.wait()
    i_row, j_row = pairs_ref[0:1, :], pairs_ref[1:2, :]
    step = ((j_row >> 7) - (i_row >> 7)) & (GROUPS - 1)
    which = jnp.where(step == 0, 0, jnp.where(step == 1, 2, 1))
    live = mask_ref[...]
    both = jnp.where(i_row == j_row, 0, live)
    row = iota((16, slots), 0)
    digits = jnp.zeros((16, slots), I32)
    for k, value in enumerate((i_row & 127, j_row & 127, which, live, both)):
        digits = jnp.where(row == k, value, digits)
    out_ref[slots : slots + 16, :] = jnp.zeros((16, out_ref.shape[1]), BF16)
    out_ref[slots : slots + 16, 0:slots] = small(digits)
    near = near_pairs_ref[...]
    live = near_mask_ref[...]
    near_slots = near.shape[1]
    row = iota((8, near_slots), 0)
    info = jnp.where(row == 0, near[0:1, :], jnp.where(row == 1, near[1:2, :], live))
    m = iota((64, near_slots), 0)
    pick = one_hot((m & 15) == iota((64, near_slots), 1))
    info_cols = mm_t(pick, small(info)).astype(I32)
    i_col, j_col = info_cols[:, 0:1], info_cols[:, 1:2]
    m = iota((64, 1), 0) >> 4
    c = jnp.where(m < 2, j_col, i_col)
    place = (c >> 2) * 16 + (c & 3) * 2 + (m & 1)
    gather_ref[...] = one_hot(iota((64, DEVS * 16), 1) == place)
    lane = iota((near_slots, 128), 1)
    pick = one_hot((lane & 15) == iota((near_slots, 128), 0))
    info_lanes = mm(small(info), pick).astype(I32)
    i_lane, j_lane, live_lane = (info_lanes[k : k + 1, :] for k in range(3))
    kind = (iota((1, 128), 1) >> 4) & 3
    used = (live_lane == 1) & ((kind < 2) | (i_lane != j_lane))
    target = jnp.where(kind < 2, i_lane, j_lane) * 2 + (kind & 1)
    target = jnp.where(used, target, -1)
    scatter_ref[...] = one_hot(iota((DEVS * 8, 128), 0) == target)
    rows = krylov_ref[...]
    gram = mm_exact(rows, rows, ((1,), (1,)))
    lane, row = iota((8, 128), 1) - 8, iota((8, 128), 0)
    inside = (lane >= 0) & (lane < 64)
    wide = mm_exact(gram, jnp.where(inside & ((lane & 7) == row), 1.0, 0.0), ((1,), (0,)))
    gram_ref[...] = jnp.sum(
        jnp.where(inside & ((lane >> 3) == row), wide, 0.0), axis=0, keepdims=True
    )
    fetched.wait()


def coeffs_body(gathered_ref, out_ref):
    parts = []
    for k in range(DEVS // 8):
        total = jnp.zeros((8, 128), F32)
        for r in range(8):
            at = (k * 8 + r) * 16
            tail = gathered_ref[at : at + 16, :].astype(F32)[8:16, :]
            total = total + (pltpu.roll(tail, r, 0) if r else tail)
        parts.append(total)
    out_ref[...] = jnp.concatenate(parts, axis=0).astype(BF16)


def near_body(gathered_ref, gather_ref, scatter_ref, tiles_ref, own_ref, before_ref, after_ref,
              out_ref, *far_refs):
    far_prep(own_ref, before_ref, after_ref, *far_refs)
    taken = mm(gather_ref[...], gathered_ref[...])
    right = jnp.concatenate([taken[0:16], taken[16:32]], axis=1).astype(BF16)
    left = jnp.concatenate([taken[32:48], taken[48:64]], axis=1).astype(BF16)
    slot = iota((16, 256), 0)
    forward = jnp.zeros((16, 256), F32)
    backward = jnp.zeros((16, 256), F32)
    for s in range(tiles_ref.shape[0]):
        tile = tiles_ref[s]
        forward = jnp.where(slot == s, mm_t(right, tile), forward)
        backward = jnp.where(slot == s, mm(left, tile), backward)
    values = jnp.concatenate(
        [forward[:, :128], forward[:, 128:], backward[:, :128], backward[:, 128:]], axis=0
    )
    out_ref[...] = mm(scatter_ref[...], jnp.concatenate(halves(values), axis=0))


def far_prep(own_ref, before_ref, after_ref, pick_ref, lanes_ref, keep_ref, owner_ref, take_ref,
             give_ref):
    slots = own_ref.shape[0] - 16
    rows = [
        ref[slots : slots + 16, 0:slots].astype(F32).astype(I32)
        for ref in (own_ref, before_ref, after_ref)
    ]
    cols = jnp.concatenate([columns(r) for r in [rows[0]] + rows], axis=0)
    i_low, j_low, which, live, both = (cols[:, k : k + 1] for k in range(5))
    slot = iota((4 * slots, 1), 0) // slots
    ahead = slot == 0
    low = jnp.where(ahead, j_low, i_low)
    source = jnp.where(ahead, which, slot - 1)
    pick_ref[...] = one_hot(iota((4 * slots, 3 * DEVS), 1) == source * DEVS + (low >> 2))
    block = iota((4 * slots, 128), 1) >> 5
    lanes_ref[...] = jnp.where(block == (low & 3), 1.0, 0.0)
    wanted = jnp.where(slot == 2, 2, jnp.where(slot == 3, 1, 0))
    used = jnp.where(ahead, live, jnp.where(which == wanted, both, 0))
    target = jnp.where(ahead, i_low, j_low)
    keep_ref[...] = jnp.where((used == 1) & (block == (target & 3)), 1.0, 0.0)
    owner = iota((DEVS, slots), 0)
    for k, row in enumerate([rows[0][0:1, :]] + [r[1:2, :] for r in rows]):
        owner_ref[k] = one_hot(owner == (row >> 2))
    for k in range(8):
        sub, lane = iota((128, 128), 0), iota((128, 128), 1)
        take_ref[k] = one_hot((sub & 31) == 4 * k + (lane >> 5))
        give_ref[k] = one_hot((lane & 31) == 4 * k + (sub >> 5))


def far_body(near_ref, own_ref, before_ref, after_ref, own_coef_ref, before_coef_ref,
             after_coef_ref, pick_ref, lanes_ref, keep_ref, owner_ref, take_ref, give_ref, out_ref):
    bundles = (own_ref, before_ref, after_ref)
    slots = own_ref.shape[0] - 16
    coeffs = jnp.concatenate([own_coef_ref[...], before_coef_ref[...], after_coef_ref[...]], axis=0)
    taken = (mm(pick_ref[...], coeffs) * lanes_ref[...]).astype(BF16)
    right, left = taken[0:slots], taken[slots:]
    sub, lane = iota((128, 128), 0), iota((128, 128), 1)
    tiled = mm(right, one_hot((sub & 31) == (lane & 31)))
    forward = jnp.zeros((2 * slots, 128), F32)
    backward = jnp.zeros(left.shape, F32)
    for k in range(8):
        parts = [b[0:slots, k * 128 : k * 128 + 128] for b in bundles]
        part = jnp.concatenate(parts, axis=0).astype(F32)
        backward = backward + part * mm(left, take_ref[k])
        split = jnp.concatenate(halves(part[0:slots] * tiled), axis=0)
        forward = forward + mm(split, give_ref[k])
    backward = backward + pltpu.roll(backward, 64, 1)
    backward = backward + pltpu.roll(backward, 32, 1)
    forward = forward[0:slots] + forward[slots:]
    sums = jnp.concatenate([forward, backward], axis=0) * keep_ref[...]
    split = jnp.concatenate(halves(sums), axis=1)
    total = jnp.zeros((DEVS, 256), F32)
    for k in range(4):
        total = total + mm(owner_ref[k], split[k * slots : k * slots + slots])
    total = total[:, 0:128] + total[:, 128:256]
    row = iota((8, 128), 0)
    far_high = total.astype(BF16).astype(F32)
    far_low = total - far_high
    for d in range(DEVS):
        near = near_ref[d * 8 : d * 8 + 8, :]
        low = jnp.where(row == 6, far_high[d : d + 1, :], near - near.astype(BF16).astype(F32))
        low = jnp.where(row == 7, far_low[d : d + 1, :], low)
        out_ref[d] = jnp.concatenate([near, low], axis=0).astype(BF16)


def product_body(pieces_ref, bases_ref, krylov_ref, gram_ref, product_ref, copies_ref):
    total = jnp.sum(pieces_ref[...].astype(F32), axis=0)
    row, lane = iota((8, 128), 0), iota((8, 128), 1)
    near = total[0:8, :] + jnp.where(row < 6, total[8:16, :], 0.0)
    coef = (total[14:15, :] + total[15:16, :]).astype(BF16).astype(F32)
    spread = jnp.where((lane >> 5) == (row >> 1), coef, 0.0).astype(BF16)
    low = mm(spread, bases_ref[:, :128])
    high = mm(spread, bases_ref[:, 128:])
    product = near + jnp.where((row & 1) == 0, low, high)
    product_ref[...] = product
    acc = jnp.zeros((8, 128), F32)
    for r in range(8):
        acc = acc + krylov_ref[:, r * 128 : r * 128 + 128] * product[r : r + 1, :]
    proj = jnp.sum(acc, axis=1, keepdims=True)
    square = jnp.sum(product * product, axis=1, keepdims=True)
    values = jnp.where(lane == row, proj, 0.0) + jnp.where(lane == 72, square, 0.0)
    payload = jnp.sum(values, axis=0, keepdims=True) + gram_ref[...]
    for d in range(copies_ref.shape[0]):
        copies_ref[d] = payload


def spread_body(pieces_ref, out_ref):
    total = jnp.sum(pieces_ref[...], axis=0)
    for d in range(out_ref.shape[0]):
        out_ref[d] = total


def last_body(count, pieces_ref, product_ref, krylov_ref, next_ref, proj_ref):
    total = jnp.sum(pieces_ref[...], axis=0)
    row, lane = iota((8, 128), 0), iota((8, 128), 1)
    proj = jnp.sum(jnp.where(lane == row, total, 0.0), axis=1, keepdims=True)
    inside = (lane >= 8) & (lane < 72)
    first = jnp.sum(jnp.where(inside & (((lane - 8) >> 3) == row), proj, 0.0), axis=0, keepdims=True)
    second = jnp.sum(jnp.where(inside & ((lane & 7) == row), proj, 0.0), axis=0, keepdims=True)
    lane = iota((1, 128), 1)
    terms = total * jnp.where(lane < 8, -2.0 * total, first * second)
    terms = jnp.where(lane == 72, total, jnp.where(lane < 72, terms, 0.0))
    length_sq = jnp.sum(terms, axis=1, keepdims=True)
    scale = 1.0 / jnp.sqrt(jnp.maximum(length_sq, 0.0) / count)
    for r in range(8):
        taken = jnp.sum(proj * krylov_ref[:, r * 128 : r * 128 + 128], axis=0, keepdims=True)
        next_ref[r : r + 1, :] = (product_ref[r : r + 1, :] - taken) * scale
    proj_ref[...] = total[:, 0:8]


def local(
    direction, krylov, bases, near_tiles, near_pairs, near_mask, far_blocks, far_pairs, far_mask
):
    panels = direction.shape[0]
    rank_rows = bases.reshape(-1, bases.shape[2])
    slots, far_slots = near_tiles.shape[0], far_blocks.shape[0]

    copies = call(
        pack_body,
        sds((DEVS, 16, 128), BF16),
        [HBM, HBM],
        [pltpu.VMEM((8, 128), F32), pltpu.VMEM(rank_rows.shape, BF16), pltpu.SemaphoreType.DMA((2,))],
    )(direction.reshape(8, 128), rank_rows)
    gathered = to_all(copies, "dev").reshape(-1, 128)
    bundle, tiles, gather, scatter, gram = call(
        prep_body,
        [
            sds((far_slots + 16, far_blocks.shape[1]), BF16),
            pltpu.VMEM(near_tiles.shape, BF16),
            sds((64, DEVS * 16), BF16),
            sds((DEVS * 8, 128), BF16),
            sds((1, 128), F32),
        ],
        [HBM] * 7,
        [
            pltpu.VMEM((2, far_slots), I32),
            pltpu.VMEM((1, far_slots), I32),
            pltpu.VMEM((2, slots), I32),
            pltpu.VMEM((1, slots), I32),
            pltpu.VMEM(krylov.shape, F32),
            pltpu.SemaphoreType.DMA((6,)),
            pltpu.SemaphoreType.DMA,
        ],
    )(near_tiles, far_blocks, far_pairs.T, far_mask[None], near_pairs.T, near_mask[None], krylov)
    before, after = group_shift(bundle, 1), group_shift(bundle, -1)

    coeffs = call(coeffs_body, sds((DEVS, 128), BF16), [VMEM])(gathered)
    coeffs_before, coeffs_after = group_shift(coeffs, 1), group_shift(coeffs, -1)
    near, *far_prepared = call(
        near_body,
        [
            sds((DEVS * 8, 128), F32),
            pltpu.VMEM((4 * far_slots, 3 * DEVS), BF16),
            pltpu.VMEM((4 * far_slots, 128), F32),
            pltpu.VMEM((4 * far_slots, 128), F32),
            pltpu.VMEM((4, DEVS, far_slots), BF16),
            pltpu.VMEM((8, 128, 128), BF16),
            pltpu.VMEM((8, 128, 128), BF16),
        ],
        [VMEM] * 7,
    )(gathered, gather, scatter, tiles, bundle, before, after)
    parts = call(far_body, sds((DEVS, 16, 128), BF16), [VMEM] * 13)(
        near, bundle, before, after, coeffs, coeffs_before, coeffs_after, *far_prepared
    )
    product, copies = call(
        product_body, [sds((8, 128), F32), sds((GROUPS, 1, 128), F32)], [VMEM] * 4
    )(to_all(parts, "dev"), rank_rows, krylov, gram)
    copies = call(spread_body, sds((DEVS, 1, 128), F32), [VMEM])(to_all(copies, "group"))
    pieces = to_all(copies, "dev")
    count = float(panels * DEVS * GROUPS)

    def finish(*refs):
        last_body(count, *refs)

    next_vector, projections = call(finish, [sds((8, 128), F32), sds((1, 8), F32)], [VMEM] * 3)(
        pieces, product, krylov
    )
    return (next_vector.reshape(-1), projections.reshape(-1))


def solution(mesh):
    in_specs = (
        P(("group", "dev")),
        P(None, ("group", "dev")),
        P(("group", "dev"), None, None),
        P(("group", "dev"), None, None),
        P(("group", "dev"), None),
        P(("group", "dev")),
        P(("group", "dev"), None),
        P(("group", "dev"), None),
        P(("group", "dev")),
    )
    out_specs = (P(("group", "dev")), P())
    return jax.shard_map(local, mesh=mesh, in_specs=in_specs, out_specs=out_specs, check_vma=False)
```
